256 devices in a mesh: comm: 8 (over z), stn: 16 (over y, x), tm: 2 (over core).
Axes of the slice: x: 4, y: 4, z: 8, core: 2. Of those that a mesh axis runs over, the one named last changes fastest.
Arguments:
- tiles: float32 [16, 512, 3, 128, 128], P('comm', ('stn', 'tm')), may hold values from -0.21875 to 0.21875
- cap_tiles: float32 [16, 512, 128, 128], P('comm', ('stn', 'tm')), may hold values from -0.125 to 0.125
- row_index: int32 [16, 512, 3], P('comm', ('stn', 'tm')), may hold values from 0 to 255, as said below
- cap_index: int32 [16, 512], P('comm', ('stn', 'tm')), may hold values from 0 to 15
- arc_scale: float32 [16, 512, 128], P('comm', ('stn', 'tm')), may hold values from 0.1 to 10
- rows_rhs: float32 [16, 256, 128], P('comm', ('stn', 'tm')), may hold values from -6 to 6
- cap_rhs: float32 [512, 128], P(('stn', 'tm')), may hold values from -6 to 6
- precond: float32 [16, 256, 128, 128], P('comm', ('stn', 'tm')), as said below
- cap_precond: float32 [512, 128, 128], P(('stn', 'tm')), as said below
Outputs:
- solution: float32 [16, 256, 128], P('comm', ('stn', 'tm'))
- cap_solution: float32 [512, 128], P(('stn', 'tm'))
- residual: float32 [16, 256, 128], P('comm', ('stn', 'tm'))
- cap_residual: float32 [512, 128], P(('stn', 'tm'))
The draws below stay inside these ranges and needn't reach their ends.
Inputs may be any that keep to these rules, and one draw needn't show every extreme that they name: For arc column block j, row_index[c, j, 0] and row_index[c, j, 1] differ and lie among the 8 row blocks from (j // 16) * 8 on; row_index[c, j, 2] lies outside them. Of the third row blocks of the 16 arc blocks from (j // 16) * 16 on of one commodity, at most 1 lie in any one other range of 8 row blocks, and exactly 1 in some. `precond`: every block is symmetric positive definite. `cap_precond`: every block is symmetric positive definite.
All inputs are finite; a program needn't handle non-finite values.
Results may differ from the reference program's by a relative error of at most 0.0003.
Values sent between devices are 32-bit elements; how exact they have to be, the bound alone decides.
No kernel may reach another device: no remote copies, remote signals or barrier semaphores. Data moves between devices by JAX's collectives and lax.ppermute only.
A program may use at most 64 MiB of HBM per device.

```python
import math
import jax
import jax.numpy as jnp
from jax import lax

BLK = 128
RB = 8
AB = 16
CB = 16
NB = 3
ITERS = 3
COMMS = 16
ROWBLK = 256
ARCBLK = 512
CAPBLK = 512
MOST = 1


def build_blocks(diagonal, raw):
    upper = jnp.triu(raw, 1)
    sym = upper + jnp.swapaxes(upper, -1, -2)
    eye = jnp.eye(BLK, dtype=jnp.float32)
    return sym * (0.9 / (BLK - 1)) + eye * diagonal[..., None]


def draw_precond(key, part):
    key = jax.random.fold_in(key, 11)
    first, second = jax.random.split(key)
    shape = (COMMS, ROWBLK, BLK, BLK)
    diagonal = jax.random.uniform(first, (COMMS, ROWBLK, BLK), jnp.float32, 1.0, 3.0)
    raw = jnp.where(jax.random.bernoulli(second, 0.5, shape), 1.0, -1.0).astype(jnp.float32)
    return build_blocks(diagonal, raw)


def draw_cap_precond(key, part):
    key = jax.random.fold_in(key, 23)
    first, second = jax.random.split(key)
    shape = (CAPBLK, BLK, BLK)
    diagonal = jax.random.uniform(first, (CAPBLK, BLK), jnp.float32, 1.0, 3.0)
    raw = jnp.where(jax.random.bernoulli(second, 0.5, shape), 1.0, -1.0).astype(jnp.float32)
    return build_blocks(diagonal, raw)


def draw_row_index(key, part):
    key = jax.random.fold_in(key, 37)
    keys = jax.random.split(key, 4)
    groups = ARCBLK // AB
    arcs = jnp.arange(ARCBLK, dtype=jnp.int32)
    owner = arcs // AB
    local = arcs % AB
    first = jax.random.randint(keys[0], (COMMS, ARCBLK), 0, RB, dtype=jnp.int32)
    second = (first + jax.random.randint(keys[1], (COMMS, ARCBLK), 1, RB, dtype=jnp.int32)) % RB
    shifts = jax.random.randint(keys[2], (COMMS, groups), 0, groups - 1, dtype=jnp.int32)
    offset = 1 + (local[None, :] // MOST + shifts[:, owner]) % (groups - 1)
    target = (owner[None, :] + offset) % groups
    third = jax.random.randint(keys[3], (COMMS, ARCBLK), 0, RB, dtype=jnp.int32)
    base = owner[None, :] * RB
    return jnp.stack([base + first, base + second, target * RB + third], axis=2).astype(jnp.int32)


def with_ends(result, rng, low, top_value):
    spot = [jax.random.randint(jax.random.fold_in(rng, axis), (), 0, length) for axis, length in enumerate(result.shape)]
    longest = result.shape.index(max(result.shape))
    next_to = spot[:longest] + [(spot[longest] + 1) % result.shape[longest]] + spot[longest + 1:]
    return result.at[tuple(spot)].set(low).at[tuple(next_to)].set(top_value)


def shard_levels(key, dims, pieces, low, largest):
    def one(position, shards_of):
        steps = jax.random.uniform(jax.random.fold_in(jax.random.fold_in(key, 6), position), (shards_of,), jnp.float32, low / len(pieces), largest / len(pieces))
        return jnp.repeat(jnp.exp(steps), dims[position] // shards_of).reshape((-1,) + (1,) * (len(dims) - position - 1))

    gain = one(*pieces[0])
    for cut in pieces[1:]:
        gain = gain * one(*cut)
    return gain


def centred(rng, shape, scale, reach, shards=(), kind=jnp.bfloat16):
    drawn = jax.random.normal(rng, shape, jnp.float32) * scale
    if len(shards) > 0:
        drawn = shard_levels(rng, shape, shards, -0.22, 0.18) * drawn
    return jnp.clip(drawn, min=-reach, max=reach).astype(kind)


def setup_inputs(seed: int = 0) -> dict:
    key_of = jax.random.split(jax.random.key(seed), 10)
    tiles = centred(key_of[0], (COMMS, ARCBLK, NB, BLK, BLK), (BLK * NB * AB // RB) ** -0.5, 0.21875, ((0, 8), (1, 32)), jnp.float32)
    cap_tiles = centred(key_of[1], (COMMS, ARCBLK, BLK, BLK), (BLK * COMMS * AB // CB) ** -0.5, 0.125, ((0, 8), (1, 32)), jnp.float32)
    row_index = draw_row_index(jax.random.fold_in(key_of[9], 71), 0)
    cap_index = with_ends(jax.random.randint(key_of[3], (COMMS, ARCBLK), 0, CB), jax.random.fold_in(key_of[3], 1), 0, CB - 1).astype(jnp.int32)
    arc_scale = jnp.clip(jnp.exp(math.log(10.0) - 4.6051702 * jax.random.uniform(key_of[4], (COMMS, ARCBLK, BLK), jnp.float32) ** shard_levels(key_of[4], (COMMS, ARCBLK, BLK), ((0, 8), (1, 32)), -0.2, 0.2)), 0.1, 10.0)
    rows_rhs = centred(key_of[5], (COMMS, ROWBLK, BLK), 1.0, 6.0, ((0, 8), (1, 32)), jnp.float32)
    cap_rhs = centred(key_of[6], (CAPBLK, BLK), 1.0, 6.0, ((0, 32),), jnp.float32)
    precond = draw_precond(jax.random.fold_in(key_of[9], 71), 0)
    cap_precond = draw_cap_precond(jax.random.fold_in(key_of[9], 71), 0)
    return dict(tiles=tiles, cap_tiles=cap_tiles, row_index=row_index, cap_index=cap_index, arc_scale=arc_scale, rows_rhs=rows_rhs, cap_rhs=cap_rhs, precond=precond, cap_precond=cap_precond)


ridge_weight = 1.0


def apply_operator(tiles, cap_tiles, row_index, cap_block, arc_scale, dirs, cap_dirs):
    high = lax.Precision.HIGHEST
    chosen = jax.vmap(lambda table, idx: table[idx])(dirs, row_index)
    upward = jnp.einsum('cjkra,cjkr->cja', tiles, chosen, precision=high)
    upward = upward + jnp.einsum('cjra,cjr->cja', cap_tiles, cap_dirs[cap_block], precision=high)
    scaled = arc_scale * upward
    parts = jnp.einsum('cjkra,cja->cjkr', tiles, scaled, precision=high)

    def place(idx, part):
        empty = jnp.zeros((ROWBLK, BLK), jnp.float32)
        return empty.at[idx.reshape(-1)].add(part.reshape(-1, BLK))

    image = jax.vmap(place)(row_index, parts) + ridge_weight * dirs
    cap_parts = jnp.einsum('cjra,cja->cjr', cap_tiles, scaled, precision=high)
    cap_image = jnp.zeros((CAPBLK, BLK), jnp.float32).at[cap_block.reshape(-1)].add(cap_parts.reshape(-1, BLK))
    return image, cap_image + ridge_weight * cap_dirs


def reference(tiles, cap_tiles, row_index, cap_index, arc_scale, rows_rhs, cap_rhs, precond, cap_precond):
    high = lax.Precision.HIGHEST
    owner = (jnp.arange(ARCBLK, dtype=jnp.int32) // AB) * CB
    cap_block = (owner[None, :] + cap_index).astype(jnp.int32)

    def condition(resid, cap_resid):
        zed = jnp.einsum('cqrs,cqs->cqr', precond, resid, precision=high)
        cap_zed = jnp.einsum('qrs,qs->qr', cap_precond, cap_resid, precision=high)
        return zed, cap_zed

    solution = jnp.zeros_like(rows_rhs)
    cap_solution = jnp.zeros_like(cap_rhs)
    residual, cap_residual = rows_rhs, cap_rhs
    zed, cap_zed = condition(residual, cap_residual)
    dirs, cap_dirs = zed, cap_zed
    rz_now = jnp.sum(residual * zed) + jnp.sum(cap_residual * cap_zed)
    for step in range(ITERS):
        image, cap_image = apply_operator(tiles, cap_tiles, row_index, cap_block, arc_scale, dirs, cap_dirs)
        alpha = rz_now / (jnp.sum(dirs * image) + jnp.sum(cap_dirs * cap_image))
        solution = solution + alpha * dirs
        cap_solution = cap_solution + alpha * cap_dirs
        residual = residual - alpha * image
        cap_residual = cap_residual - alpha * cap_image
        if step + 1 < ITERS:
            zed, cap_zed = condition(residual, cap_residual)
            rz_next = jnp.sum(residual * zed) + jnp.sum(cap_residual * cap_zed)
            ratio = rz_next / rz_now
            dirs = zed + ratio * dirs
            cap_dirs = cap_zed + ratio * cap_dirs
            rz_now = rz_next
    return solution, cap_solution, residual, cap_residual
```

```python
import jax
import jax.numpy as jnp
from jax import lax
from jax.sharding import PartitionSpec as P

ITERS = 3
GROUP = ("stn", "tm")
HIGH = lax.Precision.HIGHEST
META = 4


def body(
    tiles, cap_tiles, row_index, cap_index, arc_scale, rows_rhs, cap_rhs, precond, cap_precond
):
    comms, arcs, _ = row_index.shape
    blocks, width = rows_rhs.shape[1:]
    caps = cap_rhs.shape[0]
    groups = lax.axis_size("stn") * lax.axis_size("tm")
    peers = lax.axis_size("comm")
    me = lax.axis_index(GROUP)

    near = row_index[:, :, :2] - me * blocks
    near_hot = jax.nn.one_hot(near, blocks, dtype=jnp.float32)
    cap_hot = jax.nn.one_hot(cap_index, caps, dtype=jnp.float32)
    far_owner = row_index[:, :, 2] // blocks
    far_local = row_index[:, :, 2] % blocks
    owner_hot = jax.nn.one_hot(far_owner, groups, dtype=jnp.float32)
    want = jnp.einsum("cjo,cj->oc", owner_hot, far_local + 1.0, precision=HIGH) - 1.0

    def condition(resid, cap_resid):
        zed = jnp.einsum("cqrs,cqs->cqr", precond, resid, precision=HIGH)
        cap_zed = jnp.einsum("qrs,qs->qr", cap_precond, cap_resid, precision=HIGH)
        return zed, cap_zed

    sol = jnp.zeros_like(rows_rhs)
    cap_sol = jnp.zeros_like(cap_rhs)
    res, cap_res = rows_rhs, cap_rhs
    p = jnp.zeros_like(rows_rhs)
    cap_p = jnp.zeros_like(cap_rhs)
    w = jnp.zeros_like(rows_rhs)
    cap_w = jnp.zeros_like(cap_rhs)
    rz_prev = None
    pmp = None
    asked = None
    zed, cap_zed = condition(res, cap_res)
    for step in range(ITERS):
        if step == 0:
            send = jnp.broadcast_to(
                zed.reshape(1, comms * blocks, width), (groups, comms * blocks, width)
            )
            got = lax.all_to_all(
                send.reshape(groups * comms * blocks, width), GROUP, 0, 0, tiled=True
            ).reshape(groups, comms, blocks, width)
            far = jax.vmap(lambda c, o, b: got[o, c, b])(jnp.arange(comms), far_owner, far_local)
        else:
            send = jnp.einsum(
                "ocb,cbr->ocr",
                jax.nn.one_hot(asked.astype(jnp.int32), blocks, dtype=jnp.float32),
                zed,
                precision=HIGH,
            )
            got = lax.all_to_all(
                send.reshape(groups * comms, width), GROUP, 0, 0, tiled=True
            ).reshape(groups, comms, width)
            far = jax.vmap(lambda c, o: got[o, c])(jnp.arange(comms), far_owner)
        close = jnp.einsum("cjkb,cbr->cjkr", near_hot, zed, precision=HIGH)
        chosen = jnp.concatenate([close, far[:, :, None]], axis=2)
        upward = jnp.einsum("cjkra,cjkr->cja", tiles, chosen, precision=HIGH)
        upward = upward + jnp.einsum("cjra,cjr->cja", cap_tiles, cap_zed[cap_index], precision=HIGH)
        scaled = arc_scale * upward
        cap_parts = jnp.einsum("cjra,cja->cjr", cap_tiles, scaled, precision=HIGH)
        cap_sum = jnp.einsum("cjq,cjr->qr", cap_hot, cap_parts, precision=HIGH)
        sums = jnp.stack(
            [
                jnp.sum(res * zed),
                jnp.sum(zed * zed) + jnp.sum(upward * scaled),
                jnp.sum(zed * w),
            ]
        )
        row = jnp.pad(sums, (0, width - 3)).reshape(1, width)
        note = jnp.concatenate([cap_sum, jnp.broadcast_to(row, (8, width))], axis=0)
        notes = lax.all_to_all(
            jnp.broadcast_to(note[None], (peers,) + note.shape).reshape(-1, width),
            "comm",
            0,
            0,
            tiled=True,
        ).reshape((peers,) + note.shape)
        note = jnp.sum(notes, axis=0)
        cap_image = note[:caps] + cap_zed
        sums = note[caps, :3] + jnp.stack(
            [jnp.sum(cap_res * cap_zed), jnp.sum(cap_zed * cap_zed), jnp.sum(cap_zed * cap_w)]
        )
        parts = jnp.einsum("cjkra,cja->cjkr", tiles, scaled, precision=HIGH)
        local = jnp.einsum("cjkb,cjkr->cbr", near_hot, parts[:, :, :2], precision=HIGH)
        out = jnp.einsum("cjo,cjr->ocr", owner_hot, parts[:, :, 2], precision=HIGH)
        meta = jnp.concatenate(
            [want, jnp.broadcast_to(sums[None], (groups, 3))], axis=1
        )
        meta = jnp.pad(meta, ((0, 0), (0, width - comms - 3)))[:, None]
        pad = jnp.zeros((groups, META - comms - 1, width), jnp.float32)
        back = lax.all_to_all(
            jnp.concatenate([out, meta, pad], axis=1).reshape(groups * META, width),
            GROUP,
            0,
            0,
            tiled=True,
        ).reshape(groups, META, width)
        asked = back[:, comms, :comms]
        asked_hot = jax.nn.one_hot(asked.astype(jnp.int32), blocks, dtype=jnp.float32)
        image = (
            zed
            + local
            + jnp.einsum("ocb,ocr->cbr", asked_hot, back[:, :comms], precision=HIGH)
        )
        sums = jnp.sum(back[:, comms, comms : comms + 3], axis=0)
        rz, zmz, zw = sums[0], sums[1], sums[2]
        if step == 0:
            pmp = zmz
            p, cap_p, w, cap_w = zed, cap_zed, image, cap_image
        else:
            ratio = rz / rz_prev
            pmp = zmz + ratio * (2.0 * zw + ratio * pmp)
            p = zed + ratio * p
            cap_p = cap_zed + ratio * cap_p
            w = image + ratio * w
            cap_w = cap_image + ratio * cap_w
        alpha = rz / pmp
        rz_prev = rz
        sol = sol + alpha * p
        cap_sol = cap_sol + alpha * cap_p
        res = res - alpha * w
        cap_res = cap_res - alpha * cap_w
        if step + 1 < ITERS:
            zed, cap_zed = condition(res, cap_res)
    return sol, cap_sol, res, cap_res


def solution(mesh):
    placed = (
        P("comm", GROUP, None, None, None),
        P("comm", GROUP, None, None),
        P("comm", GROUP, None),
        P("comm", GROUP),
        P("comm", GROUP, None),
        P("comm", GROUP, None),
        P(GROUP, None),
        P("comm", GROUP, None, None),
        P(GROUP, None, None),
    )
    return jax.shard_map(
        body,
        mesh=mesh,
        in_specs=placed,
        out_specs=(
            P("comm", GROUP, None),
            P(GROUP, None),
            P("comm", GROUP, None),
            P(GROUP, None),
        ),
        check_vma=False,
    )
```

```python
import jax
import jax.numpy as jnp
from jax import lax
from jax.sharding import PartitionSpec as P

ITERS = 3
GROUP = ("stn", "tm")
HIGH = lax.Precision.HIGHEST
META = 4


def body(
    tiles, cap_tiles, row_index, cap_index, arc_scale, rows_rhs, cap_rhs, precond, cap_precond
):
    comms, arcs, _ = row_index.shape
    blocks, width = rows_rhs.shape[1:]
    caps = cap_rhs.shape[0]
    groups = lax.axis_size("stn") * lax.axis_size("tm")
    peers = lax.axis_size("comm")
    me = lax.axis_index(GROUP)

    near = row_index[:, :, :2] - me * blocks
    near_hot = jax.nn.one_hot(near, blocks, dtype=jnp.float32)
    cap_hot = jax.nn.one_hot(cap_index, caps, dtype=jnp.float32)
    far_owner = row_index[:, :, 2] // blocks
    far_local = row_index[:, :, 2] % blocks
    owner_hot = jax.nn.one_hot(far_owner, groups, dtype=jnp.float32)
    want = jnp.einsum("cjo,cj->oc", owner_hot, far_local + 1.0, precision=HIGH) - 1.0

    def condition(resid, cap_resid):
        zed = jnp.einsum("cqrs,cqs->cqr", precond, resid, precision=HIGH)
        cap_zed = jnp.einsum("qrs,qs->qr", cap_precond, cap_resid, precision=HIGH)
        return zed, cap_zed

    def far_rows_all(zed):
        send = jnp.broadcast_to(
            zed.reshape(1, comms * blocks, width), (groups, comms * blocks, width)
        )
        got = lax.all_to_all(
            send.reshape(groups * comms * blocks, width), GROUP, 0, 0, tiled=True
        ).reshape(groups, comms, blocks, width)
        return jax.vmap(lambda c, o, b: got[o, c, b])(jnp.arange(comms), far_owner, far_local)

    def far_rows(zed, asked_hot):
        send = jnp.einsum("ocb,cbr->ocr", asked_hot, zed, precision=HIGH)
        got = lax.all_to_all(
            send.reshape(groups * comms, width), GROUP, 0, 0, tiled=True
        ).reshape(groups, comms, width)
        return jax.vmap(lambda c, o: got[o, c])(jnp.arange(comms), far_owner)

    def up(zed, far, cap_zed):
        close = jnp.einsum("cjkb,cbr->cjkr", near_hot, zed, precision=HIGH)
        chosen = jnp.concatenate([close, far[:, :, None]], axis=2)
        upward = jnp.einsum("cjkra,cjkr->cja", tiles, chosen, precision=HIGH)
        return upward + jnp.einsum("cjra,cjr->cja", cap_tiles, cap_zed[cap_index], precision=HIGH)

    def cap_down(scaled, rows):
        cap_parts = jnp.einsum("cjra,cja->cjr", cap_tiles, scaled, precision=HIGH)
        cap_sum = jnp.einsum("cjq,cjr->qr", cap_hot, cap_parts, precision=HIGH)
        note = jnp.concatenate([cap_sum, rows], axis=0)
        notes = lax.all_to_all(
            jnp.broadcast_to(note[None], (peers,) + note.shape).reshape(-1, width),
            "comm",
            0,
            0,
            tiled=True,
        ).reshape((peers,) + note.shape)
        note = jnp.sum(notes, axis=0)
        return note[:caps], jnp.sum(note[caps:], axis=1)

    def rows_down(scaled, extra):
        parts = jnp.einsum("cjkra,cja->cjkr", tiles, scaled, precision=HIGH)
        local = jnp.einsum("cjkb,cjkr->cbr", near_hot, parts[:, :, :2], precision=HIGH)
        out = jnp.einsum("cjo,cjr->ocr", owner_hot, parts[:, :, 2], precision=HIGH)
        back = lax.all_to_all(
            jnp.concatenate([out, extra], axis=1).reshape(groups * META, width),
            GROUP,
            0,
            0,
            tiled=True,
        ).reshape(groups, META, width)
        return local, back

    def lanes(*rows):
        out = jnp.stack([jnp.sum(row.reshape(-1, width), axis=0) for row in rows])
        return jnp.pad(out, ((0, 8 - len(rows)), (0, 0)))

    none = jnp.zeros((8, width), jnp.float32)
    v0, q0 = condition(rows_rhs, cap_rhs)
    upward = up(v0, far_rows_all(v0), q0)
    scaled = arc_scale * upward
    cap_sum, sums = cap_down(
        scaled,
        lanes(rows_rhs * v0, jnp.concatenate([v0 * v0, upward * scaled], axis=1)),
    )
    sums = sums.at[0].add(jnp.sum(cap_rhs * q0)).at[1].add(jnp.sum(q0 * q0))
    wide = jnp.broadcast_to(want[:, :, None], want.shape + (width,))
    local, back = rows_down(scaled, wide)
    asked = back[:, comms:, 0]
    asked_hot = jax.nn.one_hot(asked.astype(jnp.int32), blocks, dtype=jnp.float32)

    def collect(v, local, back):
        return v + local + jnp.einsum("ocb,ocr->cbr", asked_hot, back[:, :comms], precision=HIGH)

    def carry(sums):
        row = jnp.pad(sums, (0, width - 8))
        row = jnp.broadcast_to(row[None, None], (groups, 1, width))
        return jnp.pad(row, ((0, 0), (0, META - comms - 1), (0, 0)))

    y0 = collect(v0, local, back)
    yq0 = q0 + cap_sum
    v1, q1 = condition(y0, yq0)
    upward = up(v1, far_rows(v1, asked_hot), q1)
    scaled = arc_scale * upward
    cap_sum, _ = cap_down(scaled, none)
    local, back = rows_down(scaled, carry(sums))
    sums = jnp.sum(back[:, comms], axis=0)
    y1 = collect(v1, local, back)
    yq1 = q1 + cap_sum
    h00 = sums[1]
    alpha = sums[0] / h00
    r1, rq1 = rows_rhs - alpha * y0, cap_rhs - alpha * yq0
    z1, zq1 = v0 - alpha * v1, q0 - alpha * q1
    yz, yzq = y0 - alpha * y1, yq0 - alpha * yq1
    v2, q2 = condition(alpha * yz, alpha * yzq)
    upward = up(v2, far_rows(v2, asked_hot), q2)
    scaled = arc_scale * upward
    pairs = [(z1, y0, zq1, yq0), (z1, yz, zq1, yzq), (v2, y0, q2, yq0), (v2, yz, q2, yzq),
             (v2, v2, q2, q2), (z1, r1, zq1, rq1), (v2, r1, q2, rq1)]
    products = [a * b for a, b, _, _ in pairs]
    products[4] = jnp.concatenate([products[4], upward * scaled], axis=1)
    cap_sum, sums = cap_down(scaled, lanes(*products))
    sums = sums + jnp.stack([jnp.sum(c * d) for _, _, c, d in pairs] + [jnp.zeros(())])
    local, back = rows_down(scaled, carry(sums))
    sums = jnp.sum(back[:, comms], axis=0)
    y2 = collect(v2, local, back)
    yq2 = q2 + cap_sum
    h1, h2 = sums[0] / h00, sums[2] / h00
    a11 = sums[1] - h1 * sums[0]
    a12 = sums[3] - h1 * sums[2]
    a22 = sums[4] - h2 * sums[2]
    lower = a12 / a11
    c2 = (sums[6] - lower * sums[5]) / (a22 - lower * a12)
    c1 = sums[5] / a11 - lower * c2
    c0 = c1 * h1 + c2 * h2
    return (
        (alpha - c0) * v0 + c1 * z1 + c2 * v2,
        (alpha - c0) * q0 + c1 * zq1 + c2 * q2,
        r1 + c0 * y0 - c1 * yz - c2 * y2,
        rq1 + c0 * yq0 - c1 * yzq - c2 * yq2,
    )


def solution(mesh):
    placed = (
        P("comm", GROUP, None, None, None),
        P("comm", GROUP, None, None),
        P("comm", GROUP, None),
        P("comm", GROUP),
        P("comm", GROUP, None),
        P("comm", GROUP, None),
        P(GROUP, None),
        P("comm", GROUP, None, None),
        P(GROUP, None, None),
    )
    return jax.shard_map(
        body,
        mesh=mesh,
        in_specs=placed,
        out_specs=(
            P("comm", GROUP, None),
            P(GROUP, None),
            P("comm", GROUP, None),
            P(GROUP, None),
        ),
        check_vma=False,
    )
```

```python
import functools

import jax
import jax.numpy as jnp
from jax import lax
from jax.experimental import pallas as pl
from jax.experimental.pallas import tpu as pltpu
from jax.sharding import PartitionSpec as P

GROUP = ("stn", "tm")
F32 = jnp.float32
SLOT = 4
NOTE = 8
VMEM = pl.BlockSpec(memory_space=pltpu.VMEM)
SMEM = pl.BlockSpec(memory_space=pltpu.SMEM)


def kept(x):
    return pltpu.with_memory_space_constraint(x, pltpu.VMEM)


def call(kernel, outs, args, scalars=0, scratch=(), aliases=None, flops=0):
    outs = [o if not isinstance(o, tuple) else jax.ShapeDtypeStruct(o, F32) for o in outs]
    return pl.pallas_call(
        kernel,
        out_shape=outs,
        in_specs=[SMEM] * scalars + [VMEM] * (len(args) - scalars),
        out_specs=[VMEM] * len(outs),
        scratch_shapes=list(scratch),
        input_output_aliases=aliases or {},
        compiler_params=pltpu.CompilerParams(vmem_limit_bytes=16 * 1024 * 1024),
        cost_estimate=pl.CostEstimate(flops=flops, bytes_accessed=4 * 1024 * 1024, transcendentals=0),
    )(*args)


def down(block, column):
    return jnp.sum(block * jnp.broadcast_to(column, block.shape), axis=0, keepdims=True)


def fold(x):
    return jnp.sum(x, axis=0, keepdims=True)


def precondition(blocks_ref, x, out_ref):
    xt = x.T
    for i in range(x.shape[0]):
        out_ref[i : i + 1] = down(blocks_ref[i], xt[:, i : i + 1])


def turn_kernel(tiles_ref, cap_tiles_ref, turned_ref):
    touched = tiles_ref.shape[1]

    def one(i, _):
        for k in range(touched):
            turned_ref[i, k] = tiles_ref[i, k].T
        turned_ref[i, touched] = cap_tiles_ref[i].T
        return 0

    lax.fori_loop(0, tiles_ref.shape[0], one, 0)


def first_kernel(rhs_ref, precond_ref, v_ref, send_ref):
    precondition(precond_ref, rhs_ref[...], v_ref)
    send_ref[...] = jnp.broadcast_to(v_ref[...][None], send_ref.shape)


def near_kernel(comms, index_ref, v_ref, tiles_ref, up_ref, wide_ref):
    rows = v_ref.shape[0]
    blocks = rows // comms
    arcs = tiles_ref.shape[0] // comms
    vt = v_ref[...].T
    for i in range(rows):
        wide_ref[i] = jnp.broadcast_to(vt[:, i : i + 1], wide_ref.shape[1:])

    def one(i, _):
        c = i // arcs
        total = jnp.zeros(wide_ref.shape[1:], F32)
        for k in range(2):
            b = c * blocks + lax.rem(index_ref[i * 3 + k], blocks)
            total = total + tiles_ref[i, k] * wide_ref[b]
        up_ref[pl.ds(i, 1)] = fold(total)
        return 0

    lax.fori_loop(0, tiles_ref.shape[0], one, 0, unroll=4)


def cap_up(cap_index_ref, q_ref, cap_tiles_ref, up_ref, out_ref, wide_ref):
    qt = q_ref[...].T
    for i in range(q_ref.shape[0]):
        wide_ref[i] = jnp.broadcast_to(qt[:, i : i + 1], wide_ref.shape[1:])

    def one(i, _):
        out_ref[pl.ds(i, 1)] = up_ref[pl.ds(i, 1)] + fold(
            cap_tiles_ref[i] * wide_ref[cap_index_ref[i]]
        )
        return 0

    lax.fori_loop(0, cap_tiles_ref.shape[0], one, 0, unroll=4)


def cap_first_kernel(
    cap_index_ref, cap_rhs_ref, up_ref, cap_precond_ref, cap_tiles_ref, q_ref, out_ref, wide_ref
):
    precondition(cap_precond_ref, cap_rhs_ref[...], q_ref)
    cap_up(cap_index_ref, q_ref, cap_tiles_ref, up_ref, out_ref, wide_ref)


def cap_second_kernel(
    cap_index_ref, cap_rhs_ref, q0_ref, half_ref, other_ref, up_ref, cap_precond_ref, cap_tiles_ref,
    yq_ref, q_ref, sums_ref, out_ref, wide_ref,
):
    caps = q0_ref.shape[0]
    note = half_ref[...] + other_ref[...]
    q0 = q0_ref[...]
    yq_ref[...] = q0 + note[:caps]
    sums_ref[...] = note[caps:]
    sums_ref[0:1] += fold(cap_rhs_ref[...] * q0)
    sums_ref[1:2] += fold(q0 * q0)
    precondition(cap_precond_ref, yq_ref[...], q_ref)
    cap_up(cap_index_ref, q_ref, cap_tiles_ref, up_ref, out_ref, wide_ref)


def cap_third_kernel(
    cap_index_ref, alpha_ref, cap_rhs_ref, q0_ref, yq0_ref, q1_ref, half_ref, other_ref, up_ref,
    cap_precond_ref, cap_tiles_ref, zq_ref, yzq_ref, rq_ref, q_ref, sums_ref, out_ref, wide_ref,
):
    caps = q0_ref.shape[0]
    alpha = alpha_ref[0:1]
    yq0, q1 = yq0_ref[...], q1_ref[...]
    yq1 = q1 + half_ref[:caps] + other_ref[:caps]
    zq = q0_ref[...] - alpha * q1
    yzq = yq0 - alpha * yq1
    rq = cap_rhs_ref[...] - alpha * yq0
    zq_ref[...] = zq
    yzq_ref[...] = yzq
    rq_ref[...] = rq
    precondition(cap_precond_ref, alpha * yzq, q_ref)
    q = q_ref[...]
    pairs = ((zq, yq0), (zq, yzq), (q, yq0), (q, yzq), (q, q), (zq, rq), (q, rq))
    for n, (one, other) in enumerate(pairs):
        sums_ref[n : n + 1] = fold(one * other)
    sums_ref[7:8] = jnp.zeros_like(sums_ref[7:8])
    cap_up(cap_index_ref, q_ref, cap_tiles_ref, up_ref, out_ref, wide_ref)


def arcs_up(comms, index_ref, blocks, up_ref, got_ref, scale_ref, tiles_ref, far_ref, scaled_ref):
    count = up_ref.shape[0]
    arcs = count // comms
    for i in range(count):
        c = i // arcs
        far = index_ref[i * 3 + 2]
        row = c if got_ref.shape[1] == comms else c * blocks + lax.rem(far, blocks)
        far_ref[i : i + 1] = got_ref[lax.div(far, blocks), pl.ds(row, 1)]
    ft = far_ref[...].T
    for i in range(count):
        far_ref[i : i + 1] = up_ref[i : i + 1] + down(tiles_ref[i, 2], ft[:, i : i + 1])
    upward = far_ref[...]
    scaled = scale_ref[...] * upward
    scaled_ref[...] = scaled
    return fold(upward * scaled)


def arcs_down(comms, index_ref, cap_index_ref, blocks, scaled_ref, turned_ref, note_ref, local_ref,
              back_ref, first):
    count = scaled_ref.shape[0]
    arcs = count // comms
    st = scaled_ref[...].T
    if back_ref is not None:
        local_ref[...] = jnp.zeros_like(local_ref)
        if first:
            back_ref[...] = jnp.full(back_ref.shape, -1.0, F32)
    for i in range(count):
        c = i // arcs
        wide = jnp.broadcast_to(st[:, i : i + 1], turned_ref.shape[2:])
        if note_ref is not None:
            cap = cap_index_ref[i]
            note_ref[pl.ds(cap, 1)] += fold(turned_ref[i, 3] * wide)
        if back_ref is None:
            continue
        for k in range(2):
            b = c * blocks + lax.rem(index_ref[i * 3 + k], blocks)
            local_ref[pl.ds(b, 1)] += fold(turned_ref[i, k] * wide)
        far = index_ref[i * 3 + 2]
        to = lax.div(far, blocks)
        back_ref[to, c : c + 1] = fold(turned_ref[i, 2] * wide)
        if first:
            local = lax.rem(far, blocks).astype(F32)
            back_ref[to, comms + c : comms + c + 1] = jnp.full((1, back_ref.shape[2]), local, F32)


def both_kernel(comms, blocks, caps, first, index_ref, cap_index_ref, rhs_ref, v_ref, sums_ref, up_ref,
                got_ref, scale_ref, tiles_ref, turned_ref, note_ref, local_ref, back_ref, far_ref,
                scaled_ref):
    energy = arcs_up(comms, index_ref, blocks, up_ref, got_ref, scale_ref, tiles_ref, far_ref, scaled_ref)
    note_ref[...] = jnp.zeros_like(note_ref)
    arcs_down(comms, index_ref, cap_index_ref, blocks, scaled_ref, turned_ref, note_ref, local_ref,
              back_ref, first)
    if first:
        v = v_ref[...]
        note_ref[caps : caps + 1] = fold(rhs_ref[...] * v)
        note_ref[caps + 1 : caps + 2] = fold(v * v) + energy
    else:
        shape = (back_ref.shape[0], 2, back_ref.shape[2])
        back_ref[:, comms : comms + 2] = jnp.broadcast_to(sums_ref[0:2][None], shape)


def last_up_kernel(comms, blocks, caps, index_ref, cap_index_ref, z_ref, yz_ref, r_ref, y0_ref, v_ref,
                   up_ref, got_ref, scale_ref, tiles_ref, turned_ref, notes_ref, scaled_ref, far_ref,
                   note_ref):
    energy = arcs_up(comms, index_ref, blocks, up_ref, got_ref, scale_ref, tiles_ref, far_ref, scaled_ref)
    note_ref[...] = jnp.zeros_like(note_ref)
    arcs_down(comms, index_ref, cap_index_ref, blocks, scaled_ref, turned_ref, note_ref, None, None, False)
    z, yz, r, y0, v = z_ref[...], yz_ref[...], r_ref[...], y0_ref[...], v_ref[...]
    pairs = ((z, y0), (z, yz), (v, y0), (v, yz), (v, v), (z, r), (v, r))
    for n, (one, other) in enumerate(pairs):
        note_ref[caps + n : caps + n + 1] = fold(one * other)
    note_ref[caps + 4 : caps + 5] += energy
    notes_ref[...] = jnp.broadcast_to(note_ref[...][None], notes_ref.shape)


def last_down_kernel(comms, blocks, index_ref, scaled_ref, turned_ref, local_ref, back_ref):
    arcs_down(comms, index_ref, None, blocks, scaled_ref, turned_ref, None, local_ref, back_ref, False)


def insert_kernel(comms, caps, notes_ref, sums_ref, back_ref, cap_ref, out_ref):
    del back_ref
    total = jnp.sum(notes_ref[...], axis=0)
    cap_ref[...] = total[:caps]
    sums = jnp.sum(total[caps:] + sums_ref[...], axis=1, keepdims=True)
    width = out_ref.shape[2]
    pick = lax.broadcasted_iota(jnp.int32, (NOTE, width), 0) == lax.broadcasted_iota(
        jnp.int32, (NOTE, width), 1
    )
    row = fold(jnp.where(pick, jnp.broadcast_to(sums, (NOTE, width)), 0.0))
    out_ref[:, comms : comms + 1] = jnp.broadcast_to(row[None], (out_ref.shape[0], 1, width))


def collect(comms, v_ref, local_ref, back_ref, asked, y_ref):
    blocks = v_ref.shape[0] // comms
    for c in range(comms):
        part = back_ref[:, c]
        for b in range(blocks):
            n = c * blocks + b
            came = fold(jnp.where(asked[c] == b, part, 0.0))
            y_ref[n : n + 1] = v_ref[n : n + 1] + local_ref[n : n + 1] + came


def pack(comms, v_ref, asked, send_ref):
    blocks = v_ref.shape[0] // comms
    for c in range(comms):
        row = jnp.zeros_like(asked[c])
        for b in range(blocks):
            n = c * blocks + b
            row = jnp.where(asked[c] == b, v_ref[n : n + 1], row)
        send_ref[:, c] = row


def rows_second_kernel(comms, v0_ref, local_ref, back_ref, precond_ref, y_ref, v_ref, send_ref, asked_ref):
    asked = [back_ref[:, comms + c] for c in range(comms)]
    for c in range(comms):
        asked_ref[c] = asked[c]
    collect(comms, v0_ref, local_ref, back_ref, asked, y_ref)
    precondition(precond_ref, y_ref[...], v_ref)
    pack(comms, v_ref, asked, send_ref)


def rows_third_kernel(comms, rhs_ref, v0_ref, y0_ref, v1_ref, local_ref, back_ref, asked_ref, precond_ref,
                      alpha_ref, z_ref, yz_ref, r_ref, v_ref, send_ref):
    asked = [asked_ref[c] for c in range(comms)]
    collect(comms, v1_ref, local_ref, back_ref, asked, yz_ref)
    first = jnp.sum(fold(back_ref[:, comms]), axis=1, keepdims=True)
    second = jnp.sum(fold(back_ref[:, comms + 1]), axis=1, keepdims=True)
    alpha = jnp.broadcast_to(first / second, (1, alpha_ref.shape[1]))
    alpha_ref[...] = jnp.broadcast_to(alpha, alpha_ref.shape)
    alpha_ref[1:2] = jnp.broadcast_to(second, (1, alpha_ref.shape[1]))
    y0 = y0_ref[...]
    z_ref[...] = v0_ref[...] - alpha * v1_ref[...]
    yz = y0 - alpha * yz_ref[...]
    yz_ref[...] = yz
    r_ref[...] = rhs_ref[...] - alpha * y0
    precondition(precond_ref, alpha * yz, v_ref)
    pack(comms, v_ref, asked, send_ref)


def last_kernel(comms, alpha_ref, v0_ref, y0_ref, z_ref, yz_ref, r_ref, v2_ref, local_ref, back_ref,
                asked_ref, q0_ref, yq0_ref, zq_ref, yzq_ref, rq_ref, q2_ref, cap_ref,
                sol_ref, cap_sol_ref, res_ref, cap_res_ref, y_ref):
    asked = [asked_ref[c] for c in range(comms)]
    collect(comms, v2_ref, local_ref, back_ref, asked, y_ref)
    row = fold(back_ref[:, comms])
    width = row.shape[1]
    lane = lax.broadcasted_iota(jnp.int32, row.shape, 1)
    s = [
        jnp.broadcast_to(
            jnp.sum(jnp.where(lane == n, row, 0.0), axis=1, keepdims=True), (1, width)
        )
        for n in range(7)
    ]
    alpha, h00 = alpha_ref[0:1], alpha_ref[1:2]
    h1, h2 = s[0] / h00, s[2] / h00
    a11 = s[1] - h1 * s[0]
    a12 = s[3] - h1 * s[2]
    a22 = s[4] - h2 * s[2]
    lower = a12 / a11
    c2 = (s[6] - lower * s[5]) / (a22 - lower * a12)
    c1 = s[5] / a11 - lower * c2
    c0 = c1 * h1 + c2 * h2
    sol_ref[...] = (alpha - c0) * v0_ref[...] + c1 * z_ref[...] + c2 * v2_ref[...]
    cap_sol_ref[...] = (alpha - c0) * q0_ref[...] + c1 * zq_ref[...] + c2 * q2_ref[...]
    res_ref[...] = r_ref[...] + c0 * y0_ref[...] - c1 * yz_ref[...] - c2 * y_ref[...]
    yq2 = q2_ref[...] + cap_ref[...]
    cap_res_ref[...] = rq_ref[...] + c0 * yq0_ref[...] - c1 * yzq_ref[...] - c2 * yq2


def body(
    tiles, cap_tiles, row_index, cap_index, arc_scale, rows_rhs, cap_rhs, precond, cap_precond
):
    comms, arcs, touched = row_index.shape
    blocks, width = rows_rhs.shape[1:]
    caps = cap_rhs.shape[0]
    groups = lax.axis_size("stn") * lax.axis_size("tm")
    peers = lax.axis_size("comm")
    rows, count = comms * blocks, comms * arcs
    flat = (width, width)
    tiles = kept(tiles.reshape(count, touched, *flat))
    cap_tiles = kept(cap_tiles.reshape(count, *flat))
    precond = kept(precond.reshape(rows, *flat))
    cap_precond = kept(cap_precond)
    index = row_index.reshape(-1)
    cap_index = cap_index.reshape(-1)
    scale = arc_scale.reshape(count, width)
    rhs = rows_rhs.reshape(rows, width)
    row_shape, cap_shape, arc_shape = (rows, width), (caps, width), (count, width)
    wide_rows = pltpu.VMEM((rows, *flat), F32)
    wide_caps = pltpu.VMEM((caps, *flat), F32)
    arc_scratch = pltpu.VMEM(arc_shape, F32)
    small = (NOTE, width)
    note_shape = (caps + NOTE, width)
    send_shape = (groups, comms, width)
    back_shape = (groups, SLOT, width)
    near_flops, far_flops = 2 * count * width * width, 10 * count * width * width

    def exchange(x):
        return lax.all_to_all(x, GROUP, 0, 0)

    def near(v):
        (up,) = call(
            functools.partial(near_kernel, comms), [arc_shape], (index, v, tiles), 1, [wide_rows],
            flops=near_flops,
        )
        return up

    def across(x, step):
        return lax.ppermute(x, "comm", [(i, i ^ step) for i in range(peers)])

    v0, send = call(first_kernel, [row_shape, (groups, rows, width)], (rhs, precond))
    got = exchange(send)
    (turned,) = call(
        turn_kernel, [pltpu.VMEM((count, touched + 1, *flat), F32)], (tiles, cap_tiles), flops=far_flops
    )
    turned = kept(turned)
    up = near(v0)
    q0, up = call(
        cap_first_kernel, [cap_shape, arc_shape], (cap_index, cap_rhs, up, cap_precond, cap_tiles), 1,
        [wide_caps], flops=near_flops,
    )

    def both(first, v, sums, up, got):
        return call(
            functools.partial(both_kernel, comms, blocks, caps, first),
            [note_shape, row_shape, back_shape],
            (index, cap_index, rhs, v, sums, up, got, scale, tiles, turned),
            2,
            [arc_scratch, arc_scratch],
            flops=far_flops,
        )

    note, local, back = both(True, v0, rhs, up, got)
    back = exchange(back)
    note = note + across(note, 1)
    note = note + across(note, 2)
    y0, v1, send, asked = call(
        functools.partial(rows_second_kernel, comms),
        [row_shape, row_shape, send_shape, (comms, groups, width)],
        (v0, local, back, precond),
    )
    got = exchange(send)
    other = across(note, 4)
    up = near(v1)
    yq0, q1, sums, up = call(
        cap_second_kernel, [cap_shape, cap_shape, small, arc_shape],
        (cap_index, cap_rhs, q0, note, other, up, cap_precond, cap_tiles), 1, [wide_caps],
        flops=near_flops,
    )
    note, local, back = both(False, v1, sums, up, got)
    back = exchange(back)
    note = note + across(note, 1)
    note = note + across(note, 2)
    alpha, z1, yz, r1, v2, send = call(
        functools.partial(rows_third_kernel, comms),
        [small, row_shape, row_shape, row_shape, row_shape, send_shape],
        (rhs, v0, y0, v1, local, back, asked, precond),
    )
    got = exchange(send)
    other = across(note, 4)
    up = near(v2)
    zq1, yzq, rq1, q2, sums, up = call(
        cap_third_kernel, [cap_shape] * 4 + [small, arc_shape],
        (cap_index, alpha, cap_rhs, q0, yq0, q1, note, other, up, cap_precond, cap_tiles), 1, [wide_caps],
        flops=near_flops,
    )
    notes, scaled = call(
        functools.partial(last_up_kernel, comms, blocks, caps),
        [(peers, *note_shape), arc_shape],
        (index, cap_index, z1, yz, r1, y0, v2, up, got, scale, tiles, turned), 2,
        [arc_scratch, pltpu.VMEM(note_shape, F32)],
        flops=near_flops,
    )
    notes = lax.all_to_all(notes, "comm", 0, 0)
    local, back = call(
        functools.partial(last_down_kernel, comms, blocks), [row_shape, back_shape],
        (index, scaled, turned), 1, flops=far_flops,
    )
    cap_sum, back = call(
        functools.partial(insert_kernel, comms, caps), [cap_shape, back_shape], (notes, sums, back),
        aliases={2: 1},
    )
    back = exchange(back)
    sol, cap_sol, res, cap_res = call(
        functools.partial(last_kernel, comms), [row_shape, cap_shape, row_shape, cap_shape],
        (alpha, v0, y0, z1, yz, r1, v2, local, back, asked, q0, yq0, zq1, yzq, rq1, q2, cap_sum), 0,
        [pltpu.VMEM(row_shape, F32)],
    )
    return sol.reshape(rows_rhs.shape), cap_sol, res.reshape(rows_rhs.shape), cap_res


def solution(mesh):
    placed = (
        P("comm", GROUP, None, None, None),
        P("comm", GROUP, None, None),
        P("comm", GROUP, None),
        P("comm", GROUP),
        P("comm", GROUP, None),
        P("comm", GROUP, None),
        P(GROUP, None),
        P("comm", GROUP, None, None),
        P(GROUP, None, None),
    )
    return jax.shard_map(
        body,
        mesh=mesh,
        in_specs=placed,
        out_specs=(
            P("comm", GROUP, None),
            P(GROUP, None),
            P("comm", GROUP, None),
            P(GROUP, None),
        ),
        check_vma=False,
    )
```

```python
import functools

import jax
import jax.numpy as jnp
from jax import lax
from jax.experimental import pallas as pl
from jax.experimental.pallas import tpu as pltpu
from jax.sharding import PartitionSpec as P

GROUP = ("stn", "tm")
F32 = jnp.float32
SLOT = 4
NOTE = 8
VMEM = pl.BlockSpec(memory_space=pltpu.VMEM)
SMEM = pl.BlockSpec(memory_space=pltpu.SMEM)
HBM = pl.BlockSpec(memory_space=pltpu.HBM)
PARTS = 4


def call(kernel, outs, args, scalars=0, scratch=(), aliases=None, flops=0, hbm=(), hbm_outs=()):
    outs = [
        pltpu.HBM(o, F32) if n in hbm_outs else jax.ShapeDtypeStruct(o, F32) for n, o in enumerate(outs)
    ]
    args = [
        pltpu.with_memory_space_constraint(x, pltpu.HBM) if n in hbm else x for n, x in enumerate(args)
    ]
    specs = [SMEM] * scalars + [VMEM] * (len(args) - scalars)
    return pl.pallas_call(
        kernel,
        out_shape=outs,
        in_specs=[HBM if n in hbm else spec for n, spec in enumerate(specs)],
        out_specs=[HBM if n in hbm_outs else VMEM for n in range(len(outs))],
        scratch_shapes=list(scratch),
        input_output_aliases=aliases or {},
        compiler_params=pltpu.CompilerParams(vmem_limit_bytes=32 * 1024 * 1024),
        cost_estimate=pl.CostEstimate(flops=flops, bytes_accessed=4 * 1024 * 1024, transcendentals=0),
    )(*args)


def fetch(source, target, sems, first, parts):
    step = target.shape[0] // parts
    copies = []
    for n in range(parts):
        part = pl.ds(n * step, step)
        copies.append(pltpu.make_async_copy(source.at[part], target.at[part], sems.at[first + n]))
        copies[-1].start()
    return copies


def down(block, column):
    return jnp.sum(block * jnp.broadcast_to(column, block.shape), axis=0, keepdims=True)


def fold(x):
    return jnp.sum(x, axis=0, keepdims=True)


def precondition(blocks_ref, x, out_ref, copies=()):
    xt = x.T
    for i in range(x.shape[0]):
        if copies and i % (x.shape[0] // len(copies)) == 0:
            copies[i // (x.shape[0] // len(copies))].wait()
        out_ref[i : i + 1] = down(blocks_ref[i], xt[:, i : i + 1])


def first_kernel(rhs_hbm, precond_hbm, v_ref, send_ref, rhs_ref, precond_ref, sems):
    (small,) = fetch(rhs_hbm, rhs_ref, sems, PARTS, 1)
    copies = fetch(precond_hbm, precond_ref, sems, 0, PARTS)
    small.wait()
    precondition(precond_ref, rhs_ref[...], v_ref, copies)
    send_ref[...] = jnp.broadcast_to(v_ref[...][None], send_ref.shape)


def widen(x, wide_ref):
    xt = x.T
    for i in range(x.shape[0]):
        wide_ref[i] = jnp.broadcast_to(xt[:, i : i + 1], wide_ref.shape[1:])


def own_rows(i, blocks, arcs, index_ref, tiles_ref, wide_ref):
    c, j = lax.div(i, arcs), lax.rem(i, arcs)
    total = tiles_ref[i, 0] * wide_ref[c * blocks + lax.rem(index_ref[0, c, j], blocks)]
    return total + tiles_ref[i, 1] * wide_ref[c * blocks + lax.rem(index_ref[1, c, j], blocks)]


def start_kernel(comms, index_ref, cap_index_ref, v_ref, cap_rhs_ref, tiles_hbm, cap_tiles_hbm, cap_precond_hbm,
                 up_ref, q_ref, turned_hbm, cap_turned_hbm, tiles_ref, third_ref, turned_ref, cap_turned_ref,
                 cap_tiles_ref, cap_precond_ref, wide_ref, cap_wide_ref, sems):
    count = up_ref.shape[0]
    arcs = count // comms
    blocks = v_ref.shape[0] // comms
    (pre,) = fetch(cap_precond_hbm, cap_precond_ref, sems, 5 * PARTS, 1)
    own = fetch(tiles_hbm.at[:, pl.ds(0, 2)], tiles_ref, sems, 0, PARTS)
    caps = fetch(cap_tiles_hbm, cap_tiles_ref, sems, PARTS, PARTS)
    thirds = fetch(tiles_hbm.at[:, 2], third_ref, sems, 2 * PARTS, PARTS)
    widen(v_ref[...], wide_ref)
    pre.wait()
    precondition(cap_precond_ref, cap_rhs_ref[...], q_ref)
    widen(q_ref[...], cap_wide_ref)
    step = count // PARTS
    out = []
    for n in range(PARTS):
        own[n].wait()
        caps[n].wait()
        thirds[n].wait()

        def one(i, _):
            total = own_rows(i, blocks, arcs, index_ref, tiles_ref, wide_ref)
            cap = cap_index_ref[lax.div(i, arcs), lax.rem(i, arcs)]
            up_ref[pl.ds(i, 1)] = fold(total + cap_tiles_ref[i] * cap_wide_ref[cap])
            for k in range(2):
                turned_ref[i, k] = tiles_ref[i, k].T
            turned_ref[i, 2] = third_ref[i].T
            cap_turned_ref[i] = cap_tiles_ref[i].T
            return 0

        lax.fori_loop(n * step, (n + 1) * step, one, 0)
        part = pl.ds(n * step, step)
        out.append(
            pltpu.make_async_copy(turned_ref.at[part], turned_hbm.at[part], sems.at[3 * PARTS + n])
        )
        out[-1].start()
        out.append(
            pltpu.make_async_copy(
                cap_turned_ref.at[part], cap_turned_hbm.at[part], sems.at[4 * PARTS + n]
            )
        )
        out[-1].start()
    for copy in out:
        copy.wait()


def near_kernel(comms, index_ref, v_ref, tiles_hbm, up_ref, tiles_ref, wide_ref, sems):
    count = up_ref.shape[0]
    arcs = count // comms
    blocks = v_ref.shape[0] // comms
    own = fetch(tiles_hbm.at[:, pl.ds(0, 2)], tiles_ref, sems, 0, PARTS)
    widen(v_ref[...], wide_ref)
    step = count // PARTS
    for n in range(PARTS):
        own[n].wait()

        def one(i, _):
            up_ref[pl.ds(i, 1)] = fold(own_rows(i, blocks, arcs, index_ref, tiles_ref, wide_ref))
            return 0

        lax.fori_loop(n * step, (n + 1) * step, one, 0, unroll=4)


def cap_up(comms, cap_index_ref, q_ref, cap_tiles_ref, up_ref, out_ref, wide_ref, copy):
    copy.wait()
    arcs = out_ref.shape[0] // comms
    widen(q_ref[...], wide_ref)

    def one(i, _):
        cap = cap_index_ref[lax.div(i, arcs), lax.rem(i, arcs)]
        out_ref[pl.ds(i, 1)] = up_ref[pl.ds(i, 1)] + fold(cap_tiles_ref[i] * wide_ref[cap])
        return 0

    lax.fori_loop(0, cap_tiles_ref.shape[0], one, 0, unroll=4)


def cap_second_kernel(
    comms, cap_index_ref, cap_rhs_ref, q0_ref, half_ref, other_ref, up_ref, cap_precond_hbm, cap_tiles_hbm,
    yq_ref, q_ref, sums_ref, out_ref, wide_ref, cap_precond_ref, cap_tiles_ref, sems,
):
    (pre,) = fetch(cap_precond_hbm, cap_precond_ref, sems, 0, 1)
    (caps_in,) = fetch(cap_tiles_hbm, cap_tiles_ref, sems, 1, 1)
    caps = q0_ref.shape[0]
    note = half_ref[...] + other_ref[...]
    q0 = q0_ref[...]
    yq_ref[...] = q0 + note[:caps]
    sums_ref[...] = note[caps:]
    sums_ref[0:1] += fold(cap_rhs_ref[...] * q0)
    sums_ref[1:2] += fold(q0 * q0)
    precondition(cap_precond_ref, yq_ref[...], q_ref, [pre])
    cap_up(comms, cap_index_ref, q_ref, cap_tiles_ref, up_ref, out_ref, wide_ref, caps_in)


def cap_third_kernel(
    comms, cap_index_ref, alpha_ref, cap_rhs_ref, q0_ref, yq0_ref, q1_ref, half_ref, other_ref, up_ref,
    cap_precond_hbm, cap_tiles_hbm, zq_ref, yzq_ref, rq_ref, q_ref, sums_ref, out_ref, wide_ref,
    cap_precond_ref, cap_tiles_ref, sems,
):
    (pre,) = fetch(cap_precond_hbm, cap_precond_ref, sems, 0, 1)
    (caps_in,) = fetch(cap_tiles_hbm, cap_tiles_ref, sems, 1, 1)
    caps = q0_ref.shape[0]
    alpha = alpha_ref[0:1]
    yq0, q1 = yq0_ref[...], q1_ref[...]
    yq1 = q1 + half_ref[:caps] + other_ref[:caps]
    zq = q0_ref[...] - alpha * q1
    yzq = yq0 - alpha * yq1
    rq = cap_rhs_ref[...] - alpha * yq0
    zq_ref[...] = zq
    yzq_ref[...] = yzq
    rq_ref[...] = rq
    precondition(cap_precond_ref, alpha * yzq, q_ref, [pre])
    q = q_ref[...]
    pairs = ((zq, yq0), (zq, yzq), (q, yq0), (q, yzq), (q, q), (zq, rq), (q, rq))
    for n, (one, other) in enumerate(pairs):
        sums_ref[n : n + 1] = fold(one * other)
    sums_ref[7:8] = jnp.zeros_like(sums_ref[7:8])
    cap_up(comms, cap_index_ref, q_ref, cap_tiles_ref, up_ref, out_ref, wide_ref, caps_in)


def arcs_up(comms, index_ref, blocks, up_ref, got_ref, scale_ref, third_ref, far_ref, scaled_ref, copies):
    count = up_ref.shape[0]
    arcs = count // comms
    for i in range(count):
        c = i // arcs
        far = index_ref[2, c, i % arcs]
        row = c if got_ref.shape[1] == comms else c * blocks + lax.rem(far, blocks)
        far_ref[i : i + 1] = got_ref[lax.div(far, blocks), pl.ds(row, 1)]
    ft = far_ref[...].T
    for i in range(count):
        if i % (count // len(copies)) == 0:
            copies[i // (count // len(copies))].wait()
        far_ref[i : i + 1] = up_ref[i : i + 1] + down(third_ref[i], ft[:, i : i + 1])
    upward = far_ref[...]
    scaled = scale_ref[...] * upward
    scaled_ref[...] = scaled
    return fold(upward * scaled)


def arcs_cap(comms, cap_index_ref, scaled_ref, cap_turned_ref, note_ref, copies):
    count = scaled_ref.shape[0]
    arcs = count // comms
    st = scaled_ref[...].T
    for i in range(count):
        if i % (count // len(copies)) == 0:
            copies[i // (count // len(copies))].wait()
        cap = cap_index_ref[i // arcs, i % arcs]
        note_ref[pl.ds(cap, 1)] += down(cap_turned_ref[i], st[:, i : i + 1])


def arcs_rows(comms, index_ref, blocks, scaled_ref, turned_ref, local_ref, back_ref, first, copies):
    count = scaled_ref.shape[0]
    arcs = count // comms
    st = scaled_ref[...].T
    local_ref[...] = jnp.zeros_like(local_ref)
    if first:
        back_ref[...] = jnp.full(back_ref.shape, -1.0, F32)
    for i in range(count):
        if i % (count // len(copies)) == 0:
            copies[i // (count // len(copies))].wait()
        c, j = i // arcs, i % arcs
        wide = jnp.broadcast_to(st[:, i : i + 1], turned_ref.shape[2:])
        for k in range(2):
            b = c * blocks + lax.rem(index_ref[k, c, j], blocks)
            local_ref[pl.ds(b, 1)] += fold(turned_ref[i, k] * wide)
        far = index_ref[2, c, j]
        to = lax.div(far, blocks)
        back_ref[to, c : c + 1] = fold(turned_ref[i, 2] * wide)
        if first:
            local = lax.rem(far, blocks).astype(F32)
            back_ref[to, comms + c : comms + c + 1] = jnp.full((1, back_ref.shape[2]), local, F32)


def both_kernel(comms, blocks, caps, first, index_ref, cap_index_ref, rhs_ref, v_ref, sums_ref, up_ref, got_ref,
                scale_ref, tiles_hbm, turned_hbm, cap_turned_hbm, note_ref, local_ref, back_ref, far_ref,
                scaled_ref, third_ref, turned_ref, cap_turned_ref, sems):
    thirds = fetch(tiles_hbm.at[:, 2], third_ref, sems, 0, PARTS)
    caps_in = fetch(cap_turned_hbm, cap_turned_ref, sems, PARTS, PARTS)
    rows_in = fetch(turned_hbm, turned_ref, sems, 2 * PARTS, PARTS)
    energy = arcs_up(comms, index_ref, blocks, up_ref, got_ref, scale_ref, third_ref, far_ref, scaled_ref, thirds)
    note_ref[...] = jnp.zeros_like(note_ref)
    arcs_cap(comms, cap_index_ref, scaled_ref, cap_turned_ref, note_ref, caps_in)
    arcs_rows(comms, index_ref, blocks, scaled_ref, turned_ref, local_ref, back_ref, first, rows_in)
    if first:
        v = v_ref[...]
        note_ref[caps : caps + 1] = fold(rhs_ref[...] * v)
        note_ref[caps + 1 : caps + 2] = fold(v * v) + energy
    else:
        shape = (back_ref.shape[0], 2, back_ref.shape[2])
        back_ref[:, comms : comms + 2] = jnp.broadcast_to(sums_ref[0:2][None], shape)


def last_up_kernel(comms, blocks, caps, index_ref, cap_index_ref, z_ref, yz_ref, r_ref, y0_ref, v_ref,
                   up_ref, got_ref, scale_ref, tiles_hbm, cap_turned_hbm, notes_ref, scaled_ref, far_ref,
                   note_ref, third_ref, cap_turned_ref, sems):
    thirds = fetch(tiles_hbm.at[:, 2], third_ref, sems, 0, PARTS)
    caps_in = fetch(cap_turned_hbm, cap_turned_ref, sems, PARTS, PARTS)
    energy = arcs_up(comms, index_ref, blocks, up_ref, got_ref, scale_ref, third_ref, far_ref, scaled_ref, thirds)
    note_ref[...] = jnp.zeros_like(note_ref)
    arcs_cap(comms, cap_index_ref, scaled_ref, cap_turned_ref, note_ref, caps_in)
    z, yz, r, y0, v = z_ref[...], yz_ref[...], r_ref[...], y0_ref[...], v_ref[...]
    pairs = ((z, y0), (z, yz), (v, y0), (v, yz), (v, v), (z, r), (v, r))
    for n, (one, other) in enumerate(pairs):
        note_ref[caps + n : caps + n + 1] = fold(one * other)
    note_ref[caps + 4 : caps + 5] += energy
    notes_ref[...] = jnp.broadcast_to(note_ref[...][None], notes_ref.shape)


def last_down_kernel(comms, blocks, index_ref, scaled_ref, turned_hbm, local_ref, back_ref, turned_ref, sems):
    rows_in = fetch(turned_hbm, turned_ref, sems, 0, PARTS)
    arcs_rows(comms, index_ref, blocks, scaled_ref, turned_ref, local_ref, back_ref, False, rows_in)


def insert_kernel(comms, caps, notes_ref, sums_ref, back_ref, cap_ref, out_ref):
    del back_ref
    total = jnp.sum(notes_ref[...], axis=0)
    cap_ref[...] = total[:caps]
    sums = jnp.sum(total[caps:] + sums_ref[...], axis=1, keepdims=True)
    width = out_ref.shape[2]
    pick = lax.broadcasted_iota(jnp.int32, (NOTE, width), 0) == lax.broadcasted_iota(
        jnp.int32, (NOTE, width), 1
    )
    row = fold(jnp.where(pick, jnp.broadcast_to(sums, (NOTE, width)), 0.0))
    out_ref[:, comms : comms + 1] = jnp.broadcast_to(row[None], (out_ref.shape[0], 1, width))


def collect(comms, v_ref, local_ref, back_ref, asked, y_ref):
    blocks = v_ref.shape[0] // comms
    for c in range(comms):
        part = back_ref[:, c]
        for b in range(blocks):
            n = c * blocks + b
            came = fold(jnp.where(asked[c] == b, part, 0.0))
            y_ref[n : n + 1] = v_ref[n : n + 1] + local_ref[n : n + 1] + came


def pack(comms, v_ref, asked, send_ref):
    blocks = v_ref.shape[0] // comms
    for c in range(comms):
        row = jnp.zeros_like(asked[c])
        for b in range(blocks):
            n = c * blocks + b
            row = jnp.where(asked[c] == b, v_ref[n : n + 1], row)
        send_ref[:, c] = row


def rows_second_kernel(comms, v0_ref, local_ref, back_ref, note_ref, came_ref, precond_hbm, half_ref, y_ref,
                       v_ref, send_ref, asked_ref, precond_ref, sems):
    (pre,) = fetch(precond_hbm, precond_ref, sems, 0, 1)
    half_ref[...] = note_ref[...] + came_ref[...]
    asked = [back_ref[:, comms + c] for c in range(comms)]
    for c in range(comms):
        asked_ref[c] = asked[c]
    collect(comms, v0_ref, local_ref, back_ref, asked, y_ref)
    precondition(precond_ref, y_ref[...], v_ref, [pre])
    pack(comms, v_ref, asked, send_ref)


def rows_third_kernel(comms, rhs_ref, v0_ref, y0_ref, v1_ref, local_ref, back_ref, note_ref, came_ref, asked_ref,
                      precond_hbm, half_ref, alpha_ref, z_ref, yz_ref, r_ref, v_ref, send_ref, precond_ref,
                      sems):
    (pre,) = fetch(precond_hbm, precond_ref, sems, 0, 1)
    half_ref[...] = note_ref[...] + came_ref[...]
    asked = [asked_ref[c] for c in range(comms)]
    collect(comms, v1_ref, local_ref, back_ref, asked, yz_ref)
    first = jnp.sum(fold(back_ref[:, comms]), axis=1, keepdims=True)
    second = jnp.sum(fold(back_ref[:, comms + 1]), axis=1, keepdims=True)
    alpha = jnp.broadcast_to(first / second, (1, alpha_ref.shape[1]))
    alpha_ref[...] = jnp.broadcast_to(alpha, alpha_ref.shape)
    alpha_ref[1:2] = jnp.broadcast_to(second, (1, alpha_ref.shape[1]))
    y0 = y0_ref[...]
    z_ref[...] = v0_ref[...] - alpha * v1_ref[...]
    yz = y0 - alpha * yz_ref[...]
    yz_ref[...] = yz
    r_ref[...] = rhs_ref[...] - alpha * y0
    precondition(precond_ref, alpha * yz, v_ref, [pre])
    pack(comms, v_ref, asked, send_ref)


def last_kernel(comms, alpha_ref, v0_ref, y0_ref, z_ref, yz_ref, r_ref, v2_ref, local_ref, back_ref,
                asked_ref, q0_ref, yq0_ref, zq_ref, yzq_ref, rq_ref, q2_ref, cap_ref,
                sol_ref, cap_sol_ref, res_ref, cap_res_ref, y_ref):
    asked = [asked_ref[c] for c in range(comms)]
    collect(comms, v2_ref, local_ref, back_ref, asked, y_ref)
    row = fold(back_ref[:, comms])
    width = row.shape[1]
    lane = lax.broadcasted_iota(jnp.int32, row.shape, 1)
    s = [
        jnp.broadcast_to(
            jnp.sum(jnp.where(lane == n, row, 0.0), axis=1, keepdims=True), (1, width)
        )
        for n in range(7)
    ]
    alpha, h00 = alpha_ref[0:1], alpha_ref[1:2]
    h1, h2 = s[0] / h00, s[2] / h00
    a11 = s[1] - h1 * s[0]
    a12 = s[3] - h1 * s[2]
    a22 = s[4] - h2 * s[2]
    lower = a12 / a11
    c2 = (s[6] - lower * s[5]) / (a22 - lower * a12)
    c1 = s[5] / a11 - lower * c2
    c0 = c1 * h1 + c2 * h2
    sol_ref[...] = (alpha - c0) * v0_ref[...] + c1 * z_ref[...] + c2 * v2_ref[...]
    cap_sol_ref[...] = (alpha - c0) * q0_ref[...] + c1 * zq_ref[...] + c2 * q2_ref[...]
    res_ref[...] = r_ref[...] + c0 * y0_ref[...] - c1 * yz_ref[...] - c2 * y_ref[...]
    yq2 = q2_ref[...] + cap_ref[...]
    cap_res_ref[...] = rq_ref[...] + c0 * yq0_ref[...] - c1 * yzq_ref[...] - c2 * yq2


def body(
    tiles, cap_tiles, row_index, cap_index, arc_scale, rows_rhs, cap_rhs, precond, cap_precond
):
    comms, arcs, touched = row_index.shape
    blocks, width = rows_rhs.shape[1:]
    caps = cap_rhs.shape[0]
    groups = lax.axis_size("stn") * lax.axis_size("tm")
    peers = lax.axis_size("comm")
    rows, count = comms * blocks, comms * arcs
    flat = (width, width)
    tiles = tiles.reshape(count, touched, *flat)
    cap_tiles = cap_tiles.reshape(count, *flat)
    precond = precond.reshape(rows, *flat)
    index = jnp.transpose(row_index, (2, 0, 1))
    scale = arc_scale.reshape(count, width)
    rhs = rows_rhs.reshape(rows, width)
    row_shape, cap_shape, arc_shape = (rows, width), (caps, width), (count, width)
    tall, cap_tall = (count, touched, *flat), (count, *flat)
    wide_rows = pltpu.VMEM((rows, *flat), F32)
    wide_caps = pltpu.VMEM((caps, *flat), F32)
    own_tiles = pltpu.VMEM((count, 2, *flat), F32)
    cap_blocks = pltpu.VMEM((caps, *flat), F32)
    row_blocks = pltpu.VMEM((rows, *flat), F32)
    cap_scratch = pltpu.VMEM(cap_tall, F32)
    arc_scratch = pltpu.VMEM(arc_shape, F32)
    small = (NOTE, width)
    note_shape = (caps + NOTE, width)
    send_shape = (groups, comms, width)
    back_shape = (groups, SLOT, width)
    unit = 2 * count * width * width

    def exchange(x):
        return lax.all_to_all(x, GROUP, 0, 0)

    def across(x, step):
        return lax.ppermute(x, "comm", [(i, i ^ step) for i in range(peers)])

    def sems(n):
        return pltpu.SemaphoreType.DMA((n,))

    v0, send = call(
        first_kernel, [row_shape, (groups, rows, width)], (rhs, precond), 0,
        [pltpu.VMEM(row_shape, F32), pltpu.VMEM((rows, *flat), F32), sems(PARTS + 1)], hbm=(0, 1),
    )
    got = exchange(send)
    up, q0, turned, cap_turned = call(
        functools.partial(start_kernel, comms),
        [arc_shape, cap_shape, tall, cap_tall],
        (index, cap_index, v0, cap_rhs, tiles, cap_tiles, cap_precond),
        2,
        [own_tiles, cap_scratch, pltpu.VMEM(tall, F32), cap_scratch, cap_scratch, cap_blocks, wide_rows, wide_caps,
         sems(5 * PARTS + 1)],
        flops=8 * unit,
        hbm=(4, 5, 6),
        hbm_outs=(2, 3),
    )

    def both(first, v, sums, up, got):
        return call(
            functools.partial(both_kernel, comms, blocks, caps, first),
            [note_shape, row_shape, back_shape],
            (index, cap_index, rhs, v, sums, up, got, scale, tiles, turned, cap_turned),
            2,
            [arc_scratch, arc_scratch, cap_scratch, pltpu.VMEM(tall, F32), cap_scratch, sems(3 * PARTS)],
            flops=5 * unit,
            hbm=(8, 9, 10),
        )

    def near(v):
        (up,) = call(
            functools.partial(near_kernel, comms),
            [arc_shape],
            (index, v, tiles),
            1,
            [own_tiles, wide_rows, sems(PARTS)],
            flops=2 * unit,
            hbm=(2,),
        )
        return up

    note, local, back = both(True, v0, rhs, up, got)
    back = exchange(back)
    note = note + across(note, 1)
    half, y0, v1, send, asked = call(
        functools.partial(rows_second_kernel, comms),
        [note_shape, row_shape, row_shape, send_shape, (comms, groups, width)],
        (v0, local, back, note, across(note, 2), precond), 0, [row_blocks, sems(1)], hbm=(5,),
    )
    got = exchange(send)
    other = across(half, 4)
    cap_room = [wide_caps, cap_blocks, cap_scratch, sems(2)]
    up = near(v1)
    yq0, q1, sums, up = call(
        functools.partial(cap_second_kernel, comms), [cap_shape, cap_shape, small, arc_shape],
        (cap_index, cap_rhs, q0, half, other, up, cap_precond, cap_tiles), 1, cap_room, flops=2 * unit,
        hbm=(6, 7),
    )
    note, local, back = both(False, v1, sums, up, got)
    back = exchange(back)
    note = note + across(note, 1)
    half, alpha, z1, yz, r1, v2, send = call(
        functools.partial(rows_third_kernel, comms),
        [note_shape, small, row_shape, row_shape, row_shape, row_shape, send_shape],
        (rhs, v0, y0, v1, local, back, note, across(note, 2), asked, precond), 0, [row_blocks, sems(1)],
        hbm=(9,),
    )
    got = exchange(send)
    other = across(half, 4)
    up = near(v2)
    zq1, yzq, rq1, q2, sums, up = call(
        functools.partial(cap_third_kernel, comms), [cap_shape] * 4 + [small, arc_shape],
        (cap_index, alpha, cap_rhs, q0, yq0, q1, half, other, up, cap_precond, cap_tiles), 1, cap_room,
        flops=2 * unit, hbm=(9, 10),
    )
    notes, scaled = call(
        functools.partial(last_up_kernel, comms, blocks, caps),
        [(peers, *note_shape), arc_shape],
        (index, cap_index, z1, yz, r1, y0, v2, up, got, scale, tiles, cap_turned), 2,
        [arc_scratch, pltpu.VMEM(note_shape, F32), cap_scratch, cap_scratch, sems(2 * PARTS)],
        flops=2 * unit,
        hbm=(10, 11),
    )
    notes = lax.all_to_all(notes, "comm", 0, 0)
    local, back = call(
        functools.partial(last_down_kernel, comms, blocks), [row_shape, back_shape],
        (index, scaled, turned), 1, [pltpu.VMEM(tall, F32), sems(PARTS)], flops=3 * unit, hbm=(2,),
    )
    cap_sum, back = call(
        functools.partial(insert_kernel, comms, caps), [cap_shape, back_shape], (notes, sums, back),
        aliases={2: 1},
    )
    back = exchange(back)
    sol, cap_sol, res, cap_res = call(
        functools.partial(last_kernel, comms), [row_shape, cap_shape, row_shape, cap_shape],
        (alpha, v0, y0, z1, yz, r1, v2, local, back, asked, q0, yq0, zq1, yzq, rq1, q2, cap_sum), 0,
        [pltpu.VMEM(row_shape, F32)],
    )
    return sol.reshape(rows_rhs.shape), cap_sol, res.reshape(rows_rhs.shape), cap_res


def solution(mesh):
    placed = (
        P("comm", GROUP, None, None, None),
        P("comm", GROUP, None, None),
        P("comm", GROUP, None),
        P("comm", GROUP),
        P("comm", GROUP, None),
        P("comm", GROUP, None),
        P(GROUP, None),
        P("comm", GROUP, None, None),
        P(GROUP, None, None),
    )
    return jax.shard_map(
        body,
        mesh=mesh,
        in_specs=placed,
        out_specs=(
            P("comm", GROUP, None),
            P(GROUP, None),
            P("comm", GROUP, None),
            P(GROUP, None),
        ),
        check_vma=False,
    )
```

```python
import functools

import jax
import jax.numpy as jnp
from jax import lax
from jax.experimental import pallas as pl
from jax.experimental.pallas import tpu as pltpu
from jax.sharding import PartitionSpec as P

GROUP = ("stn", "tm")
F32 = jnp.float32
SLOT = 4
NOTE = 8
VMEM = pl.BlockSpec(memory_space=pltpu.VMEM)
SMEM = pl.BlockSpec(memory_space=pltpu.SMEM)
HBM = pl.BlockSpec(memory_space=pltpu.HBM)
ANY = pl.BlockSpec(memory_space=pl.ANY)
PARTS = 4


def call(kernel, outs, args, scalars=0, scratch=(), aliases=None, flops=0, hbm=(), still=()):
    outs = [jax.ShapeDtypeStruct(o, F32) for o in outs]
    args = [
        pltpu.with_memory_space_constraint(x, pltpu.HBM) if n in hbm else x for n, x in enumerate(args)
    ]
    specs = [SMEM] * scalars + [VMEM] * (len(args) - scalars)
    return pl.pallas_call(
        kernel,
        out_shape=outs,
        in_specs=[
            HBM if n in hbm else ANY if (aliases or {}).get(n) in still else spec for n, spec in enumerate(specs)
        ],
        out_specs=[ANY if n in still else VMEM for n in range(len(outs))],
        scratch_shapes=list(scratch),
        input_output_aliases=aliases or {},
        compiler_params=pltpu.CompilerParams(vmem_limit_bytes=32 * 1024 * 1024),
        cost_estimate=pl.CostEstimate(flops=flops, bytes_accessed=4 * 1024 * 1024, transcendentals=0),
    )(*args)


def fetch(source, target, sems, first, parts):
    step = target.shape[0] // parts
    copies = []
    for n in range(parts):
        part = pl.ds(n * step, step)
        copies.append(pltpu.make_async_copy(source.at[part], target.at[part], sems.at[first + n]))
        copies[-1].start()
    return copies


def kept(x):
    return pltpu.with_memory_space_constraint(x, pltpu.VMEM)


def down(block, column):
    return jnp.sum(block * jnp.broadcast_to(column, block.shape), axis=0, keepdims=True)


def fold(x):
    return jnp.sum(x, axis=0, keepdims=True)


def precondition(blocks_ref, x, out_ref, copies=()):
    xt = x.T
    for i in range(x.shape[0]):
        if copies and i % (x.shape[0] // len(copies)) == 0:
            copies[i // (x.shape[0] // len(copies))].wait()
        out_ref[i : i + 1] = down(blocks_ref[i], xt[:, i : i + 1])


def first_kernel(rhs_hbm, precond_hbm, v_ref, send_ref, rhs_ref, precond_ref, sems):
    (small,) = fetch(rhs_hbm, rhs_ref, sems, PARTS, 1)
    copies = fetch(precond_hbm, precond_ref, sems, 0, PARTS)
    small.wait()
    precondition(precond_ref, rhs_ref[...], v_ref, copies)
    send_ref[...] = jnp.broadcast_to(v_ref[...][None], send_ref.shape)


def widen(x, wide_ref):
    xt = x.T
    for i in range(x.shape[0]):
        wide_ref[i] = jnp.broadcast_to(xt[:, i : i + 1], wide_ref.shape[1:])


def own_rows(i, blocks, arcs, index_ref, tiles_ref, wide_ref):
    c, j = lax.div(i, arcs), lax.rem(i, arcs)
    total = tiles_ref[i, 0] * wide_ref[c * blocks + lax.rem(index_ref[0, c, j], blocks)]
    return total + tiles_ref[i, 1] * wide_ref[c * blocks + lax.rem(index_ref[1, c, j], blocks)]


def near_kernel(comms, index_ref, v_ref, tiles_hbm, up_ref, tiles_ref, wide_ref, sems):
    count = up_ref.shape[0]
    arcs = count // comms
    blocks = v_ref.shape[0] // comms
    own = fetch(tiles_hbm.at[:, pl.ds(0, 2)], tiles_ref, sems, 0, PARTS)
    widen(v_ref[...], wide_ref)
    step = count // PARTS
    for n in range(PARTS):
        own[n].wait()

        def one(i, _):
            up_ref[pl.ds(i, 1)] = fold(own_rows(i, blocks, arcs, index_ref, tiles_ref, wide_ref))
            return 0

        lax.fori_loop(n * step, (n + 1) * step, one, 0, unroll=4)


def cap_first_kernel(cap_rhs_ref, cap_precond_ref, q_ref):
    precondition(cap_precond_ref, cap_rhs_ref[...], q_ref)


def cap_second_kernel(
    cap_rhs_ref, q0_ref, half_ref, other_ref, cap_precond_ref, yq_ref, q_ref, sums_ref
):
    caps = q0_ref.shape[0]
    note = half_ref[...] + other_ref[...]
    q0 = q0_ref[...]
    yq_ref[...] = q0 + note[:caps]
    sums_ref[...] = note[caps:]
    sums_ref[0:1] += fold(cap_rhs_ref[...] * q0)
    sums_ref[1:2] += fold(q0 * q0)
    precondition(cap_precond_ref, yq_ref[...], q_ref)


def cap_third_kernel(
    alpha_ref, cap_rhs_ref, q0_ref, yq0_ref, q1_ref, half_ref, other_ref, cap_precond_ref,
    zq_ref, yzq_ref, rq_ref, q_ref, sums_ref,
):
    caps = q0_ref.shape[0]
    alpha = alpha_ref[0:1]
    yq0, q1 = yq0_ref[...], q1_ref[...]
    yq1 = q1 + half_ref[:caps] + other_ref[:caps]
    zq = q0_ref[...] - alpha * q1
    yzq = yq0 - alpha * yq1
    rq = cap_rhs_ref[...] - alpha * yq0
    zq_ref[...] = zq
    yzq_ref[...] = yzq
    rq_ref[...] = rq
    precondition(cap_precond_ref, alpha * yzq, q_ref)
    q = q_ref[...]
    pairs = ((zq, yq0), (zq, yzq), (q, yq0), (q, yzq), (q, q), (zq, rq), (q, rq))
    for n, (one, other) in enumerate(pairs):
        sums_ref[n : n + 1] = fold(one * other)
    sums_ref[7:8] = jnp.zeros_like(sums_ref[7:8])


def beside(block, row, lane, n, total):
    return jnp.where(lane == n, jnp.sum(block * row, axis=1, keepdims=True), total)


def arcs_up(comms, blocks, index_ref, cap_index_ref, up_ref, got_ref, q_ref, scale_ref, tiles_hbm, cap_tiles_hbm,
            scaled_ref, note_ref, far_ref, third_ref, cap_tiles_ref, wide_ref, turn_ref, sems):
    count = up_ref.shape[0]
    arcs = count // comms
    width = scale_ref.shape[1]
    thirds = fetch(tiles_hbm.at[:, 2], third_ref, sems, 0, PARTS)
    caps_in = fetch(cap_tiles_hbm, cap_tiles_ref, sems, PARTS, PARTS)

    def place(i, _):
        c, j = lax.div(i, arcs), lax.rem(i, arcs)
        far = index_ref[2, c, j]
        row = c if got_ref.shape[1] == comms else c * blocks + lax.rem(far, blocks)
        far_ref[pl.ds(i, 1)] = got_ref[lax.div(far, blocks), pl.ds(row, 1)]
        return 0

    lax.fori_loop(0, count, place, 0, unroll=4)
    widen(q_ref[...], wide_ref)
    ft = far_ref[...].T
    step = count // PARTS
    for i in range(count):
        if i % step == 0:
            thirds[i // step].wait()
            caps_in[i // step].wait()
        column = jnp.broadcast_to(ft[:, i : i + 1], third_ref.shape[1:])
        total = third_ref[i] * column + cap_tiles_ref[i] * wide_ref[cap_index_ref[i // arcs, i % arcs]]
        far_ref[i : i + 1] = up_ref[i : i + 1] + fold(total)
    upward = far_ref[...]
    scaled = scale_ref[...] * upward
    scaled_ref[...] = scaled
    lane = lax.broadcasted_iota(jnp.int32, (width, width), 1)

    def one(i, total):
        return beside(cap_tiles_ref[i], scaled_ref[pl.ds(i, 1)], lane, i, total)

    turn_ref[...] = lax.fori_loop(0, count, one, jnp.zeros((width, width), F32), unroll=2).T
    note_ref[...] = jnp.zeros_like(note_ref)

    def put(i, _):
        cap = cap_index_ref[lax.div(i, arcs), lax.rem(i, arcs)]
        note_ref[pl.ds(cap, 1)] += turn_ref[pl.ds(i, 1)]
        return 0

    lax.fori_loop(0, count, put, 0, unroll=4)
    return fold(upward * scaled)


def up_first_kernel(comms, blocks, caps, index_ref, cap_index_ref, up_ref, got_ref, q_ref, scale_ref, rhs_ref, v_ref,
                    tiles_hbm, cap_tiles_hbm, scaled_ref, note_ref, *room):
    energy = arcs_up(comms, blocks, index_ref, cap_index_ref, up_ref, got_ref, q_ref, scale_ref, tiles_hbm,
                     cap_tiles_hbm, scaled_ref, note_ref, *room)
    v = v_ref[...]
    note_ref[caps : caps + 1] = fold(rhs_ref[...] * v)
    note_ref[caps + 1 : caps + 2] = fold(v * v) + energy


def up_second_kernel(comms, blocks, index_ref, cap_index_ref, up_ref, got_ref, q_ref, scale_ref, tiles_hbm,
                     cap_tiles_hbm, scaled_ref, note_ref, *room):
    arcs_up(comms, blocks, index_ref, cap_index_ref, up_ref, got_ref, q_ref, scale_ref, tiles_hbm,
            cap_tiles_hbm, scaled_ref, note_ref, *room)


def up_third_kernel(comms, blocks, caps, index_ref, cap_index_ref, up_ref, got_ref, q_ref, scale_ref, z_ref, yz_ref,
                    r_ref, y0_ref, v_ref, tiles_hbm, cap_tiles_hbm, scaled_ref, notes_ref, note_ref, *room):
    energy = arcs_up(comms, blocks, index_ref, cap_index_ref, up_ref, got_ref, q_ref, scale_ref, tiles_hbm,
                     cap_tiles_hbm, scaled_ref, note_ref, *room)
    z, yz, r, y0, v = z_ref[...], yz_ref[...], r_ref[...], y0_ref[...], v_ref[...]
    pairs = ((z, y0), (z, yz), (v, y0), (v, yz), (v, v), (z, r), (v, r))
    for n, (one, other) in enumerate(pairs):
        note_ref[caps + n : caps + n + 1] = fold(one * other)
    note_ref[caps + 4 : caps + 5] += energy
    notes_ref[...] = jnp.broadcast_to(note_ref[...][None], notes_ref.shape)


def down_kernel(comms, blocks, step_number, index_ref, scaled_ref, sums_ref, tiles_hbm, local_ref, back_ref,
                tiles_ref, turn_ref, sems):
    count, touched = tiles_ref.shape[:2]
    width = tiles_ref.shape[3]
    arcs = count // comms
    parts = 2 * PARTS
    step = count // parts
    copies = fetch(tiles_hbm, tiles_ref, sems, 0, parts)
    local_ref[...] = jnp.zeros_like(local_ref)
    if step_number == 0:
        back_ref[...] = jnp.full(back_ref.shape, -1.0, F32)
    lane = lax.broadcasted_iota(jnp.int32, (width, width), 1)
    total = jnp.zeros((width, width), F32)
    for n in range(parts):
        copies[n].wait()

        def one(i, total):
            row = scaled_ref[pl.ds(i, 1)]
            for k in range(touched):
                total = beside(tiles_ref[i, k], row, lane, k * count + i, total)
            return total

        total = lax.fori_loop(n * step, (n + 1) * step, one, total)
    turn_ref[...] = total.T

    def put(i, _):
        c, j = lax.div(i, arcs), lax.rem(i, arcs)
        for k in range(2):
            b = c * blocks + lax.rem(index_ref[k, c, j], blocks)
            local_ref[pl.ds(b, 1)] += turn_ref[pl.ds(k * count + i, 1)]
        far = index_ref[2, c, j]
        to = lax.div(far, blocks)
        back_ref[to, pl.ds(c, 1)] = turn_ref[pl.ds(2 * count + i, 1)]
        if step_number == 0:
            local = lax.rem(far, blocks).astype(F32)
            back_ref[to, pl.ds(comms + c, 1)] = jnp.full((1, width), local, F32)
        return 0

    lax.fori_loop(0, count, put, 0, unroll=4)
    if step_number == 1:
        shape = (back_ref.shape[0], 2, width)
        back_ref[:, comms : comms + 2] = jnp.broadcast_to(sums_ref[0:2][None], shape)


def add_kernel(note_ref, other_ref, back_ref, out_ref, same_ref):
    del back_ref, same_ref
    out_ref[...] = note_ref[...] + other_ref[...]


def insert_kernel(comms, caps, notes_ref, sums_ref, back_ref, cap_ref, out_ref):
    del back_ref
    total = jnp.sum(notes_ref[...], axis=0)
    cap_ref[...] = total[:caps]
    sums = jnp.sum(total[caps:] + sums_ref[...], axis=1, keepdims=True)
    width = out_ref.shape[2]
    pick = lax.broadcasted_iota(jnp.int32, (NOTE, width), 0) == lax.broadcasted_iota(
        jnp.int32, (NOTE, width), 1
    )
    row = fold(jnp.where(pick, jnp.broadcast_to(sums, (NOTE, width)), 0.0))
    out_ref[:, comms : comms + 1] = jnp.broadcast_to(row[None], (out_ref.shape[0], 1, width))


def collect(comms, v_ref, local_ref, back_ref, asked, y_ref):
    blocks = v_ref.shape[0] // comms
    for c in range(comms):
        part = back_ref[:, c]
        for b in range(blocks):
            n = c * blocks + b
            came = fold(jnp.where(asked[c] == b, part, 0.0))
            y_ref[n : n + 1] = v_ref[n : n + 1] + local_ref[n : n + 1] + came


def pack(comms, v_ref, asked, send_ref):
    blocks = v_ref.shape[0] // comms
    for c in range(comms):
        row = jnp.zeros_like(asked[c])
        for b in range(blocks):
            n = c * blocks + b
            row = jnp.where(asked[c] == b, v_ref[n : n + 1], row)
        send_ref[:, c] = row


def rows_second_kernel(comms, v0_ref, local_ref, back_ref, note_ref, came_ref, precond_ref, half_ref, y_ref,
                       v_ref, send_ref, asked_ref):
    half_ref[...] = note_ref[...] + came_ref[...]
    asked = [back_ref[:, comms + c] for c in range(comms)]
    for c in range(comms):
        asked_ref[c] = asked[c]
    collect(comms, v0_ref, local_ref, back_ref, asked, y_ref)
    precondition(precond_ref, y_ref[...], v_ref)
    pack(comms, v_ref, asked, send_ref)


def rows_third_kernel(comms, rhs_ref, v0_ref, y0_ref, v1_ref, local_ref, back_ref, note_ref, came_ref, asked_ref,
                      precond_ref, half_ref, alpha_ref, z_ref, yz_ref, r_ref, v_ref, send_ref):
    half_ref[...] = note_ref[...] + came_ref[...]
    asked = [asked_ref[c] for c in range(comms)]
    collect(comms, v1_ref, local_ref, back_ref, asked, yz_ref)
    first = jnp.sum(fold(back_ref[:, comms]), axis=1, keepdims=True)
    second = jnp.sum(fold(back_ref[:, comms + 1]), axis=1, keepdims=True)
    alpha = jnp.broadcast_to(first / second, (1, alpha_ref.shape[1]))
    alpha_ref[...] = jnp.broadcast_to(alpha, alpha_ref.shape)
    alpha_ref[1:2] = jnp.broadcast_to(second, (1, alpha_ref.shape[1]))
    y0 = y0_ref[...]
    z_ref[...] = v0_ref[...] - alpha * v1_ref[...]
    yz = y0 - alpha * yz_ref[...]
    yz_ref[...] = yz
    r_ref[...] = rhs_ref[...] - alpha * y0
    precondition(precond_ref, alpha * yz, v_ref)
    pack(comms, v_ref, asked, send_ref)


def last_kernel(comms, alpha_ref, v0_ref, y0_ref, z_ref, yz_ref, r_ref, v2_ref, local_ref, back_ref,
                asked_ref, q0_ref, yq0_ref, zq_ref, yzq_ref, rq_ref, q2_ref, cap_ref,
                sol_ref, cap_sol_ref, res_ref, cap_res_ref, y_ref):
    asked = [asked_ref[c] for c in range(comms)]
    collect(comms, v2_ref, local_ref, back_ref, asked, y_ref)
    row = fold(back_ref[:, comms])
    width = row.shape[1]
    lane = lax.broadcasted_iota(jnp.int32, row.shape, 1)
    s = [
        jnp.broadcast_to(
            jnp.sum(jnp.where(lane == n, row, 0.0), axis=1, keepdims=True), (1, width)
        )
        for n in range(7)
    ]
    alpha, h00 = alpha_ref[0:1], alpha_ref[1:2]
    h1, h2 = s[0] / h00, s[2] / h00
    a11 = s[1] - h1 * s[0]
    a12 = s[3] - h1 * s[2]
    a22 = s[4] - h2 * s[2]
    lower = a12 / a11
    c2 = (s[6] - lower * s[5]) / (a22 - lower * a12)
    c1 = s[5] / a11 - lower * c2
    c0 = c1 * h1 + c2 * h2
    sol_ref[...] = (alpha - c0) * v0_ref[...] + c1 * z_ref[...] + c2 * v2_ref[...]
    cap_sol_ref[...] = (alpha - c0) * q0_ref[...] + c1 * zq_ref[...] + c2 * q2_ref[...]
    res_ref[...] = r_ref[...] + c0 * y0_ref[...] - c1 * yz_ref[...] - c2 * y_ref[...]
    yq2 = q2_ref[...] + cap_ref[...]
    cap_res_ref[...] = rq_ref[...] + c0 * yq0_ref[...] - c1 * yzq_ref[...] - c2 * yq2


def body(
    tiles, cap_tiles, row_index, cap_index, arc_scale, rows_rhs, cap_rhs, precond, cap_precond
):
    comms, arcs, touched = row_index.shape
    blocks, width = rows_rhs.shape[1:]
    caps = cap_rhs.shape[0]
    groups = lax.axis_size("stn") * lax.axis_size("tm")
    peers = lax.axis_size("comm")
    rows, count = comms * blocks, comms * arcs
    flat = (width, width)
    tiles = tiles.reshape(count, touched, *flat)
    cap_tiles = cap_tiles.reshape(count, *flat)
    precond = precond.reshape(rows, *flat)
    index = jnp.transpose(row_index, (2, 0, 1))
    scale = arc_scale.reshape(count, width)
    rhs = rows_rhs.reshape(rows, width)
    row_shape, cap_shape, arc_shape = (rows, width), (caps, width), (count, width)
    small = (NOTE, width)
    note_shape = (caps + NOTE, width)
    send_shape = (groups, comms, width)
    back_shape = (groups, SLOT, width)
    unit = 2 * count * width * width

    def room(*shape):
        return pltpu.VMEM(shape, F32)

    def sems(n):
        return pltpu.SemaphoreType.DMA((n,))

    def exchange(x):
        return lax.all_to_all(x, GROUP, 0, 0)

    def across(x, step):
        return lax.ppermute(x, "comm", [(i, i ^ step) for i in range(peers)])

    def near(v):
        (up,) = call(
            functools.partial(near_kernel, comms), [arc_shape], (index, v, tiles), 1,
            [room(count, 2, *flat), room(rows, *flat), sems(PARTS)], flops=2 * unit, hbm=(2,),
        )
        return up

    up_room = [
        room(*arc_shape), room(count, *flat), room(count, *flat), room(caps, *flat), room(*flat), sems(2 * PARTS),
    ]

    def spread(step_number, scaled, sums):
        return call(
            functools.partial(down_kernel, comms, blocks, step_number), [row_shape, back_shape],
            (index, scaled, sums, tiles), 1,
            [room(count, touched, *flat), room(*flat), sems(2 * PARTS)], flops=3 * unit, hbm=(3,),
        )

    def add(note, other, back):
        return call(add_kernel, [note_shape, back_shape], (note, other, back), aliases={2: 1}, still=(1,))

    v0, send = call(
        first_kernel, [row_shape, (groups, rows, width)], (rhs, precond), 0,
        [room(*row_shape), room(rows, *flat), sems(PARTS + 1)], hbm=(0, 1),
    )
    got = exchange(send)
    up = near(v0)
    (q0,) = call(cap_first_kernel, [cap_shape], (cap_rhs, kept(cap_precond)), flops=unit)
    scaled, note = call(
        functools.partial(up_first_kernel, comms, blocks, caps), [arc_shape, note_shape],
        (index, cap_index, up, got, q0, scale, rhs, v0, tiles, cap_tiles), 2, up_room, flops=3 * unit, hbm=(8, 9),
    )
    other = across(note, 4)
    local, back = spread(0, scaled, rhs)
    note, back = add(note, other, back)
    back = exchange(back)
    half, y0, v1, send, asked = call(
        functools.partial(rows_second_kernel, comms),
        [note_shape, row_shape, row_shape, send_shape, (comms, groups, width)],
        (v0, local, back, note, across(note, 1), kept(precond)),
    )
    got = exchange(send)
    other = across(half, 2)
    up = near(v1)
    yq0, q1, sums = call(
        cap_second_kernel, [cap_shape, cap_shape, small], (cap_rhs, q0, half, other, kept(cap_precond)), flops=unit,
    )
    scaled, note = call(
        functools.partial(up_second_kernel, comms, blocks), [arc_shape, note_shape],
        (index, cap_index, up, got, q1, scale, tiles, cap_tiles), 2, up_room, flops=3 * unit, hbm=(6, 7),
    )
    other = across(note, 4)
    local, back = spread(1, scaled, sums)
    note, back = add(note, other, back)
    back = exchange(back)
    half, alpha, z1, yz, r1, v2, send = call(
        functools.partial(rows_third_kernel, comms),
        [note_shape, small, row_shape, row_shape, row_shape, row_shape, send_shape],
        (rhs, v0, y0, v1, local, back, note, across(note, 1), asked, kept(precond)),
    )
    got = exchange(send)
    other = across(half, 2)
    up = near(v2)
    zq1, yzq, rq1, q2, sums = call(
        cap_third_kernel, [cap_shape] * 4 + [small],
        (alpha, cap_rhs, q0, yq0, q1, half, other, kept(cap_precond)), flops=unit,
    )
    scaled, notes = call(
        functools.partial(up_third_kernel, comms, blocks, caps), [arc_shape, (peers, *note_shape)],
        (index, cap_index, up, got, q2, scale, z1, yz, r1, y0, v2, tiles, cap_tiles), 2,
        [room(*note_shape), *up_room], flops=3 * unit, hbm=(11, 12),
    )
    notes = lax.all_to_all(notes, "comm", 0, 0)
    local, back = spread(2, scaled, sums)
    cap_sum, back = call(
        functools.partial(insert_kernel, comms, caps), [cap_shape, back_shape], (notes, sums, back),
        aliases={2: 1},
    )
    back = exchange(back)
    sol, cap_sol, res, cap_res = call(
        functools.partial(last_kernel, comms), [row_shape, cap_shape, row_shape, cap_shape],
        (alpha, v0, y0, z1, yz, r1, v2, local, back, asked, q0, yq0, zq1, yzq, rq1, q2, cap_sum), 0,
        [pltpu.VMEM(row_shape, F32)],
    )
    return sol.reshape(rows_rhs.shape), cap_sol, res.reshape(rows_rhs.shape), cap_res


def solution(mesh):
    placed = (
        P("comm", GROUP, None, None, None),
        P("comm", GROUP, None, None),
        P("comm", GROUP, None),
        P("comm", GROUP),
        P("comm", GROUP, None),
        P("comm", GROUP, None),
        P(GROUP, None),
        P("comm", GROUP, None, None),
        P(GROUP, None, None),
    )
    return jax.shard_map(
        body,
        mesh=mesh,
        in_specs=placed,
        out_specs=(
            P("comm", GROUP, None),
            P(GROUP, None),
            P("comm", GROUP, None),
            P(GROUP, None),
        ),
        check_vma=False,
    )
```

```python
import functools

import jax
import jax.numpy as jnp
from jax import lax
from jax.experimental import pallas as pl
from jax.experimental.pallas import tpu as pltpu
from jax.sharding import PartitionSpec as P

GROUP = ("stn", "tm")
F32 = jnp.float32
SLOT = 4
NOTE = 8
VMEM = pl.BlockSpec(memory_space=pltpu.VMEM)
SMEM = pl.BlockSpec(memory_space=pltpu.SMEM)
HBM = pl.BlockSpec(memory_space=pltpu.HBM)
ANY = pl.BlockSpec(memory_space=pl.ANY)
PARTS = 4


def call(kernel, outs, args, scalars=0, scratch=(), aliases=None, flops=0, hbm=(), still=()):
    outs = [jax.ShapeDtypeStruct(o, F32) for o in outs]
    args = [
        pltpu.with_memory_space_constraint(x, pltpu.HBM) if n in hbm else x for n, x in enumerate(args)
    ]
    specs = [SMEM] * scalars + [VMEM] * (len(args) - scalars)
    return pl.pallas_call(
        kernel,
        out_shape=outs,
        in_specs=[
            HBM if n in hbm else ANY if (aliases or {}).get(n) in still else spec for n, spec in enumerate(specs)
        ],
        out_specs=[ANY if n in still else VMEM for n in range(len(outs))],
        scratch_shapes=list(scratch),
        input_output_aliases=aliases or {},
        compiler_params=pltpu.CompilerParams(vmem_limit_bytes=12 * 1024 * 1024),
        cost_estimate=pl.CostEstimate(flops=flops, bytes_accessed=4 * 1024 * 1024, transcendentals=0),
    )(*args)


def fetch(source, target, sems, first, parts):
    step = target.shape[0] // parts
    copies = []
    for n in range(parts):
        part = pl.ds(n * step, step)
        copies.append(pltpu.make_async_copy(source.at[part], target.at[part], sems.at[first + n]))
        copies[-1].start()
    return copies


def kept(x):
    return pltpu.with_memory_space_constraint(x, pltpu.VMEM)


def down(block, column):
    return jnp.sum(block * jnp.broadcast_to(column, block.shape), axis=0, keepdims=True)


def fold(x):
    return jnp.sum(x, axis=0, keepdims=True)


def precondition(blocks_ref, x, out_ref, copies=()):
    xt = x.T
    for i in range(x.shape[0]):
        if copies and i % (x.shape[0] // len(copies)) == 0:
            copies[i // (x.shape[0] // len(copies))].wait()
        out_ref[i : i + 1] = down(blocks_ref[i], xt[:, i : i + 1])


def first_kernel(rhs_hbm, precond_hbm, v_ref, send_ref, rhs_ref, precond_ref, sems):
    (small,) = fetch(rhs_hbm, rhs_ref, sems, PARTS, 1)
    copies = fetch(precond_hbm, precond_ref, sems, 0, PARTS)
    small.wait()
    precondition(precond_ref, rhs_ref[...], v_ref, copies)
    send_ref[...] = jnp.broadcast_to(v_ref[...][None], send_ref.shape)


def widen(x, wide_ref):
    xt = x.T
    for i in range(x.shape[0]):
        wide_ref[i] = jnp.broadcast_to(xt[:, i : i + 1], wide_ref.shape[1:])


def own_rows(i, blocks, arcs, index_ref, tiles_ref, wide_ref):
    c, j = lax.div(i, arcs), lax.rem(i, arcs)
    total = tiles_ref[i, 0] * wide_ref[c * blocks + lax.rem(index_ref[0, c, j], blocks)]
    return total + tiles_ref[i, 1] * wide_ref[c * blocks + lax.rem(index_ref[1, c, j], blocks)]


def near_kernel(comms, index_ref, v_ref, tiles_hbm, up_ref, tiles_ref, wide_ref, sems):
    count = up_ref.shape[0]
    arcs = count // comms
    blocks = v_ref.shape[0] // comms
    own = fetch(tiles_hbm.at[:, pl.ds(0, 2)], tiles_ref, sems, 0, PARTS)
    widen(v_ref[...], wide_ref)
    step = count // PARTS
    for n in range(PARTS):
        own[n].wait()

        def one(i, _):
            up_ref[pl.ds(i, 1)] = fold(own_rows(i, blocks, arcs, index_ref, tiles_ref, wide_ref))
            return 0

        lax.fori_loop(n * step, (n + 1) * step, one, 0, unroll=4)


def cap_first_kernel(cap_rhs_ref, cap_precond_ref, q_ref):
    precondition(cap_precond_ref, cap_rhs_ref[...], q_ref)


def cap_second_kernel(
    cap_rhs_ref, q0_ref, half_ref, other_ref, cap_precond_ref, yq_ref, q_ref, sums_ref
):
    caps = q0_ref.shape[0]
    note = half_ref[...] + other_ref[...]
    q0 = q0_ref[...]
    yq_ref[...] = q0 + note[:caps]
    sums_ref[...] = note[caps:]
    sums_ref[0:1] += fold(cap_rhs_ref[...] * q0)
    sums_ref[1:2] += fold(q0 * q0)
    precondition(cap_precond_ref, yq_ref[...], q_ref)


def cap_third_kernel(
    alpha_ref, cap_rhs_ref, q0_ref, yq0_ref, q1_ref, half_ref, other_ref, cap_precond_ref,
    zq_ref, yzq_ref, rq_ref, q_ref, sums_ref,
):
    caps = q0_ref.shape[0]
    alpha = alpha_ref[0:1]
    yq0, q1 = yq0_ref[...], q1_ref[...]
    yq1 = q1 + half_ref[:caps] + other_ref[:caps]
    zq = q0_ref[...] - alpha * q1
    yzq = yq0 - alpha * yq1
    rq = cap_rhs_ref[...] - alpha * yq0
    zq_ref[...] = zq
    yzq_ref[...] = yzq
    rq_ref[...] = rq
    precondition(cap_precond_ref, alpha * yzq, q_ref)
    q = q_ref[...]
    pairs = ((zq, yq0), (zq, yzq), (q, yq0), (q, yzq), (q, q), (zq, rq), (q, rq))
    for n, (one, other) in enumerate(pairs):
        sums_ref[n : n + 1] = fold(one * other)
    sums_ref[7:8] = jnp.zeros_like(sums_ref[7:8])


def beside(block, row, lane, n, total):
    return jnp.where(lane == n, jnp.sum(block * row, axis=1, keepdims=True), total)


def arcs_up(comms, blocks, index_ref, cap_index_ref, up_ref, got_ref, q_ref, scale_ref, tiles_hbm, cap_tiles_ref,
            scaled_ref, note_ref, far_ref, third_ref, wide_ref, turn_ref, sems, caps_in=None):
    count = up_ref.shape[0]
    arcs = count // comms
    width = scale_ref.shape[1]
    thirds = fetch(tiles_hbm.at[:, 2], third_ref, sems, 0, PARTS)

    def place(i, _):
        c, j = lax.div(i, arcs), lax.rem(i, arcs)
        far = index_ref[2, c, j]
        row = c if got_ref.shape[1] == comms else c * blocks + lax.rem(far, blocks)
        far_ref[pl.ds(i, 1)] = got_ref[lax.div(far, blocks), pl.ds(row, 1)]
        return 0

    lax.fori_loop(0, count, place, 0, unroll=4)
    widen(q_ref[...], wide_ref)
    ft = far_ref[...].T
    step = count // PARTS
    for i in range(count):
        if i % step == 0:
            thirds[i // step].wait()
            if caps_in:
                caps_in[i // step].wait()
        column = jnp.broadcast_to(ft[:, i : i + 1], third_ref.shape[1:])
        total = third_ref[i] * column + cap_tiles_ref[i] * wide_ref[cap_index_ref[i // arcs, i % arcs]]
        far_ref[i : i + 1] = up_ref[i : i + 1] + fold(total)
    upward = far_ref[...]
    scaled = scale_ref[...] * upward
    scaled_ref[...] = scaled
    lane = lax.broadcasted_iota(jnp.int32, (width, width), 1)

    total = jnp.zeros((width, width), F32)
    for i in range(count):
        total = beside(cap_tiles_ref[i], scaled[i : i + 1], lane, i, total)
    turn_ref[...] = total.T
    note_ref[...] = jnp.zeros_like(note_ref)

    def put(i, _):
        cap = cap_index_ref[lax.div(i, arcs), lax.rem(i, arcs)]
        note_ref[pl.ds(cap, 1)] += turn_ref[pl.ds(i, 1)]
        return 0

    lax.fori_loop(0, count, put, 0, unroll=4)
    return fold(upward * scaled)


def up_first_kernel(comms, blocks, caps, index_ref, cap_index_ref, up_ref, got_ref, q_ref, scale_ref, rhs_ref, v_ref,
                    tiles_hbm, cap_tiles_hbm, scaled_ref, note_ref, cap_tiles_ref, *room):
    caps_in = fetch(cap_tiles_hbm, cap_tiles_ref, room[-1], PARTS, PARTS)
    energy = arcs_up(comms, blocks, index_ref, cap_index_ref, up_ref, got_ref, q_ref, scale_ref, tiles_hbm,
                     cap_tiles_ref, scaled_ref, note_ref, *room, caps_in)
    v = v_ref[...]
    note_ref[caps : caps + 1] = fold(rhs_ref[...] * v)
    note_ref[caps + 1 : caps + 2] = fold(v * v) + energy


def up_second_kernel(comms, blocks, index_ref, cap_index_ref, up_ref, got_ref, q_ref, scale_ref, tiles_hbm,
                     cap_tiles_hbm, scaled_ref, note_ref, cap_tiles_ref, *room):
    caps_in = fetch(cap_tiles_hbm, cap_tiles_ref, room[-1], PARTS, PARTS)
    arcs_up(comms, blocks, index_ref, cap_index_ref, up_ref, got_ref, q_ref, scale_ref, tiles_hbm,
            cap_tiles_ref, scaled_ref, note_ref, *room, caps_in)


def up_third_kernel(comms, blocks, caps, index_ref, cap_index_ref, up_ref, got_ref, q_ref, scale_ref, z_ref, yz_ref,
                    r_ref, y0_ref, v_ref, tiles_hbm, cap_tiles_ref, scaled_ref, notes_ref, note_ref, *room):
    energy = arcs_up(comms, blocks, index_ref, cap_index_ref, up_ref, got_ref, q_ref, scale_ref, tiles_hbm,
                     cap_tiles_ref, scaled_ref, note_ref, *room)
    z, yz, r, y0, v = z_ref[...], yz_ref[...], r_ref[...], y0_ref[...], v_ref[...]
    pairs = ((z, y0), (z, yz), (v, y0), (v, yz), (v, v), (z, r), (v, r))
    for n, (one, other) in enumerate(pairs):
        note_ref[caps + n : caps + n + 1] = fold(one * other)
    note_ref[caps + 4 : caps + 5] += energy
    notes_ref[...] = jnp.broadcast_to(note_ref[...][None], notes_ref.shape)


def down_kernel(comms, blocks, step_number, index_ref, scaled_ref, sums_ref, tiles_ref, local_ref, back_ref, turn_ref):
    count, touched = tiles_ref.shape[:2]
    width = tiles_ref.shape[3]
    arcs = count // comms
    local_ref[...] = jnp.zeros_like(local_ref)
    if step_number == 0:
        back_ref[...] = jnp.full(back_ref.shape, -1.0, F32)
    lane = lax.broadcasted_iota(jnp.int32, (width, width), 1)
    total = jnp.zeros((width, width), F32)
    for i in range(count):
        row = scaled_ref[i : i + 1]
        for k in range(touched):
            total = beside(tiles_ref[i, k], row, lane, k * count + i, total)
    turn_ref[...] = total.T

    def put(i, _):
        c, j = lax.div(i, arcs), lax.rem(i, arcs)
        for k in range(2):
            b = c * blocks + lax.rem(index_ref[k, c, j], blocks)
            local_ref[pl.ds(b, 1)] += turn_ref[pl.ds(k * count + i, 1)]
        far = index_ref[2, c, j]
        to = lax.div(far, blocks)
        back_ref[to, pl.ds(c, 1)] = turn_ref[pl.ds(2 * count + i, 1)]
        if step_number == 0:
            local = lax.rem(far, blocks).astype(F32)
            back_ref[to, pl.ds(comms + c, 1)] = jnp.full((1, width), local, F32)
        return 0

    lax.fori_loop(0, count, put, 0, unroll=4)
    if step_number == 1:
        shape = (back_ref.shape[0], 2, width)
        back_ref[:, comms : comms + 2] = jnp.broadcast_to(sums_ref[0:2][None], shape)


def add_kernel(note_ref, other_ref, back_ref, out_ref, same_ref):
    del back_ref, same_ref
    out_ref[...] = note_ref[...] + other_ref[...]


def insert_kernel(comms, caps, notes_ref, sums_ref, back_ref, cap_ref, out_ref):
    del back_ref
    total = jnp.sum(notes_ref[...], axis=0)
    cap_ref[...] = total[:caps]
    sums = jnp.sum(total[caps:] + sums_ref[...], axis=1, keepdims=True)
    width = out_ref.shape[2]
    pick = lax.broadcasted_iota(jnp.int32, (NOTE, width), 0) == lax.broadcasted_iota(
        jnp.int32, (NOTE, width), 1
    )
    row = fold(jnp.where(pick, jnp.broadcast_to(sums, (NOTE, width)), 0.0))
    out_ref[:, comms : comms + 1] = jnp.broadcast_to(row[None], (out_ref.shape[0], 1, width))


def collect(comms, v_ref, local_ref, back_ref, asked, y_ref):
    blocks = v_ref.shape[0] // comms
    for c in range(comms):
        part = back_ref[:, c]
        for b in range(blocks):
            n = c * blocks + b
            came = fold(jnp.where(asked[c] == b, part, 0.0))
            y_ref[n : n + 1] = v_ref[n : n + 1] + local_ref[n : n + 1] + came


def pack(comms, v_ref, asked, send_ref):
    blocks = v_ref.shape[0] // comms
    for c in range(comms):
        row = jnp.zeros_like(asked[c])
        for b in range(blocks):
            n = c * blocks + b
            row = jnp.where(asked[c] == b, v_ref[n : n + 1], row)
        send_ref[:, c] = row


def rows_second_kernel(comms, v0_ref, local_ref, back_ref, note_ref, came_ref, precond_ref, half_ref, y_ref,
                       v_ref, send_ref, asked_ref):
    half_ref[...] = note_ref[...] + came_ref[...]
    asked = [back_ref[:, comms + c] for c in range(comms)]
    for c in range(comms):
        asked_ref[c] = asked[c]
    collect(comms, v0_ref, local_ref, back_ref, asked, y_ref)
    precondition(precond_ref, y_ref[...], v_ref)
    pack(comms, v_ref, asked, send_ref)


def rows_third_kernel(comms, rhs_ref, v0_ref, y0_ref, v1_ref, local_ref, back_ref, note_ref, came_ref, asked_ref,
                      precond_ref, half_ref, alpha_ref, z_ref, yz_ref, r_ref, v_ref, send_ref):
    half_ref[...] = note_ref[...] + came_ref[...]
    asked = [asked_ref[c] for c in range(comms)]
    collect(comms, v1_ref, local_ref, back_ref, asked, yz_ref)
    first = jnp.sum(fold(back_ref[:, comms]), axis=1, keepdims=True)
    second = jnp.sum(fold(back_ref[:, comms + 1]), axis=1, keepdims=True)
    alpha = jnp.broadcast_to(first / second, (1, alpha_ref.shape[1]))
    alpha_ref[...] = jnp.broadcast_to(alpha, alpha_ref.shape)
    alpha_ref[1:2] = jnp.broadcast_to(second, (1, alpha_ref.shape[1]))
    y0 = y0_ref[...]
    z_ref[...] = v0_ref[...] - alpha * v1_ref[...]
    yz = y0 - alpha * yz_ref[...]
    yz_ref[...] = yz
    r_ref[...] = rhs_ref[...] - alpha * y0
    precondition(precond_ref, alpha * yz, v_ref)
    pack(comms, v_ref, asked, send_ref)


def last_kernel(comms, alpha_ref, v0_ref, y0_ref, z_ref, yz_ref, r_ref, v2_ref, local_ref, back_ref,
                asked_ref, q0_ref, yq0_ref, zq_ref, yzq_ref, rq_ref, q2_ref, cap_ref,
                sol_ref, cap_sol_ref, res_ref, cap_res_ref, y_ref):
    asked = [asked_ref[c] for c in range(comms)]
    collect(comms, v2_ref, local_ref, back_ref, asked, y_ref)
    row = fold(back_ref[:, comms])
    width = row.shape[1]
    lane = lax.broadcasted_iota(jnp.int32, row.shape, 1)
    s = [
        jnp.broadcast_to(
            jnp.sum(jnp.where(lane == n, row, 0.0), axis=1, keepdims=True), (1, width)
        )
        for n in range(7)
    ]
    alpha, h00 = alpha_ref[0:1], alpha_ref[1:2]
    h1, h2 = s[0] / h00, s[2] / h00
    a11 = s[1] - h1 * s[0]
    a12 = s[3] - h1 * s[2]
    a22 = s[4] - h2 * s[2]
    lower = a12 / a11
    c2 = (s[6] - lower * s[5]) / (a22 - lower * a12)
    c1 = s[5] / a11 - lower * c2
    c0 = c1 * h1 + c2 * h2
    sol_ref[...] = (alpha - c0) * v0_ref[...] + c1 * z_ref[...] + c2 * v2_ref[...]
    cap_sol_ref[...] = (alpha - c0) * q0_ref[...] + c1 * zq_ref[...] + c2 * q2_ref[...]
    res_ref[...] = r_ref[...] + c0 * y0_ref[...] - c1 * yz_ref[...] - c2 * y_ref[...]
    yq2 = q2_ref[...] + cap_ref[...]
    cap_res_ref[...] = rq_ref[...] + c0 * yq0_ref[...] - c1 * yzq_ref[...] - c2 * yq2


def body(
    tiles, cap_tiles, row_index, cap_index, arc_scale, rows_rhs, cap_rhs, precond, cap_precond
):
    comms, arcs, touched = row_index.shape
    blocks, width = rows_rhs.shape[1:]
    caps = cap_rhs.shape[0]
    groups = lax.axis_size("stn") * lax.axis_size("tm")
    peers = lax.axis_size("comm")
    rows, count = comms * blocks, comms * arcs
    flat = (width, width)
    tiles = tiles.reshape(count, touched, *flat)
    cap_tiles = cap_tiles.reshape(count, *flat)
    precond = precond.reshape(rows, *flat)
    index = jnp.transpose(row_index, (2, 0, 1))
    scale = arc_scale.reshape(count, width)
    rhs = rows_rhs.reshape(rows, width)
    row_shape, cap_shape, arc_shape = (rows, width), (caps, width), (count, width)
    small = (NOTE, width)
    note_shape = (caps + NOTE, width)
    send_shape = (groups, comms, width)
    back_shape = (groups, SLOT, width)
    unit = 2 * count * width * width

    def room(*shape):
        return pltpu.VMEM(shape, F32)

    def sems(n):
        return pltpu.SemaphoreType.DMA((n,))

    def exchange(x):
        return lax.all_to_all(x, GROUP, 0, 0)

    def across(x, step):
        return lax.ppermute(x, "comm", [(i, i ^ step) for i in range(peers)])

    def near(v):
        (up,) = call(
            functools.partial(near_kernel, comms), [arc_shape], (index, v, tiles), 1,
            [room(count, 2, *flat), room(rows, *flat), sems(PARTS)], flops=2 * unit, hbm=(2,),
        )
        return up

    up_room = [
        room(*arc_shape), room(count, *flat), room(caps, *flat), room(*flat), sems(2 * PARTS),
    ]
    both_room = [room(count, *flat), *up_room]

    def spread(step_number, scaled, sums):
        return call(
            functools.partial(down_kernel, comms, blocks, step_number), [row_shape, back_shape],
            (index, scaled, sums, kept(tiles)), 1, [room(*flat)], flops=3 * unit,
        )

    def add(note, other, back):
        return call(add_kernel, [note_shape, back_shape], (note, other, back), aliases={2: 1}, still=(1,))

    v0, send = call(
        first_kernel, [row_shape, (groups, rows, width)], (rhs, precond), 0,
        [room(*row_shape), room(rows, *flat), sems(PARTS + 1)], hbm=(0, 1),
    )
    got = exchange(send)
    up = near(v0)
    (q0,) = call(cap_first_kernel, [cap_shape], (cap_rhs, kept(cap_precond)), flops=unit)
    scaled, note = call(
        functools.partial(up_first_kernel, comms, blocks, caps), [arc_shape, note_shape],
        (index, cap_index, up, got, q0, scale, rhs, v0, tiles, cap_tiles), 2, both_room, flops=3 * unit, hbm=(8, 9),
    )
    other = across(note, 4)
    local, back = spread(0, scaled, rhs)
    note, back = add(note, other, back)
    back = exchange(back)
    half, y0, v1, send, asked = call(
        functools.partial(rows_second_kernel, comms),
        [note_shape, row_shape, row_shape, send_shape, (comms, groups, width)],
        (v0, local, back, note, across(note, 1), kept(precond)),
    )
    got = exchange(send)
    other = across(half, 2)
    up = near(v1)
    yq0, q1, sums = call(
        cap_second_kernel, [cap_shape, cap_shape, small], (cap_rhs, q0, half, other, kept(cap_precond)), flops=unit,
    )
    scaled, note = call(
        functools.partial(up_second_kernel, comms, blocks), [arc_shape, note_shape],
        (index, cap_index, up, got, q1, scale, tiles, cap_tiles), 2, both_room, flops=3 * unit, hbm=(6, 7),
    )
    other = across(note, 4)
    local, back = spread(1, scaled, sums)
    note, back = add(note, other, back)
    back = exchange(back)
    half, alpha, z1, yz, r1, v2, send = call(
        functools.partial(rows_third_kernel, comms),
        [note_shape, small, row_shape, row_shape, row_shape, row_shape, send_shape],
        (rhs, v0, y0, v1, local, back, note, across(note, 1), asked, kept(precond)),
    )
    got = exchange(send)
    other = across(half, 2)
    up = near(v2)
    zq1, yzq, rq1, q2, sums = call(
        cap_third_kernel, [cap_shape] * 4 + [small],
        (alpha, cap_rhs, q0, yq0, q1, half, other, kept(cap_precond)), flops=unit,
    )
    scaled, notes = call(
        functools.partial(up_third_kernel, comms, blocks, caps), [arc_shape, (peers, *note_shape)],
        (index, cap_index, up, got, q2, scale, z1, yz, r1, y0, v2, tiles, kept(cap_tiles)), 2,
        [room(*note_shape), *up_room], flops=3 * unit, hbm=(11,),
    )
    notes = lax.all_to_all(notes, "comm", 0, 0)
    local, back = spread(2, scaled, sums)
    cap_sum, back = call(
        functools.partial(insert_kernel, comms, caps), [cap_shape, back_shape], (notes, sums, back),
        aliases={2: 1},
    )
    back = exchange(back)
    sol, cap_sol, res, cap_res = call(
        functools.partial(last_kernel, comms), [row_shape, cap_shape, row_shape, cap_shape],
        (alpha, v0, y0, z1, yz, r1, v2, local, back, asked, q0, yq0, zq1, yzq, rq1, q2, cap_sum), 0,
        [pltpu.VMEM(row_shape, F32)],
    )
    return sol.reshape(rows_rhs.shape), cap_sol, res.reshape(rows_rhs.shape), cap_res


def solution(mesh):
    placed = (
        P("comm", GROUP, None, None, None),
        P("comm", GROUP, None, None),
        P("comm", GROUP, None),
        P("comm", GROUP),
        P("comm", GROUP, None),
        P("comm", GROUP, None),
        P(GROUP, None),
        P("comm", GROUP, None, None),
        P(GROUP, None, None),
    )
    return jax.shard_map(
        body,
        mesh=mesh,
        in_specs=placed,
        out_specs=(
            P("comm", GROUP, None),
            P(GROUP, None),
            P("comm", GROUP, None),
            P(GROUP, None),
        ),
        check_vma=False,
    )
```

```python
import functools

import jax
import jax.numpy as jnp
from jax import lax
from jax.experimental import pallas as pl
from jax.experimental.pallas import tpu as pltpu
from jax.sharding import PartitionSpec as P

GROUP = ("stn", "tm")
F32 = jnp.float32
SLOT = 4
NOTE = 8
VMEM = pl.BlockSpec(memory_space=pltpu.VMEM)
SMEM = pl.BlockSpec(memory_space=pltpu.SMEM)
HBM = pl.BlockSpec(memory_space=pltpu.HBM)
ANY = pl.BlockSpec(memory_space=pl.ANY)
PARTS = 4


def call(kernel, outs, args, scalars=0, scratch=(), aliases=None, flops=0, hbm=(), still=()):
    outs = [jax.ShapeDtypeStruct(o, F32) if isinstance(o, tuple) else o for o in outs]
    args = [
        pltpu.with_memory_space_constraint(x, pltpu.HBM) if n in hbm else x for n, x in enumerate(args)
    ]
    specs = [SMEM] * scalars + [VMEM] * (len(args) - scalars)
    return pl.pallas_call(
        kernel,
        out_shape=outs,
        in_specs=[
            HBM if n in hbm else ANY if (aliases or {}).get(n) in still else spec for n, spec in enumerate(specs)
        ],
        out_specs=[ANY if n in still else VMEM for n in range(len(outs))],
        scratch_shapes=list(scratch),
        input_output_aliases=aliases or {},
        compiler_params=pltpu.CompilerParams(vmem_limit_bytes=12 * 1024 * 1024),
        cost_estimate=pl.CostEstimate(flops=flops, bytes_accessed=4 * 1024 * 1024, transcendentals=0),
    )(*args)


def fetch(source, target, sems, first, parts):
    step = target.shape[0] // parts
    copies = []
    for n in range(parts):
        part = pl.ds(n * step, step)
        copies.append(pltpu.make_async_copy(source.at[part], target.at[part], sems.at[first + n]))
        copies[-1].start()
    return copies


def kept(x):
    return pltpu.with_memory_space_constraint(x, pltpu.VMEM)


def down(block, column):
    return jnp.sum(block * jnp.broadcast_to(column, block.shape), axis=0, keepdims=True)


def fold(x):
    return jnp.sum(x, axis=0, keepdims=True)


def precondition(blocks_ref, x, out_ref, copies=()):
    xt = x.T
    for i in range(x.shape[0]):
        if copies and i % (x.shape[0] // len(copies)) == 0:
            copies[i // (x.shape[0] // len(copies))].wait()
        out_ref[i : i + 1] = down(blocks_ref[i], xt[:, i : i + 1])


def first_kernel(rhs_hbm, precond_hbm, v_ref, send_ref, rhs_ref, precond_ref, sems):
    (small,) = fetch(rhs_hbm, rhs_ref, sems, PARTS, 1)
    copies = fetch(precond_hbm, precond_ref, sems, 0, PARTS)
    small.wait()
    precondition(precond_ref, rhs_ref[...], v_ref, copies)
    send_ref[...] = jnp.broadcast_to(v_ref[...][None], send_ref.shape)


def widen(x, wide_ref):
    xt = x.T
    for i in range(x.shape[0]):
        wide_ref[i] = jnp.broadcast_to(xt[:, i : i + 1], wide_ref.shape[1:])


def own_rows(i, blocks, arcs, index_ref, tiles_ref, wide_ref):
    c, j = lax.div(i, arcs), lax.rem(i, arcs)
    total = tiles_ref[i, 0] * wide_ref[c * blocks + lax.rem(index_ref[0, c, j], blocks)]
    return total + tiles_ref[i, 1] * wide_ref[c * blocks + lax.rem(index_ref[1, c, j], blocks)]


def near_kernel(comms, index_ref, v_ref, tiles_hbm, pre_hbm, up_ref, pre_ref, tiles_ref, wide_ref, sems):
    count = up_ref.shape[0]
    arcs = count // comms
    blocks = v_ref.shape[0] // comms
    own = fetch(tiles_hbm.at[:, pl.ds(0, 2)], tiles_ref, sems, 0, PARTS)
    (pre,) = fetch(pre_hbm, pre_ref, sems, PARTS, 1)
    widen(v_ref[...], wide_ref)
    step = count // PARTS
    for n in range(PARTS):
        own[n].wait()

        def one(i, _):
            up_ref[pl.ds(i, 1)] = fold(own_rows(i, blocks, arcs, index_ref, tiles_ref, wide_ref))
            return 0

        lax.fori_loop(n * step, (n + 1) * step, one, 0, unroll=4)
    pre.wait()


def cap_first_kernel(cap_rhs_ref, cap_precond_ref, q_ref):
    precondition(cap_precond_ref, cap_rhs_ref[...], q_ref)


def cap_second_kernel(
    cap_rhs_ref, q0_ref, half_ref, other_ref, cap_precond_ref, yq_ref, q_ref, sums_ref
):
    caps = q0_ref.shape[0]
    note = half_ref[...] + other_ref[...]
    q0 = q0_ref[...]
    yq_ref[...] = q0 + note[:caps]
    sums_ref[...] = note[caps:]
    sums_ref[0:1] += fold(cap_rhs_ref[...] * q0)
    sums_ref[1:2] += fold(q0 * q0)
    precondition(cap_precond_ref, yq_ref[...], q_ref)


def cap_third_kernel(
    alpha_ref, cap_rhs_ref, q0_ref, yq0_ref, q1_ref, half_ref, other_ref, cap_precond_ref,
    zq_ref, yzq_ref, rq_ref, q_ref, sums_ref,
):
    caps = q0_ref.shape[0]
    alpha = alpha_ref[0:1]
    yq0, q1 = yq0_ref[...], q1_ref[...]
    yq1 = q1 + half_ref[:caps] + other_ref[:caps]
    zq = q0_ref[...] - alpha * q1
    yzq = yq0 - alpha * yq1
    rq = cap_rhs_ref[...] - alpha * yq0
    zq_ref[...] = zq
    yzq_ref[...] = yzq
    rq_ref[...] = rq
    precondition(cap_precond_ref, alpha * yzq, q_ref)
    q = q_ref[...]
    pairs = ((zq, yq0), (zq, yzq), (q, yq0), (q, yzq), (q, q), (zq, rq), (q, rq))
    for n, (one, other) in enumerate(pairs):
        sums_ref[n : n + 1] = fold(one * other)
    sums_ref[7:8] = jnp.zeros_like(sums_ref[7:8])


def beside(block, row, lane, n, total):
    return jnp.where(lane == n, jnp.sum(block * row, axis=1, keepdims=True), total)


def arcs_up(comms, blocks, index_ref, cap_index_ref, up_ref, got_ref, q_ref, scale_ref, tiles_hbm, cap_tiles_hbm,
            scaled_ref, note_ref, far_ref, third_ref, cap_tiles_ref, wide_ref, turn_ref, sems):
    count = up_ref.shape[0]
    arcs = count // comms
    width = scale_ref.shape[1]
    thirds = fetch(tiles_hbm.at[:, 2], third_ref, sems, 0, PARTS)
    caps_in = fetch(cap_tiles_hbm, cap_tiles_ref, sems, PARTS, PARTS)

    def place(i, _):
        c, j = lax.div(i, arcs), lax.rem(i, arcs)
        far = index_ref[2, c, j]
        row = c if got_ref.shape[1] == comms else c * blocks + lax.rem(far, blocks)
        far_ref[pl.ds(i, 1)] = got_ref[lax.div(far, blocks), pl.ds(row, 1)]
        return 0

    lax.fori_loop(0, count, place, 0, unroll=4)
    widen(q_ref[...], wide_ref)
    ft = far_ref[...].T
    step = count // PARTS
    lane = lax.broadcasted_iota(jnp.int32, (width, width), 1)
    turned = jnp.zeros((width, width), F32)
    for i in range(count):
        if i % step == 0:
            thirds[i // step].wait()
            caps_in[i // step].wait()
        column = jnp.broadcast_to(ft[:, i : i + 1], third_ref.shape[1:])
        total = third_ref[i] * column + cap_tiles_ref[i] * wide_ref[cap_index_ref[i // arcs, i % arcs]]
        upward = up_ref[i : i + 1] + fold(total)
        far_ref[i : i + 1] = upward
        turned = beside(cap_tiles_ref[i], scale_ref[i : i + 1] * upward, lane, i, turned)
    upward = far_ref[...]
    scaled = scale_ref[...] * upward
    scaled_ref[...] = scaled
    turn_ref[...] = turned.T
    note_ref[...] = jnp.zeros_like(note_ref)

    def put(i, _):
        cap = cap_index_ref[lax.div(i, arcs), lax.rem(i, arcs)]
        note_ref[pl.ds(cap, 1)] += turn_ref[pl.ds(i, 1)]
        return 0

    lax.fori_loop(0, count, put, 0, unroll=4)
    return fold(upward * scaled)


def up_first_kernel(comms, blocks, caps, index_ref, cap_index_ref, up_ref, got_ref, q_ref, scale_ref, rhs_ref, v_ref,
                    tiles_hbm, cap_tiles_hbm, scaled_ref, note_ref, *room):
    energy = arcs_up(comms, blocks, index_ref, cap_index_ref, up_ref, got_ref, q_ref, scale_ref, tiles_hbm,
                     cap_tiles_hbm, scaled_ref, note_ref, *room)
    v = v_ref[...]
    note_ref[caps : caps + 1] = fold(rhs_ref[...] * v)
    note_ref[caps + 1 : caps + 2] = fold(v * v) + energy


def up_second_kernel(comms, blocks, index_ref, cap_index_ref, up_ref, got_ref, q_ref, scale_ref, tiles_hbm,
                     cap_tiles_hbm, scaled_ref, note_ref, *room):
    arcs_up(comms, blocks, index_ref, cap_index_ref, up_ref, got_ref, q_ref, scale_ref, tiles_hbm,
            cap_tiles_hbm, scaled_ref, note_ref, *room)


def up_third_kernel(comms, blocks, caps, index_ref, cap_index_ref, up_ref, got_ref, q_ref, scale_ref, z_ref, yz_ref,
                    r_ref, y0_ref, v_ref, tiles_hbm, cap_tiles_hbm, scaled_ref, notes_ref, note_ref, *room):
    energy = arcs_up(comms, blocks, index_ref, cap_index_ref, up_ref, got_ref, q_ref, scale_ref, tiles_hbm,
                     cap_tiles_hbm, scaled_ref, note_ref, *room)
    z, yz, r, y0, v = z_ref[...], yz_ref[...], r_ref[...], y0_ref[...], v_ref[...]
    pairs = ((z, y0), (z, yz), (v, y0), (v, yz), (v, v), (z, r), (v, r))
    for n, (one, other) in enumerate(pairs):
        note_ref[caps + n : caps + n + 1] = fold(one * other)
    note_ref[caps + 4 : caps + 5] += energy
    notes_ref[...] = jnp.broadcast_to(note_ref[...][None], notes_ref.shape)


def down_kernel(comms, blocks, step_number, index_ref, scaled_ref, sums_ref, tiles_ref, local_ref, back_ref, turn_ref):
    count, touched = tiles_ref.shape[:2]
    width = tiles_ref.shape[3]
    arcs = count // comms
    local_ref[...] = jnp.zeros_like(local_ref)
    if step_number == 0:
        back_ref[...] = jnp.full(back_ref.shape, -1.0, F32)
    lane = lax.broadcasted_iota(jnp.int32, (width, width), 1)
    total = jnp.zeros((width, width), F32)
    for i in range(count):
        row = scaled_ref[i : i + 1]
        for k in range(touched):
            total = beside(tiles_ref[i, k], row, lane, k * count + i, total)
    turn_ref[...] = total.T

    def put(i, _):
        c, j = lax.div(i, arcs), lax.rem(i, arcs)
        for k in range(2):
            b = c * blocks + lax.rem(index_ref[k, c, j], blocks)
            local_ref[pl.ds(b, 1)] += turn_ref[pl.ds(k * count + i, 1)]
        far = index_ref[2, c, j]
        to = lax.div(far, blocks)
        back_ref[to, pl.ds(c, 1)] = turn_ref[pl.ds(2 * count + i, 1)]
        if step_number == 0:
            local = lax.rem(far, blocks).astype(F32)
            back_ref[to, pl.ds(comms + c, 1)] = jnp.full((1, width), local, F32)
        return 0

    lax.fori_loop(0, count, put, 0, unroll=4)
    if step_number == 1:
        shape = (back_ref.shape[0], 2, width)
        back_ref[:, comms : comms + 2] = jnp.broadcast_to(sums_ref[0:2][None], shape)


def add_kernel(note_ref, other_ref, back_ref, out_ref, same_ref):
    del back_ref, same_ref
    out_ref[...] = note_ref[...] + other_ref[...]


def insert_kernel(comms, caps, notes_ref, sums_ref, back_ref, cap_ref, out_ref):
    del back_ref
    total = jnp.sum(notes_ref[...], axis=0)
    cap_ref[...] = total[:caps]
    sums = jnp.sum(total[caps:] + sums_ref[...], axis=1, keepdims=True)
    width = out_ref.shape[2]
    pick = lax.broadcasted_iota(jnp.int32, (NOTE, width), 0) == lax.broadcasted_iota(
        jnp.int32, (NOTE, width), 1
    )
    row = fold(jnp.where(pick, jnp.broadcast_to(sums, (NOTE, width)), 0.0))
    out_ref[:, comms : comms + 1] = jnp.broadcast_to(row[None], (out_ref.shape[0], 1, width))


def collect(comms, v_ref, local_ref, back_ref, asked, y_ref):
    blocks = v_ref.shape[0] // comms
    for c in range(comms):
        part = back_ref[:, c]
        for b in range(blocks):
            n = c * blocks + b
            came = fold(jnp.where(asked[c] == b, part, 0.0))
            y_ref[n : n + 1] = v_ref[n : n + 1] + local_ref[n : n + 1] + came


def pack(comms, v_ref, asked, send_ref):
    blocks = v_ref.shape[0] // comms
    for c in range(comms):
        row = jnp.zeros_like(asked[c])
        for b in range(blocks):
            n = c * blocks + b
            row = jnp.where(asked[c] == b, v_ref[n : n + 1], row)
        send_ref[:, c] = row


def rows_second_kernel(comms, v0_ref, local_ref, back_ref, note_ref, came_ref, precond_ref, half_ref, y_ref,
                       v_ref, send_ref, asked_ref):
    half_ref[...] = note_ref[...] + came_ref[...]
    asked = [back_ref[:, comms + c] for c in range(comms)]
    for c in range(comms):
        asked_ref[c] = asked[c]
    collect(comms, v0_ref, local_ref, back_ref, asked, y_ref)
    precondition(precond_ref, y_ref[...], v_ref)
    pack(comms, v_ref, asked, send_ref)


def rows_third_kernel(comms, rhs_ref, v0_ref, y0_ref, v1_ref, local_ref, back_ref, note_ref, came_ref, asked_ref,
                      precond_ref, half_ref, alpha_ref, z_ref, yz_ref, r_ref, v_ref, send_ref):
    half_ref[...] = note_ref[...] + came_ref[...]
    asked = [asked_ref[c] for c in range(comms)]
    collect(comms, v1_ref, local_ref, back_ref, asked, yz_ref)
    first = jnp.sum(fold(back_ref[:, comms]), axis=1, keepdims=True)
    second = jnp.sum(fold(back_ref[:, comms + 1]), axis=1, keepdims=True)
    alpha = jnp.broadcast_to(first / second, (1, alpha_ref.shape[1]))
    alpha_ref[...] = jnp.broadcast_to(alpha, alpha_ref.shape)
    alpha_ref[1:2] = jnp.broadcast_to(second, (1, alpha_ref.shape[1]))
    y0 = y0_ref[...]
    z_ref[...] = v0_ref[...] - alpha * v1_ref[...]
    yz = y0 - alpha * yz_ref[...]
    yz_ref[...] = yz
    r_ref[...] = rhs_ref[...] - alpha * y0
    precondition(precond_ref, alpha * yz, v_ref)
    pack(comms, v_ref, asked, send_ref)


def last_kernel(comms, alpha_ref, v0_ref, y0_ref, z_ref, yz_ref, r_ref, v2_ref, local_ref, back_ref,
                asked_ref, q0_ref, yq0_ref, zq_ref, yzq_ref, rq_ref, q2_ref, cap_ref,
                sol_ref, cap_sol_ref, res_ref, cap_res_ref, y_ref):
    asked = [asked_ref[c] for c in range(comms)]
    collect(comms, v2_ref, local_ref, back_ref, asked, y_ref)
    row = fold(back_ref[:, comms])
    width = row.shape[1]
    lane = lax.broadcasted_iota(jnp.int32, row.shape, 1)
    s = [
        jnp.broadcast_to(
            jnp.sum(jnp.where(lane == n, row, 0.0), axis=1, keepdims=True), (1, width)
        )
        for n in range(7)
    ]
    alpha, h00 = alpha_ref[0:1], alpha_ref[1:2]
    h1, h2 = s[0] / h00, s[2] / h00
    a11 = s[1] - h1 * s[0]
    a12 = s[3] - h1 * s[2]
    a22 = s[4] - h2 * s[2]
    lower = a12 / a11
    c2 = (s[6] - lower * s[5]) / (a22 - lower * a12)
    c1 = s[5] / a11 - lower * c2
    c0 = c1 * h1 + c2 * h2
    sol_ref[...] = (alpha - c0) * v0_ref[...] + c1 * z_ref[...] + c2 * v2_ref[...]
    cap_sol_ref[...] = (alpha - c0) * q0_ref[...] + c1 * zq_ref[...] + c2 * q2_ref[...]
    res_ref[...] = r_ref[...] + c0 * y0_ref[...] - c1 * yz_ref[...] - c2 * y_ref[...]
    yq2 = q2_ref[...] + cap_ref[...]
    cap_res_ref[...] = rq_ref[...] + c0 * yq0_ref[...] - c1 * yzq_ref[...] - c2 * yq2


def body(
    tiles, cap_tiles, row_index, cap_index, arc_scale, rows_rhs, cap_rhs, precond, cap_precond
):
    comms, arcs, touched = row_index.shape
    blocks, width = rows_rhs.shape[1:]
    caps = cap_rhs.shape[0]
    groups = lax.axis_size("stn") * lax.axis_size("tm")
    peers = lax.axis_size("comm")
    rows, count = comms * blocks, comms * arcs
    flat = (width, width)
    tiles = tiles.reshape(count, touched, *flat)
    cap_tiles = cap_tiles.reshape(count, *flat)
    precond = precond.reshape(rows, *flat)
    index = jnp.transpose(row_index, (2, 0, 1))
    scale = arc_scale.reshape(count, width)
    rhs = rows_rhs.reshape(rows, width)
    row_shape, cap_shape, arc_shape = (rows, width), (caps, width), (count, width)
    small = (NOTE, width)
    note_shape = (caps + NOTE, width)
    send_shape = (groups, comms, width)
    back_shape = (groups, SLOT, width)
    unit = 2 * count * width * width

    def room(*shape):
        return pltpu.VMEM(shape, F32)

    def sems(n):
        return pltpu.SemaphoreType.DMA((n,))

    def exchange(x):
        return lax.all_to_all(x, GROUP, 0, 0)

    def across(x, step):
        return lax.ppermute(x, "comm", [(i, i ^ step) for i in range(peers)])

    def near(v):
        up, pre = call(
            functools.partial(near_kernel, comms), [arc_shape, pltpu.VMEM((caps, *flat), F32)],
            (index, v, tiles, cap_precond), 1,
            [room(count, 2, *flat), room(rows, *flat), sems(PARTS + 1)], flops=2 * unit, hbm=(2, 3),
        )
        return up, kept(pre)

    up_room = [
        room(*arc_shape), room(count, *flat), room(count, *flat), room(caps, *flat), room(*flat), sems(2 * PARTS),
    ]

    def spread(step_number, scaled, sums):
        return call(
            functools.partial(down_kernel, comms, blocks, step_number), [row_shape, back_shape],
            (index, scaled, sums, kept(tiles)), 1, [room(*flat)], flops=3 * unit,
        )

    def add(note, other, back):
        return call(add_kernel, [note_shape, back_shape], (note, other, back), aliases={2: 1}, still=(1,))

    v0, send = call(
        first_kernel, [row_shape, (groups, rows, width)], (rhs, precond), 0,
        [room(*row_shape), room(rows, *flat), sems(PARTS + 1)], hbm=(0, 1),
    )
    got = exchange(send)
    up, pre = near(v0)
    (q0,) = call(cap_first_kernel, [cap_shape], (cap_rhs, pre), flops=unit)
    scaled, note = call(
        functools.partial(up_first_kernel, comms, blocks, caps), [arc_shape, note_shape],
        (index, cap_index, up, got, q0, scale, rhs, v0, tiles, cap_tiles), 2, up_room, flops=3 * unit, hbm=(8, 9),
    )
    other = across(note, 1)
    local, back = spread(0, scaled, rhs)
    note, back = add(note, other, back)
    back = exchange(back)
    half, y0, v1, send, asked = call(
        functools.partial(rows_second_kernel, comms),
        [note_shape, row_shape, row_shape, send_shape, (comms, groups, width)],
        (v0, local, back, note, across(note, 2), kept(precond)),
    )
    got = exchange(send)
    other = across(half, 4)
    up, pre = near(v1)
    yq0, q1, sums = call(
        cap_second_kernel, [cap_shape, cap_shape, small], (cap_rhs, q0, half, other, pre), flops=unit,
    )
    scaled, note = call(
        functools.partial(up_second_kernel, comms, blocks), [arc_shape, note_shape],
        (index, cap_index, up, got, q1, scale, tiles, cap_tiles), 2, up_room, flops=3 * unit, hbm=(6, 7),
    )
    other = across(note, 1)
    local, back = spread(1, scaled, sums)
    note, back = add(note, other, back)
    back = exchange(back)
    half, alpha, z1, yz, r1, v2, send = call(
        functools.partial(rows_third_kernel, comms),
        [note_shape, small, row_shape, row_shape, row_shape, row_shape, send_shape],
        (rhs, v0, y0, v1, local, back, note, across(note, 2), asked, kept(precond)),
    )
    got = exchange(send)
    other = across(half, 4)
    up, pre = near(v2)
    zq1, yzq, rq1, q2, sums = call(
        cap_third_kernel, [cap_shape] * 4 + [small],
        (alpha, cap_rhs, q0, yq0, q1, half, other, pre), flops=unit,
    )
    scaled, notes = call(
        functools.partial(up_third_kernel, comms, blocks, caps), [arc_shape, (peers, *note_shape)],
        (index, cap_index, up, got, q2, scale, z1, yz, r1, y0, v2, tiles, cap_tiles), 2,
        [room(*note_shape), *up_room], flops=3 * unit, hbm=(11, 12),
    )
    notes = lax.all_to_all(notes, "comm", 0, 0)
    local, back = spread(2, scaled, sums)
    cap_sum, back = call(
        functools.partial(insert_kernel, comms, caps), [cap_shape, back_shape], (notes, sums, back),
        aliases={2: 1},
    )
    back = exchange(back)
    sol, cap_sol, res, cap_res = call(
        functools.partial(last_kernel, comms), [row_shape, cap_shape, row_shape, cap_shape],
        (alpha, v0, y0, z1, yz, r1, v2, local, back, asked, q0, yq0, zq1, yzq, rq1, q2, cap_sum), 0,
        [pltpu.VMEM(row_shape, F32)],
    )
    return sol.reshape(rows_rhs.shape), cap_sol, res.reshape(rows_rhs.shape), cap_res


def solution(mesh):
    placed = (
        P("comm", GROUP, None, None, None),
        P("comm", GROUP, None, None),
        P("comm", GROUP, None),
        P("comm", GROUP),
        P("comm", GROUP, None),
        P("comm", GROUP, None),
        P(GROUP, None),
        P("comm", GROUP, None, None),
        P(GROUP, None, None),
    )
    return jax.shard_map(
        body,
        mesh=mesh,
        in_specs=placed,
        out_specs=(
            P("comm", GROUP, None),
            P(GROUP, None),
            P("comm", GROUP, None),
            P(GROUP, None),
        ),
        check_vma=False,
    )
```

```python
import functools

import jax
import jax.numpy as jnp
from jax import lax
from jax.experimental import pallas as pl
from jax.experimental.pallas import tpu as pltpu
from jax.sharding import PartitionSpec as P

GROUP = ("stn", "tm")
F32 = jnp.float32
SLOT = 4
NOTE = 8
VMEM = pl.BlockSpec(memory_space=pltpu.VMEM)
HBM = pl.BlockSpec(memory_space=pltpu.HBM)
ANY = pl.BlockSpec(memory_space=pl.ANY)
PARTS = 4


def call(kernel, outs, args, scalars=0, scratch=(), aliases=None, flops=0, hbm=(), still=()):
    if scalars:
        inner = kernel

        def kernel(*refs):
            sems, held = refs[-1], refs[-1 - scalars : -1]
            copies = [pltpu.make_async_copy(refs[n], held[n], sems.at[n]) for n in range(scalars)]
            for copy in copies:
                copy.start()

            def ready():
                for copy in copies:
                    copy.wait()

            inner(*held, *refs[scalars : -1 - scalars], ready=ready)

        hbm = (*range(scalars), *hbm)
        scratch = [
            *scratch, *(pltpu.SMEM(x.shape, x.dtype) for x in args[:scalars]), pltpu.SemaphoreType.DMA((scalars,)),
        ]
    outs = [jax.ShapeDtypeStruct(o, F32) if isinstance(o, tuple) else o for o in outs]
    args = [
        pltpu.with_memory_space_constraint(x, pltpu.HBM) if n in hbm else x for n, x in enumerate(args)
    ]
    return pl.pallas_call(
        kernel,
        out_shape=outs,
        in_specs=[
            HBM if n in hbm else ANY if (aliases or {}).get(n) in still else VMEM for n in range(len(args))
        ],
        out_specs=[ANY if n in still else VMEM for n in range(len(outs))],
        scratch_shapes=list(scratch),
        input_output_aliases=aliases or {},
        compiler_params=pltpu.CompilerParams(vmem_limit_bytes=12 * 1024 * 1024),
        cost_estimate=pl.CostEstimate(flops=flops, bytes_accessed=4 * 1024 * 1024, transcendentals=0),
    )(*args)


def fetch(source, target, sems, first, parts):
    step = target.shape[0] // parts
    copies = []
    for n in range(parts):
        part = pl.ds(n * step, step)
        copies.append(pltpu.make_async_copy(source.at[part], target.at[part], sems.at[first + n]))
        copies[-1].start()
    return copies


def kept(x):
    return pltpu.with_memory_space_constraint(x, pltpu.VMEM)


def down(block, column):
    return jnp.sum(block * jnp.broadcast_to(column, block.shape), axis=0, keepdims=True)


def fold(x):
    return jnp.sum(x, axis=0, keepdims=True)


def precondition(blocks_ref, x, out_ref, copies=()):
    xt = x.T
    for i in range(x.shape[0]):
        if copies and i % (x.shape[0] // len(copies)) == 0:
            copies[i // (x.shape[0] // len(copies))].wait()
        out_ref[i : i + 1] = down(blocks_ref[i], xt[:, i : i + 1])


def first_kernel(rhs_hbm, precond_hbm, v_ref, send_ref, rhs_ref, precond_ref, sems):
    (small,) = fetch(rhs_hbm, rhs_ref, sems, PARTS, 1)
    copies = fetch(precond_hbm, precond_ref, sems, 0, PARTS)
    small.wait()
    precondition(precond_ref, rhs_ref[...], v_ref, copies)
    send_ref[...] = jnp.broadcast_to(v_ref[...][None], send_ref.shape)


def widen(x, wide_ref):
    xt = x.T
    for i in range(x.shape[0]):
        wide_ref[i] = jnp.broadcast_to(xt[:, i : i + 1], wide_ref.shape[1:])


def own_rows(i, blocks, arcs, index_ref, tiles_ref, wide_ref):
    c, j = lax.div(i, arcs), lax.rem(i, arcs)
    total = tiles_ref[i, 0] * wide_ref[c * blocks + lax.rem(index_ref[0, c, j], blocks)]
    return total + tiles_ref[i, 1] * wide_ref[c * blocks + lax.rem(index_ref[1, c, j], blocks)]


def near_kernel(comms, index_ref, v_ref, tiles_hbm, pre_hbm, up_ref, pre_ref, tiles_ref, wide_ref, sems, ready):
    count = up_ref.shape[0]
    arcs = count // comms
    blocks = v_ref.shape[0] // comms
    own = fetch(tiles_hbm.at[:, pl.ds(0, 2)], tiles_ref, sems, 0, PARTS)
    (pre,) = fetch(pre_hbm, pre_ref, sems, PARTS, 1)
    widen(v_ref[...], wide_ref)
    ready()
    step = count // PARTS
    for n in range(PARTS):
        own[n].wait()

        def one(i, _):
            up_ref[pl.ds(i, 1)] = fold(own_rows(i, blocks, arcs, index_ref, tiles_ref, wide_ref))
            return 0

        lax.fori_loop(n * step, (n + 1) * step, one, 0, unroll=4)
    pre.wait()


def cap_first_kernel(cap_rhs_ref, cap_precond_ref, q_ref):
    precondition(cap_precond_ref, cap_rhs_ref[...], q_ref)


def cap_second_kernel(
    cap_rhs_ref, q0_ref, half_ref, other_ref, cap_precond_ref, yq_ref, q_ref, sums_ref
):
    caps = q0_ref.shape[0]
    note = half_ref[...] + other_ref[...]
    q0 = q0_ref[...]
    yq_ref[...] = q0 + note[:caps]
    sums_ref[...] = note[caps:]
    sums_ref[0:1] += fold(cap_rhs_ref[...] * q0)
    sums_ref[1:2] += fold(q0 * q0)
    precondition(cap_precond_ref, yq_ref[...], q_ref)


def cap_third_kernel(
    alpha_ref, cap_rhs_ref, q0_ref, yq0_ref, q1_ref, half_ref, other_ref, cap_precond_ref,
    zq_ref, yzq_ref, rq_ref, q_ref, sums_ref,
):
    caps = q0_ref.shape[0]
    alpha = alpha_ref[0:1]
    yq0, q1 = yq0_ref[...], q1_ref[...]
    yq1 = q1 + half_ref[:caps] + other_ref[:caps]
    zq = q0_ref[...] - alpha * q1
    yzq = yq0 - alpha * yq1
    rq = cap_rhs_ref[...] - alpha * yq0
    zq_ref[...] = zq
    yzq_ref[...] = yzq
    rq_ref[...] = rq
    precondition(cap_precond_ref, alpha * yzq, q_ref)
    q = q_ref[...]
    pairs = ((zq, yq0), (zq, yzq), (q, yq0), (q, yzq), (q, q), (zq, rq), (q, rq))
    for n, (one, other) in enumerate(pairs):
        sums_ref[n : n + 1] = fold(one * other)
    sums_ref[7:8] = jnp.zeros_like(sums_ref[7:8])


def beside(block, row, lane, n, total):
    return jnp.where(lane == n, jnp.sum(block * row, axis=1, keepdims=True), total)


def arcs_up(comms, blocks, index_ref, cap_index_ref, up_ref, got_ref, q_ref, scale_ref, tiles_hbm, cap_tiles_hbm,
            scaled_ref, note_ref, far_ref, third_ref, cap_tiles_ref, wide_ref, turn_ref, sems, ready):
    count = up_ref.shape[0]
    arcs = count // comms
    width = scale_ref.shape[1]
    thirds = fetch(tiles_hbm.at[:, 2], third_ref, sems, 0, PARTS)
    caps_in = fetch(cap_tiles_hbm, cap_tiles_ref, sems, PARTS, PARTS)
    widen(q_ref[...], wide_ref)
    ready()

    def place(i, _):
        c, j = lax.div(i, arcs), lax.rem(i, arcs)
        far = index_ref[2, c, j]
        row = c if got_ref.shape[1] == comms else c * blocks + lax.rem(far, blocks)
        far_ref[pl.ds(i, 1)] = got_ref[lax.div(far, blocks), pl.ds(row, 1)]
        return 0

    lax.fori_loop(0, count, place, 0, unroll=4)
    ft = far_ref[...].T
    step = count // PARTS
    for i in range(count):
        if i % step == 0:
            thirds[i // step].wait()
            caps_in[i // step].wait()
        column = jnp.broadcast_to(ft[:, i : i + 1], third_ref.shape[1:])
        total = third_ref[i] * column + cap_tiles_ref[i] * wide_ref[cap_index_ref[i // arcs, i % arcs]]
        far_ref[i : i + 1] = up_ref[i : i + 1] + fold(total)
    upward = far_ref[...]
    scaled = scale_ref[...] * upward
    scaled_ref[...] = scaled
    lane = lax.broadcasted_iota(jnp.int32, (width, width), 1)

    total = jnp.zeros((width, width), F32)
    for i in range(count):
        total = beside(cap_tiles_ref[i], scaled[i : i + 1], lane, i, total)
    turn_ref[...] = total.T
    note_ref[...] = jnp.zeros_like(note_ref)

    def put(i, _):
        cap = cap_index_ref[lax.div(i, arcs), lax.rem(i, arcs)]
        note_ref[pl.ds(cap, 1)] += turn_ref[pl.ds(i, 1)]
        return 0

    lax.fori_loop(0, count, put, 0, unroll=4)
    return fold(upward * scaled)


def up_first_kernel(comms, blocks, caps, index_ref, cap_index_ref, up_ref, got_ref, q_ref, scale_ref, rhs_ref, v_ref,
                    tiles_hbm, cap_tiles_hbm, scaled_ref, note_ref, *room, ready):
    energy = arcs_up(comms, blocks, index_ref, cap_index_ref, up_ref, got_ref, q_ref, scale_ref, tiles_hbm,
                     cap_tiles_hbm, scaled_ref, note_ref, *room, ready)
    v = v_ref[...]
    note_ref[caps : caps + 1] = fold(rhs_ref[...] * v)
    note_ref[caps + 1 : caps + 2] = fold(v * v) + energy


def up_second_kernel(comms, blocks, index_ref, cap_index_ref, up_ref, got_ref, q_ref, scale_ref, tiles_hbm,
                     cap_tiles_hbm, scaled_ref, note_ref, *room, ready):
    arcs_up(comms, blocks, index_ref, cap_index_ref, up_ref, got_ref, q_ref, scale_ref, tiles_hbm,
            cap_tiles_hbm, scaled_ref, note_ref, *room, ready)


def up_third_kernel(comms, blocks, caps, index_ref, cap_index_ref, up_ref, got_ref, q_ref, scale_ref, z_ref, yz_ref,
                    r_ref, y0_ref, v_ref, tiles_hbm, cap_tiles_hbm, scaled_ref, notes_ref, note_ref, *room, ready):
    energy = arcs_up(comms, blocks, index_ref, cap_index_ref, up_ref, got_ref, q_ref, scale_ref, tiles_hbm,
                     cap_tiles_hbm, scaled_ref, note_ref, *room, ready)
    z, yz, r, y0, v = z_ref[...], yz_ref[...], r_ref[...], y0_ref[...], v_ref[...]
    pairs = ((z, y0), (z, yz), (v, y0), (v, yz), (v, v), (z, r), (v, r))
    for n, (one, other) in enumerate(pairs):
        note_ref[caps + n : caps + n + 1] = fold(one * other)
    note_ref[caps + 4 : caps + 5] += energy
    notes_ref[...] = jnp.broadcast_to(note_ref[...][None], notes_ref.shape)


def down_kernel(comms, blocks, step_number, index_ref, scaled_ref, sums_ref, tiles_ref, local_ref, back_ref, turn_ref, ready):
    count, touched = tiles_ref.shape[:2]
    width = tiles_ref.shape[3]
    arcs = count // comms
    local_ref[...] = jnp.zeros_like(local_ref)
    if step_number == 0:
        back_ref[...] = jnp.full(back_ref.shape, -1.0, F32)
    lane = lax.broadcasted_iota(jnp.int32, (width, width), 1)
    total = jnp.zeros((width, width), F32)
    for i in range(count):
        row = scaled_ref[i : i + 1]
        for k in range(touched):
            total = beside(tiles_ref[i, k], row, lane, k * count + i, total)
    turn_ref[...] = total.T
    ready()

    def put(i, _):
        c, j = lax.div(i, arcs), lax.rem(i, arcs)
        for k in range(2):
            b = c * blocks + lax.rem(index_ref[k, c, j], blocks)
            local_ref[pl.ds(b, 1)] += turn_ref[pl.ds(k * count + i, 1)]
        far = index_ref[2, c, j]
        to = lax.div(far, blocks)
        back_ref[to, pl.ds(c, 1)] = turn_ref[pl.ds(2 * count + i, 1)]
        if step_number == 0:
            local = lax.rem(far, blocks).astype(F32)
            back_ref[to, pl.ds(comms + c, 1)] = jnp.full((1, width), local, F32)
        return 0

    lax.fori_loop(0, count, put, 0, unroll=4)
    if step_number == 1:
        shape = (back_ref.shape[0], 2, width)
        back_ref[:, comms : comms + 2] = jnp.broadcast_to(sums_ref[0:2][None], shape)


def add_kernel(note_ref, other_ref, back_ref, out_ref, same_ref):
    del back_ref, same_ref
    out_ref[...] = note_ref[...] + other_ref[...]


def insert_kernel(comms, caps, notes_ref, sums_ref, back_ref, cap_ref, out_ref):
    del back_ref
    total = jnp.sum(notes_ref[...], axis=0)
    cap_ref[...] = total[:caps]
    sums = jnp.sum(total[caps:] + sums_ref[...], axis=1, keepdims=True)
    width = out_ref.shape[2]
    pick = lax.broadcasted_iota(jnp.int32, (NOTE, width), 0) == lax.broadcasted_iota(
        jnp.int32, (NOTE, width), 1
    )
    row = fold(jnp.where(pick, jnp.broadcast_to(sums, (NOTE, width)), 0.0))
    out_ref[:, comms : comms + 1] = jnp.broadcast_to(row[None], (out_ref.shape[0], 1, width))


def collect(comms, v_ref, local_ref, back_ref, asked, y_ref):
    blocks = v_ref.shape[0] // comms
    for c in range(comms):
        part = back_ref[:, c]
        for b in range(blocks):
            n = c * blocks + b
            came = fold(jnp.where(asked[c] == b, part, 0.0))
            y_ref[n : n + 1] = v_ref[n : n + 1] + local_ref[n : n + 1] + came


def pack(comms, v_ref, asked, send_ref):
    blocks = v_ref.shape[0] // comms
    for c in range(comms):
        row = jnp.zeros_like(asked[c])
        for b in range(blocks):
            n = c * blocks + b
            row = jnp.where(asked[c] == b, v_ref[n : n + 1], row)
        send_ref[:, c] = row


def rows_second_kernel(comms, v0_ref, local_ref, back_ref, note_ref, came_ref, precond_ref, half_ref, y_ref,
                       v_ref, send_ref, asked_ref):
    half_ref[...] = note_ref[...] + came_ref[...]
    asked = [back_ref[:, comms + c] for c in range(comms)]
    for c in range(comms):
        asked_ref[c] = asked[c]
    collect(comms, v0_ref, local_ref, back_ref, asked, y_ref)
    precondition(precond_ref, y_ref[...], v_ref)
    pack(comms, v_ref, asked, send_ref)


def rows_third_kernel(comms, rhs_ref, v0_ref, y0_ref, v1_ref, local_ref, back_ref, note_ref, came_ref, asked_ref,
                      precond_ref, half_ref, alpha_ref, z_ref, yz_ref, r_ref, v_ref, send_ref):
    half_ref[...] = note_ref[...] + came_ref[...]
    asked = [asked_ref[c] for c in range(comms)]
    collect(comms, v1_ref, local_ref, back_ref, asked, yz_ref)
    first = jnp.sum(fold(back_ref[:, comms]), axis=1, keepdims=True)
    second = jnp.sum(fold(back_ref[:, comms + 1]), axis=1, keepdims=True)
    alpha = jnp.broadcast_to(first / second, (1, alpha_ref.shape[1]))
    alpha_ref[...] = jnp.broadcast_to(alpha, alpha_ref.shape)
    alpha_ref[1:2] = jnp.broadcast_to(second, (1, alpha_ref.shape[1]))
    y0 = y0_ref[...]
    z_ref[...] = v0_ref[...] - alpha * v1_ref[...]
    yz = y0 - alpha * yz_ref[...]
    yz_ref[...] = yz
    r_ref[...] = rhs_ref[...] - alpha * y0
    precondition(precond_ref, alpha * yz, v_ref)
    pack(comms, v_ref, asked, send_ref)


def last_kernel(comms, alpha_ref, v0_ref, y0_ref, z_ref, yz_ref, r_ref, v2_ref, local_ref, back_ref,
                asked_ref, q0_ref, yq0_ref, zq_ref, yzq_ref, rq_ref, q2_ref, cap_ref,
                sol_ref, cap_sol_ref, res_ref, cap_res_ref, y_ref):
    asked = [asked_ref[c] for c in range(comms)]
    collect(comms, v2_ref, local_ref, back_ref, asked, y_ref)
    row = fold(back_ref[:, comms])
    width = row.shape[1]
    lane = lax.broadcasted_iota(jnp.int32, row.shape, 1)
    s = [
        jnp.broadcast_to(
            jnp.sum(jnp.where(lane == n, row, 0.0), axis=1, keepdims=True), (1, width)
        )
        for n in range(7)
    ]
    alpha, h00 = alpha_ref[0:1], alpha_ref[1:2]
    h1, h2 = s[0] / h00, s[2] / h00
    a11 = s[1] - h1 * s[0]
    a12 = s[3] - h1 * s[2]
    a22 = s[4] - h2 * s[2]
    lower = a12 / a11
    c2 = (s[6] - lower * s[5]) / (a22 - lower * a12)
    c1 = s[5] / a11 - lower * c2
    c0 = c1 * h1 + c2 * h2
    sol_ref[...] = (alpha - c0) * v0_ref[...] + c1 * z_ref[...] + c2 * v2_ref[...]
    cap_sol_ref[...] = (alpha - c0) * q0_ref[...] + c1 * zq_ref[...] + c2 * q2_ref[...]
    res_ref[...] = r_ref[...] + c0 * y0_ref[...] - c1 * yz_ref[...] - c2 * y_ref[...]
    yq2 = q2_ref[...] + cap_ref[...]
    cap_res_ref[...] = rq_ref[...] + c0 * yq0_ref[...] - c1 * yzq_ref[...] - c2 * yq2


def body(
    tiles, cap_tiles, row_index, cap_index, arc_scale, rows_rhs, cap_rhs, precond, cap_precond
):
    comms, arcs, touched = row_index.shape
    blocks, width = rows_rhs.shape[1:]
    caps = cap_rhs.shape[0]
    groups = lax.axis_size("stn") * lax.axis_size("tm")
    peers = lax.axis_size("comm")
    rows, count = comms * blocks, comms * arcs
    flat = (width, width)
    tiles = tiles.reshape(count, touched, *flat)
    cap_tiles = cap_tiles.reshape(count, *flat)
    precond = precond.reshape(rows, *flat)
    index = jnp.transpose(row_index, (2, 0, 1))
    scale = arc_scale.reshape(count, width)
    rhs = rows_rhs.reshape(rows, width)
    row_shape, cap_shape, arc_shape = (rows, width), (caps, width), (count, width)
    small = (NOTE, width)
    note_shape = (caps + NOTE, width)
    send_shape = (groups, comms, width)
    back_shape = (groups, SLOT, width)
    unit = 2 * count * width * width

    def room(*shape):
        return pltpu.VMEM(shape, F32)

    def sems(n):
        return pltpu.SemaphoreType.DMA((n,))

    def exchange(x):
        return lax.all_to_all(x, GROUP, 0, 0)

    def across(x, step):
        return lax.ppermute(x, "comm", [(i, i ^ step) for i in range(peers)])

    def near(v):
        up, pre = call(
            functools.partial(near_kernel, comms), [arc_shape, pltpu.VMEM((caps, *flat), F32)],
            (index, v, tiles, cap_precond), 1,
            [room(count, 2, *flat), room(rows, *flat), sems(PARTS + 1)], flops=2 * unit, hbm=(2, 3),
        )
        return up, kept(pre)

    up_room = [
        room(*arc_shape), room(count, *flat), room(count, *flat), room(caps, *flat), room(*flat), sems(2 * PARTS),
    ]

    def spread(step_number, scaled, sums):
        return call(
            functools.partial(down_kernel, comms, blocks, step_number), [row_shape, back_shape],
            (index, scaled, sums, kept(tiles)), 1, [room(*flat)], flops=3 * unit,
        )

    def add(note, other, back):
        return call(add_kernel, [note_shape, back_shape], (note, other, back), aliases={2: 1}, still=(1,))

    v0, send = call(
        first_kernel, [row_shape, (groups, rows, width)], (rhs, precond), 0,
        [room(*row_shape), room(rows, *flat), sems(PARTS + 1)], hbm=(0, 1),
    )
    got = exchange(send)
    up, pre = near(v0)
    (q0,) = call(cap_first_kernel, [cap_shape], (cap_rhs, pre), flops=unit)
    scaled, note = call(
        functools.partial(up_first_kernel, comms, blocks, caps), [arc_shape, note_shape],
        (index, cap_index, up, got, q0, scale, rhs, v0, tiles, cap_tiles), 2, up_room, flops=3 * unit, hbm=(8, 9),
    )
    other = across(note, 4)
    local, back = spread(0, scaled, rhs)
    note, back = add(note, other, back)
    back = exchange(back)
    half, y0, v1, send, asked = call(
        functools.partial(rows_second_kernel, comms),
        [note_shape, row_shape, row_shape, send_shape, (comms, groups, width)],
        (v0, local, back, note, across(note, 1), kept(precond)),
    )
    got = exchange(send)
    other = across(half, 2)
    up, pre = near(v1)
    yq0, q1, sums = call(
        cap_second_kernel, [cap_shape, cap_shape, small], (cap_rhs, q0, half, other, pre), flops=unit,
    )
    scaled, note = call(
        functools.partial(up_second_kernel, comms, blocks), [arc_shape, note_shape],
        (index, cap_index, up, got, q1, scale, tiles, cap_tiles), 2, up_room, flops=3 * unit, hbm=(6, 7),
    )
    other = across(note, 4)
    local, back = spread(1, scaled, sums)
    note, back = add(note, other, back)
    back = exchange(back)
    half, alpha, z1, yz, r1, v2, send = call(
        functools.partial(rows_third_kernel, comms),
        [note_shape, small, row_shape, row_shape, row_shape, row_shape, send_shape],
        (rhs, v0, y0, v1, local, back, note, across(note, 1), asked, kept(precond)),
    )
    got = exchange(send)
    other = across(half, 2)
    up, pre = near(v2)
    zq1, yzq, rq1, q2, sums = call(
        cap_third_kernel, [cap_shape] * 4 + [small],
        (alpha, cap_rhs, q0, yq0, q1, half, other, pre), flops=unit,
    )
    scaled, notes = call(
        functools.partial(up_third_kernel, comms, blocks, caps), [arc_shape, (peers, *note_shape)],
        (index, cap_index, up, got, q2, scale, z1, yz, r1, y0, v2, tiles, cap_tiles), 2,
        [room(*note_shape), *up_room], flops=3 * unit, hbm=(11, 12),
    )
    notes = lax.all_to_all(notes, "comm", 0, 0)
    local, back = spread(2, scaled, sums)
    cap_sum, back = call(
        functools.partial(insert_kernel, comms, caps), [cap_shape, back_shape], (notes, sums, back),
        aliases={2: 1},
    )
    back = exchange(back)
    sol, cap_sol, res, cap_res = call(
        functools.partial(last_kernel, comms), [row_shape, cap_shape, row_shape, cap_shape],
        (alpha, v0, y0, z1, yz, r1, v2, local, back, asked, q0, yq0, zq1, yzq, rq1, q2, cap_sum), 0,
        [pltpu.VMEM(row_shape, F32)],
    )
    return sol.reshape(rows_rhs.shape), cap_sol, res.reshape(rows_rhs.shape), cap_res


def solution(mesh):
    placed = (
        P("comm", GROUP, None, None, None),
        P("comm", GROUP, None, None),
        P("comm", GROUP, None),
        P("comm", GROUP),
        P("comm", GROUP, None),
        P("comm", GROUP, None),
        P(GROUP, None),
        P("comm", GROUP, None, None),
        P(GROUP, None, None),
    )
    return jax.shard_map(
        body,
        mesh=mesh,
        in_specs=placed,
        out_specs=(
            P("comm", GROUP, None),
            P(GROUP, None),
            P("comm", GROUP, None),
            P(GROUP, None),
        ),
        check_vma=False,
    )
```

```python
import functools

import jax
import jax.numpy as jnp
from jax import lax
from jax.experimental import pallas as pl
from jax.experimental.pallas import tpu as pltpu
from jax.sharding import PartitionSpec as P

GROUP = ("stn", "tm")
F32 = jnp.float32
SLOT = 4
NOTE = 8
VMEM = pl.BlockSpec(memory_space=pltpu.VMEM)
HBM = pl.BlockSpec(memory_space=pltpu.HBM)
ANY = pl.BlockSpec(memory_space=pl.ANY)
PARTS = 4


def call(kernel, outs, args, scalars=0, scratch=(), aliases=None, flops=0, hbm=(), still=()):
    if scalars:
        inner = kernel

        def kernel(*refs):
            sems, held = refs[-1], refs[-1 - scalars : -1]
            copies = [pltpu.make_async_copy(refs[n], held[n], sems.at[n]) for n in range(scalars)]
            for copy in copies:
                copy.start()

            def ready():
                for copy in copies:
                    copy.wait()

            inner(*held, *refs[scalars : -1 - scalars], ready=ready)

        hbm = (*range(scalars), *hbm)
        scratch = [
            *scratch, *(pltpu.SMEM(x.shape, x.dtype) for x in args[:scalars]), pltpu.SemaphoreType.DMA((scalars,)),
        ]
    outs = [jax.ShapeDtypeStruct(o, F32) if isinstance(o, tuple) else o for o in outs]
    args = [
        pltpu.with_memory_space_constraint(x, pltpu.HBM) if n in hbm else x for n, x in enumerate(args)
    ]
    return pl.pallas_call(
        kernel,
        out_shape=outs,
        in_specs=[
            HBM if n in hbm else ANY if (aliases or {}).get(n) in still else VMEM for n in range(len(args))
        ],
        out_specs=[ANY if n in still else VMEM for n in range(len(outs))],
        scratch_shapes=list(scratch),
        input_output_aliases=aliases or {},
        compiler_params=pltpu.CompilerParams(vmem_limit_bytes=12 * 1024 * 1024),
        cost_estimate=pl.CostEstimate(flops=flops, bytes_accessed=4 * 1024 * 1024, transcendentals=0),
    )(*args)


def fetch(source, target, sems, first, parts):
    step = target.shape[0] // parts
    copies = []
    for n in range(parts):
        part = pl.ds(n * step, step)
        copies.append(pltpu.make_async_copy(source.at[part], target.at[part], sems.at[first + n]))
        copies[-1].start()
    return copies


def kept(x):
    return pltpu.with_memory_space_constraint(x, pltpu.VMEM)


def down(block, column):
    return jnp.sum(block * jnp.broadcast_to(column, block.shape), axis=0, keepdims=True)


def fold(x):
    return jnp.sum(x, axis=0, keepdims=True)


def precondition(blocks_ref, x, out_ref, copies=()):
    xt = x.T
    for i in range(x.shape[0]):
        if copies and i % (x.shape[0] // len(copies)) == 0:
            copies[i // (x.shape[0] // len(copies))].wait()
        out_ref[i : i + 1] = down(blocks_ref[i], xt[:, i : i + 1])


def first_kernel(rhs_hbm, precond_hbm, v_ref, send_ref, rhs_ref, precond_ref, sems):
    (small,) = fetch(rhs_hbm, rhs_ref, sems, PARTS, 1)
    copies = fetch(precond_hbm, precond_ref, sems, 0, PARTS)
    small.wait()
    precondition(precond_ref, rhs_ref[...], v_ref, copies)
    send_ref[...] = jnp.broadcast_to(v_ref[...][None], send_ref.shape)


def widen(x, wide_ref):
    xt = x.T
    for i in range(x.shape[0]):
        wide_ref[i] = jnp.broadcast_to(xt[:, i : i + 1], wide_ref.shape[1:])


def own_rows(i, blocks, arcs, index_ref, tiles_ref, wide_ref):
    c, j = lax.div(i, arcs), lax.rem(i, arcs)
    total = tiles_ref[i, 0] * wide_ref[c * blocks + lax.rem(index_ref[0, c, j], blocks)]
    return total + tiles_ref[i, 1] * wide_ref[c * blocks + lax.rem(index_ref[1, c, j], blocks)]


def near_kernel(comms, index_ref, v_ref, tiles_hbm, pre_hbm, up_ref, pre_ref, tiles_ref, wide_ref, sems, ready):
    count = up_ref.shape[0]
    arcs = count // comms
    blocks = v_ref.shape[0] // comms
    own = fetch(tiles_hbm.at[:, pl.ds(0, 2)], tiles_ref, sems, 0, PARTS)
    (pre,) = fetch(pre_hbm, pre_ref, sems, PARTS, 1)
    widen(v_ref[...], wide_ref)
    ready()
    step = count // PARTS
    for n in range(PARTS):
        own[n].wait()

        def one(i, _):
            up_ref[pl.ds(i, 1)] = fold(own_rows(i, blocks, arcs, index_ref, tiles_ref, wide_ref))
            return 0

        lax.fori_loop(n * step, (n + 1) * step, one, 0, unroll=4)
    pre.wait()


def cap_first_kernel(cap_rhs_ref, cap_precond_ref, q_ref):
    precondition(cap_precond_ref, cap_rhs_ref[...], q_ref)


def cap_second_kernel(
    cap_rhs_ref, q0_ref, half_ref, other_ref, cap_precond_ref, yq_ref, q_ref, sums_ref
):
    caps = q0_ref.shape[0]
    note = half_ref[...] + other_ref[...]
    q0 = q0_ref[...]
    yq_ref[...] = q0 + note[:caps]
    sums_ref[...] = note[caps:]
    sums_ref[0:1] += fold(cap_rhs_ref[...] * q0)
    sums_ref[1:2] += fold(q0 * q0)
    precondition(cap_precond_ref, yq_ref[...], q_ref)


def cap_third_kernel(
    alpha_ref, cap_rhs_ref, q0_ref, yq0_ref, q1_ref, half_ref, other_ref, cap_precond_ref,
    zq_ref, yzq_ref, rq_ref, q_ref, sums_ref,
):
    caps = q0_ref.shape[0]
    alpha = alpha_ref[0:1]
    yq0, q1 = yq0_ref[...], q1_ref[...]
    yq1 = q1 + half_ref[:caps] + other_ref[:caps]
    zq = q0_ref[...] - alpha * q1
    yzq = yq0 - alpha * yq1
    rq = cap_rhs_ref[...] - alpha * yq0
    zq_ref[...] = zq
    yzq_ref[...] = yzq
    rq_ref[...] = rq
    precondition(cap_precond_ref, alpha * yzq, q_ref)
    q = q_ref[...]
    pairs = ((zq, yq0), (zq, yzq), (q, yq0), (q, yzq), (q, q), (zq, rq), (q, rq))
    for n, (one, other) in enumerate(pairs):
        sums_ref[n : n + 1] = fold(one * other)
    sums_ref[7:8] = jnp.zeros_like(sums_ref[7:8])


def beside(block, row, lane, n, total):
    return jnp.where(lane == n, jnp.sum(block * row, axis=1, keepdims=True), total)


def arcs_up(comms, blocks, index_ref, cap_index_ref, up_ref, got_ref, q_ref, scale_ref, tiles_hbm, cap_tiles_hbm,
            scaled_ref, note_ref, far_ref, third_ref, cap_tiles_ref, wide_ref, turn_ref, sems, ready):
    count = up_ref.shape[0]
    arcs = count // comms
    width = scale_ref.shape[1]
    thirds = fetch(tiles_hbm.at[:, 2], third_ref, sems, 0, PARTS)
    caps_in = fetch(cap_tiles_hbm, cap_tiles_ref, sems, PARTS, PARTS)
    widen(q_ref[...], wide_ref)
    ready()

    def place(i, _):
        c, j = lax.div(i, arcs), lax.rem(i, arcs)
        far = index_ref[2, c, j]
        row = c if got_ref.shape[1] == comms else c * blocks + lax.rem(far, blocks)
        far_ref[pl.ds(i, 1)] = got_ref[lax.div(far, blocks), pl.ds(row, 1)]
        return 0

    lax.fori_loop(0, count, place, 0, unroll=4)
    ft = far_ref[...].T
    step = count // PARTS
    for i in range(count):
        if i % step == 0:
            thirds[i // step].wait()
            caps_in[i // step].wait()
        column = jnp.broadcast_to(ft[:, i : i + 1], third_ref.shape[1:])
        total = third_ref[i] * column + cap_tiles_ref[i] * wide_ref[cap_index_ref[i // arcs, i % arcs]]
        far_ref[i : i + 1] = up_ref[i : i + 1] + fold(total)
    upward = far_ref[...]
    scaled = scale_ref[...] * upward
    scaled_ref[...] = scaled
    lane = lax.broadcasted_iota(jnp.int32, (width, width), 1)

    total = jnp.zeros((width, width), F32)
    for i in range(count):
        total = beside(cap_tiles_ref[i], scaled[i : i + 1], lane, i, total)
    turn_ref[...] = total.T
    note_ref[...] = jnp.zeros_like(note_ref)

    def put(i, _):
        cap = cap_index_ref[lax.div(i, arcs), lax.rem(i, arcs)]
        note_ref[pl.ds(cap, 1)] += turn_ref[pl.ds(i, 1)]
        return 0

    lax.fori_loop(0, count, put, 0, unroll=4)
    return fold(upward * scaled)


def up_first_kernel(comms, blocks, caps, index_ref, cap_index_ref, up_ref, got_ref, q_ref, scale_ref, rhs_ref, v_ref,
                    tiles_hbm, cap_tiles_hbm, scaled_ref, note_ref, *room, ready):
    energy = arcs_up(comms, blocks, index_ref, cap_index_ref, up_ref, got_ref, q_ref, scale_ref, tiles_hbm,
                     cap_tiles_hbm, scaled_ref, note_ref, *room, ready)
    v = v_ref[...]
    note_ref[caps : caps + 1] = fold(rhs_ref[...] * v)
    note_ref[caps + 1 : caps + 2] = fold(v * v) + energy


def up_second_kernel(comms, blocks, index_ref, cap_index_ref, up_ref, got_ref, q_ref, scale_ref, tiles_hbm,
                     cap_tiles_hbm, scaled_ref, note_ref, *room, ready):
    arcs_up(comms, blocks, index_ref, cap_index_ref, up_ref, got_ref, q_ref, scale_ref, tiles_hbm,
            cap_tiles_hbm, scaled_ref, note_ref, *room, ready)


def up_third_kernel(comms, blocks, caps, index_ref, cap_index_ref, up_ref, got_ref, q_ref, scale_ref, z_ref, yz_ref,
                    r_ref, y0_ref, v_ref, tiles_hbm, cap_tiles_hbm, scaled_ref, notes_ref, note_ref, *room, ready):
    energy = arcs_up(comms, blocks, index_ref, cap_index_ref, up_ref, got_ref, q_ref, scale_ref, tiles_hbm,
                     cap_tiles_hbm, scaled_ref, note_ref, *room, ready)
    z, yz, r, y0, v = z_ref[...], yz_ref[...], r_ref[...], y0_ref[...], v_ref[...]
    pairs = ((z, y0), (z, yz), (v, y0), (v, yz), (v, v), (z, r), (v, r))
    for n, (one, other) in enumerate(pairs):
        note_ref[caps + n : caps + n + 1] = fold(one * other)
    note_ref[caps + 4 : caps + 5] += energy
    notes_ref[...] = jnp.broadcast_to(note_ref[...][None], notes_ref.shape)


def down_kernel(comms, blocks, step_number, index_ref, scaled_ref, sums_ref, tiles_ref, local_ref, back_ref, turn_ref, ready):
    count, touched = tiles_ref.shape[:2]
    width = tiles_ref.shape[3]
    arcs = count // comms
    local_ref[...] = jnp.zeros_like(local_ref)
    if step_number == 0:
        back_ref[...] = jnp.full(back_ref.shape, -1.0, F32)
    lane = lax.broadcasted_iota(jnp.int32, (width, width), 1)
    total = jnp.zeros((width, width), F32)
    for i in range(count):
        row = scaled_ref[i : i + 1]
        for k in range(touched):
            total = beside(tiles_ref[i, k], row, lane, k * count + i, total)
    turn_ref[...] = total.T
    ready()

    def put(i, _):
        c, j = lax.div(i, arcs), lax.rem(i, arcs)
        for k in range(2):
            b = c * blocks + lax.rem(index_ref[k, c, j], blocks)
            local_ref[pl.ds(b, 1)] += turn_ref[pl.ds(k * count + i, 1)]
        far = index_ref[2, c, j]
        to = lax.div(far, blocks)
        back_ref[to, pl.ds(c, 1)] = turn_ref[pl.ds(2 * count + i, 1)]
        if step_number == 0:
            local = lax.rem(far, blocks).astype(F32)
            back_ref[to, pl.ds(comms + c, 1)] = jnp.full((1, width), local, F32)
        return 0

    lax.fori_loop(0, count, put, 0, unroll=4)
    if step_number == 1:
        shape = (back_ref.shape[0], 2, width)
        back_ref[:, comms : comms + 2] = jnp.broadcast_to(sums_ref[0:2][None], shape)


def add_kernel(note_ref, other_ref, back_ref, out_ref, same_ref):
    del back_ref, same_ref
    out_ref[...] = note_ref[...] + other_ref[...]


def insert_kernel(comms, caps, notes_ref, sums_ref, back_ref, cap_ref, out_ref):
    del back_ref
    total = jnp.sum(notes_ref[...], axis=0)
    cap_ref[...] = total[:caps]
    sums = jnp.sum(total[caps:] + sums_ref[...], axis=1, keepdims=True)
    width = out_ref.shape[2]
    pick = lax.broadcasted_iota(jnp.int32, (NOTE, width), 0) == lax.broadcasted_iota(
        jnp.int32, (NOTE, width), 1
    )
    row = fold(jnp.where(pick, jnp.broadcast_to(sums, (NOTE, width)), 0.0))
    out_ref[:, comms : comms + 1] = jnp.broadcast_to(row[None], (out_ref.shape[0], 1, width))


def collect(comms, v_ref, local_ref, back_ref, asked, y_ref):
    blocks = v_ref.shape[0] // comms
    for c in range(comms):
        part = back_ref[:, c]
        for b in range(blocks):
            n = c * blocks + b
            came = fold(jnp.where(asked[c] == b, part, 0.0))
            y_ref[n : n + 1] = v_ref[n : n + 1] + local_ref[n : n + 1] + came


def pack(comms, v_ref, asked, send_ref):
    blocks = v_ref.shape[0] // comms
    for c in range(comms):
        row = jnp.zeros_like(asked[c])
        for b in range(blocks):
            n = c * blocks + b
            row = jnp.where(asked[c] == b, v_ref[n : n + 1], row)
        send_ref[:, c] = row


def rows_second_kernel(comms, v0_ref, local_ref, back_ref, precond_ref, y_ref, v_ref, send_ref, asked_ref):
    asked = [back_ref[:, comms + c] for c in range(comms)]
    for c in range(comms):
        asked_ref[c] = asked[c]
    collect(comms, v0_ref, local_ref, back_ref, asked, y_ref)
    precondition(precond_ref, y_ref[...], v_ref)
    pack(comms, v_ref, asked, send_ref)


def rows_third_kernel(comms, rhs_ref, v0_ref, y0_ref, v1_ref, local_ref, back_ref, asked_ref,
                      precond_ref, alpha_ref, z_ref, yz_ref, r_ref, v_ref, send_ref):
    asked = [asked_ref[c] for c in range(comms)]
    collect(comms, v1_ref, local_ref, back_ref, asked, yz_ref)
    first = jnp.sum(fold(back_ref[:, comms]), axis=1, keepdims=True)
    second = jnp.sum(fold(back_ref[:, comms + 1]), axis=1, keepdims=True)
    alpha = jnp.broadcast_to(first / second, (1, alpha_ref.shape[1]))
    alpha_ref[...] = jnp.broadcast_to(alpha, alpha_ref.shape)
    alpha_ref[1:2] = jnp.broadcast_to(second, (1, alpha_ref.shape[1]))
    y0 = y0_ref[...]
    z_ref[...] = v0_ref[...] - alpha * v1_ref[...]
    yz = y0 - alpha * yz_ref[...]
    yz_ref[...] = yz
    r_ref[...] = rhs_ref[...] - alpha * y0
    precondition(precond_ref, alpha * yz, v_ref)
    pack(comms, v_ref, asked, send_ref)


def last_kernel(comms, alpha_ref, v0_ref, y0_ref, z_ref, yz_ref, r_ref, v2_ref, local_ref, back_ref,
                asked_ref, q0_ref, yq0_ref, zq_ref, yzq_ref, rq_ref, q2_ref, cap_ref,
                sol_ref, cap_sol_ref, res_ref, cap_res_ref, y_ref):
    asked = [asked_ref[c] for c in range(comms)]
    collect(comms, v2_ref, local_ref, back_ref, asked, y_ref)
    row = fold(back_ref[:, comms])
    width = row.shape[1]
    lane = lax.broadcasted_iota(jnp.int32, row.shape, 1)
    s = [
        jnp.broadcast_to(
            jnp.sum(jnp.where(lane == n, row, 0.0), axis=1, keepdims=True), (1, width)
        )
        for n in range(7)
    ]
    alpha, h00 = alpha_ref[0:1], alpha_ref[1:2]
    h1, h2 = s[0] / h00, s[2] / h00
    a11 = s[1] - h1 * s[0]
    a12 = s[3] - h1 * s[2]
    a22 = s[4] - h2 * s[2]
    lower = a12 / a11
    c2 = (s[6] - lower * s[5]) / (a22 - lower * a12)
    c1 = s[5] / a11 - lower * c2
    c0 = c1 * h1 + c2 * h2
    sol_ref[...] = (alpha - c0) * v0_ref[...] + c1 * z_ref[...] + c2 * v2_ref[...]
    cap_sol_ref[...] = (alpha - c0) * q0_ref[...] + c1 * zq_ref[...] + c2 * q2_ref[...]
    res_ref[...] = r_ref[...] + c0 * y0_ref[...] - c1 * yz_ref[...] - c2 * y_ref[...]
    yq2 = q2_ref[...] + cap_ref[...]
    cap_res_ref[...] = rq_ref[...] + c0 * yq0_ref[...] - c1 * yzq_ref[...] - c2 * yq2


def body(
    tiles, cap_tiles, row_index, cap_index, arc_scale, rows_rhs, cap_rhs, precond, cap_precond
):
    comms, arcs, touched = row_index.shape
    blocks, width = rows_rhs.shape[1:]
    caps = cap_rhs.shape[0]
    groups = lax.axis_size("stn") * lax.axis_size("tm")
    peers = lax.axis_size("comm")
    rows, count = comms * blocks, comms * arcs
    flat = (width, width)
    tiles = tiles.reshape(count, touched, *flat)
    cap_tiles = cap_tiles.reshape(count, *flat)
    precond = precond.reshape(rows, *flat)
    index = jnp.transpose(row_index, (2, 0, 1))
    scale = arc_scale.reshape(count, width)
    rhs = rows_rhs.reshape(rows, width)
    row_shape, cap_shape, arc_shape = (rows, width), (caps, width), (count, width)
    small = (NOTE, width)
    note_shape = (caps + NOTE, width)
    send_shape = (groups, comms, width)
    back_shape = (groups, SLOT, width)
    unit = 2 * count * width * width

    def room(*shape):
        return pltpu.VMEM(shape, F32)

    def sems(n):
        return pltpu.SemaphoreType.DMA((n,))

    def exchange(x):
        return lax.all_to_all(x, GROUP, 0, 0)

    def across(x, step):
        return lax.ppermute(x, "comm", [(i, i ^ step) for i in range(peers)])

    def near(v):
        up, pre = call(
            functools.partial(near_kernel, comms), [arc_shape, pltpu.VMEM((caps, *flat), F32)],
            (index, v, tiles, cap_precond), 1,
            [room(count, 2, *flat), room(rows, *flat), sems(PARTS + 1)], flops=2 * unit, hbm=(2, 3),
        )
        return up, kept(pre)

    up_room = [
        room(*arc_shape), room(count, *flat), room(count, *flat), room(caps, *flat), room(*flat), sems(2 * PARTS),
    ]

    def spread(step_number, scaled, sums):
        return call(
            functools.partial(down_kernel, comms, blocks, step_number), [row_shape, back_shape],
            (index, scaled, sums, kept(tiles)), 1, [room(*flat)], flops=3 * unit,
        )

    def add(note, other, back):
        return call(add_kernel, [note_shape, back.shape], (note, other, back), aliases={2: 1}, still=(1,))

    v0, send = call(
        first_kernel, [row_shape, (groups, rows, width)], (rhs, precond), 0,
        [room(*row_shape), room(rows, *flat), sems(PARTS + 1)], hbm=(0, 1),
    )
    got = exchange(send)
    up, pre = near(v0)
    (q0,) = call(cap_first_kernel, [cap_shape], (cap_rhs, pre), flops=unit)
    scaled, note = call(
        functools.partial(up_first_kernel, comms, blocks, caps), [arc_shape, note_shape],
        (index, cap_index, up, got, q0, scale, rhs, v0, tiles, cap_tiles), 2, up_room, flops=3 * unit, hbm=(8, 9),
    )
    other = across(note, 1)
    local, back = spread(0, scaled, rhs)
    note, back = add(note, other, back)
    back = exchange(back)
    other = across(note, 4)
    y0, v1, send, asked = call(
        functools.partial(rows_second_kernel, comms),
        [row_shape, row_shape, send_shape, (comms, groups, width)],
        (v0, local, back, kept(precond)),
    )
    half, send = add(note, other, send)
    got = exchange(send)
    other = across(half, 2)
    up, pre = near(v1)
    yq0, q1, sums = call(
        cap_second_kernel, [cap_shape, cap_shape, small], (cap_rhs, q0, half, other, pre), flops=unit,
    )
    scaled, note = call(
        functools.partial(up_second_kernel, comms, blocks), [arc_shape, note_shape],
        (index, cap_index, up, got, q1, scale, tiles, cap_tiles), 2, up_room, flops=3 * unit, hbm=(6, 7),
    )
    other = across(note, 1)
    local, back = spread(1, scaled, sums)
    note, back = add(note, other, back)
    back = exchange(back)
    other = across(note, 4)
    alpha, z1, yz, r1, v2, send = call(
        functools.partial(rows_third_kernel, comms),
        [small, row_shape, row_shape, row_shape, row_shape, send_shape],
        (rhs, v0, y0, v1, local, back, asked, kept(precond)),
    )
    half, send = add(note, other, send)
    got = exchange(send)
    other = across(half, 2)
    up, pre = near(v2)
    zq1, yzq, rq1, q2, sums = call(
        cap_third_kernel, [cap_shape] * 4 + [small],
        (alpha, cap_rhs, q0, yq0, q1, half, other, pre), flops=unit,
    )
    scaled, notes = call(
        functools.partial(up_third_kernel, comms, blocks, caps), [arc_shape, (peers, *note_shape)],
        (index, cap_index, up, got, q2, scale, z1, yz, r1, y0, v2, tiles, cap_tiles), 2,
        [room(*note_shape), *up_room], flops=3 * unit, hbm=(11, 12),
    )
    notes = lax.all_to_all(notes, "comm", 0, 0)
    local, back = spread(2, scaled, sums)
    cap_sum, back = call(
        functools.partial(insert_kernel, comms, caps), [cap_shape, back_shape], (notes, sums, back),
        aliases={2: 1},
    )
    back = exchange(back)
    sol, cap_sol, res, cap_res = call(
        functools.partial(last_kernel, comms), [row_shape, cap_shape, row_shape, cap_shape],
        (alpha, v0, y0, z1, yz, r1, v2, local, back, asked, q0, yq0, zq1, yzq, rq1, q2, cap_sum), 0,
        [pltpu.VMEM(row_shape, F32)],
    )
    return sol.reshape(rows_rhs.shape), cap_sol, res.reshape(rows_rhs.shape), cap_res


def solution(mesh):
    placed = (
        P("comm", GROUP, None, None, None),
        P("comm", GROUP, None, None),
        P("comm", GROUP, None),
        P("comm", GROUP),
        P("comm", GROUP, None),
        P("comm", GROUP, None),
        P(GROUP, None),
        P("comm", GROUP, None, None),
        P(GROUP, None, None),
    )
    return jax.shard_map(
        body,
        mesh=mesh,
        in_specs=placed,
        out_specs=(
            P("comm", GROUP, None),
            P(GROUP, None),
            P("comm", GROUP, None),
            P(GROUP, None),
        ),
        check_vma=False,
    )
```

```python
import functools

import jax
import jax.numpy as jnp
from jax import lax
from jax.experimental import pallas as pl
from jax.experimental.pallas import tpu as pltpu
from jax.sharding import PartitionSpec as P

GROUP = ("stn", "tm")
F32 = jnp.float32
SLOT = 4
NOTE = 8
VMEM = pl.BlockSpec(memory_space=pltpu.VMEM)
HBM = pl.BlockSpec(memory_space=pltpu.HBM)
ANY = pl.BlockSpec(memory_space=pl.ANY)
PARTS = 4


def call(kernel, outs, args, scalars=0, scratch=(), aliases=None, flops=0, hbm=(), still=()):
    if scalars:
        inner = kernel

        def kernel(*refs):
            sems, held = refs[-1], refs[-1 - scalars : -1]
            copies = [pltpu.make_async_copy(refs[n], held[n], sems.at[n]) for n in range(scalars)]
            for copy in copies:
                copy.start()

            def ready():
                for copy in copies:
                    copy.wait()

            inner(*held, *refs[scalars : -1 - scalars], ready=ready)

        hbm = (*range(scalars), *hbm)
        scratch = [
            *scratch, *(pltpu.SMEM(x.shape, x.dtype) for x in args[:scalars]), pltpu.SemaphoreType.DMA((scalars,)),
        ]
    outs = [jax.ShapeDtypeStruct(o, F32) if isinstance(o, tuple) else o for o in outs]
    args = [
        pltpu.with_memory_space_constraint(x, pltpu.HBM) if n in hbm else x for n, x in enumerate(args)
    ]
    return pl.pallas_call(
        kernel,
        out_shape=outs,
        in_specs=[
            HBM if n in hbm else ANY if (aliases or {}).get(n) in still else VMEM for n in range(len(args))
        ],
        out_specs=[ANY if n in still else VMEM for n in range(len(outs))],
        scratch_shapes=list(scratch),
        input_output_aliases=aliases or {},
        compiler_params=pltpu.CompilerParams(vmem_limit_bytes=12 * 1024 * 1024),
        cost_estimate=pl.CostEstimate(flops=flops, bytes_accessed=4 * 1024 * 1024, transcendentals=0),
    )(*args)


def fetch(source, target, sems, first, parts):
    step = target.shape[0] // parts
    copies = []
    for n in range(parts):
        part = pl.ds(n * step, step)
        copies.append(pltpu.make_async_copy(source.at[part], target.at[part], sems.at[first + n]))
        copies[-1].start()
    return copies


def kept(x):
    return pltpu.with_memory_space_constraint(x, pltpu.VMEM)


def down(block, column):
    return jnp.sum(block * jnp.broadcast_to(column, block.shape), axis=0, keepdims=True)


def fold(x):
    return jnp.sum(x, axis=0, keepdims=True)


def precondition(blocks_ref, x, out_ref, copies=()):
    xt = x.T
    for i in range(x.shape[0]):
        if copies and i % (x.shape[0] // len(copies)) == 0:
            copies[i // (x.shape[0] // len(copies))].wait()
        out_ref[i : i + 1] = down(blocks_ref[i], xt[:, i : i + 1])


def first_kernel(rhs_hbm, precond_hbm, v_ref, send_ref, rhs_ref, precond_ref, sems):
    (small,) = fetch(rhs_hbm, rhs_ref, sems, PARTS, 1)
    copies = fetch(precond_hbm, precond_ref, sems, 0, PARTS)
    small.wait()
    precondition(precond_ref, rhs_ref[...], v_ref, copies)
    send_ref[...] = jnp.broadcast_to(v_ref[...][None], send_ref.shape)


def widen(x, wide_ref):
    xt = x.T
    for i in range(x.shape[0]):
        wide_ref[i] = jnp.broadcast_to(xt[:, i : i + 1], wide_ref.shape[1:])


def own_rows(i, blocks, arcs, index_ref, tiles_ref, wide_ref):
    c, j = lax.div(i, arcs), lax.rem(i, arcs)
    total = tiles_ref[i, 0] * wide_ref[c * blocks + lax.rem(index_ref[0, c, j], blocks)]
    return total + tiles_ref[i, 1] * wide_ref[c * blocks + lax.rem(index_ref[1, c, j], blocks)]


def near_kernel(comms, index_ref, v_ref, tiles_hbm, pre_hbm, up_ref, pre_ref, tiles_ref, wide_ref, sems, ready):
    count = up_ref.shape[0]
    arcs = count // comms
    blocks = v_ref.shape[0] // comms
    own = fetch(tiles_hbm.at[:, pl.ds(0, 2)], tiles_ref, sems, 0, PARTS)
    (pre,) = fetch(pre_hbm, pre_ref, sems, PARTS, 1)
    widen(v_ref[...], wide_ref)
    ready()
    step = count // PARTS
    for n in range(PARTS):
        own[n].wait()

        def one(i, _):
            up_ref[pl.ds(i, 1)] = fold(own_rows(i, blocks, arcs, index_ref, tiles_ref, wide_ref))
            return 0

        lax.fori_loop(n * step, (n + 1) * step, one, 0, unroll=4)
    pre.wait()


def cap_first_kernel(cap_rhs_ref, cap_precond_ref, q_ref):
    precondition(cap_precond_ref, cap_rhs_ref[...], q_ref)


def cap_second_kernel(
    cap_rhs_ref, q0_ref, half_ref, other_ref, cap_precond_ref, yq_ref, q_ref, sums_ref
):
    caps = q0_ref.shape[0]
    note = half_ref[...] + other_ref[...]
    q0 = q0_ref[...]
    yq_ref[...] = q0 + note[:caps]
    sums_ref[...] = note[caps:]
    sums_ref[0:1] += fold(cap_rhs_ref[...] * q0)
    sums_ref[1:2] += fold(q0 * q0)
    precondition(cap_precond_ref, yq_ref[...], q_ref)


def cap_third_kernel(
    alpha_ref, cap_rhs_ref, q0_ref, yq0_ref, q1_ref, half_ref, other_ref, cap_precond_ref,
    zq_ref, yzq_ref, rq_ref, q_ref, sums_ref,
):
    caps = q0_ref.shape[0]
    alpha = alpha_ref[0:1]
    yq0, q1 = yq0_ref[...], q1_ref[...]
    yq1 = q1 + half_ref[:caps] + other_ref[:caps]
    zq = q0_ref[...] - alpha * q1
    yzq = yq0 - alpha * yq1
    rq = cap_rhs_ref[...] - alpha * yq0
    zq_ref[...] = zq
    yzq_ref[...] = yzq
    rq_ref[...] = rq
    precondition(cap_precond_ref, alpha * yzq, q_ref)
    q = q_ref[...]
    pairs = ((zq, yq0), (zq, yzq), (q, yq0), (q, yzq), (q, q), (zq, rq), (q, rq))
    for n, (one, other) in enumerate(pairs):
        sums_ref[n : n + 1] = fold(one * other)
    sums_ref[7:8] = jnp.zeros_like(sums_ref[7:8])


def beside(block, row, lane, n, total):
    return jnp.where(lane == n, jnp.sum(block * row, axis=1, keepdims=True), total)


def arcs_up(comms, blocks, index_ref, cap_index_ref, up_ref, got_ref, q_ref, scale_ref, tiles_hbm, cap_tiles_hbm,
            scaled_ref, note_ref, far_ref, third_ref, cap_tiles_ref, wide_ref, turn_ref, sems, ready):
    count = up_ref.shape[0]
    arcs = count // comms
    width = scale_ref.shape[1]
    thirds = fetch(tiles_hbm.at[:, 2], third_ref, sems, 0, PARTS)
    caps_in = fetch(cap_tiles_hbm, cap_tiles_ref, sems, PARTS, PARTS)
    widen(q_ref[...], wide_ref)
    ready()

    def place(i, _):
        c, j = lax.div(i, arcs), lax.rem(i, arcs)
        far = index_ref[2, c, j]
        row = c if got_ref.shape[1] == comms else c * blocks + lax.rem(far, blocks)
        far_ref[pl.ds(i, 1)] = got_ref[lax.div(far, blocks), pl.ds(row, 1)]
        return 0

    lax.fori_loop(0, count, place, 0, unroll=4)
    ft = far_ref[...].T
    step = count // PARTS
    for i in range(count):
        if i % step == 0:
            thirds[i // step].wait()
            caps_in[i // step].wait()
        column = jnp.broadcast_to(ft[:, i : i + 1], third_ref.shape[1:])
        total = third_ref[i] * column + cap_tiles_ref[i] * wide_ref[cap_index_ref[i // arcs, i % arcs]]
        far_ref[i : i + 1] = up_ref[i : i + 1] + fold(total)
    upward = far_ref[...]
    scaled = scale_ref[...] * upward
    scaled_ref[...] = scaled
    lane = lax.broadcasted_iota(jnp.int32, (width, width), 1)

    total = jnp.zeros((width, width), F32)
    for i in range(count):
        total = beside(cap_tiles_ref[i], scaled[i : i + 1], lane, i, total)
    turn_ref[...] = total.T
    note_ref[...] = jnp.zeros_like(note_ref)

    def put(i, _):
        cap = cap_index_ref[lax.div(i, arcs), lax.rem(i, arcs)]
        note_ref[pl.ds(cap, 1)] += turn_ref[pl.ds(i, 1)]
        return 0

    lax.fori_loop(0, count, put, 0, unroll=4)
    return fold(upward * scaled)


def up_first_kernel(comms, blocks, caps, index_ref, cap_index_ref, up_ref, got_ref, q_ref, scale_ref, rhs_ref, v_ref,
                    tiles_hbm, cap_tiles_hbm, scaled_ref, note_ref, *room, ready):
    energy = arcs_up(comms, blocks, index_ref, cap_index_ref, up_ref, got_ref, q_ref, scale_ref, tiles_hbm,
                     cap_tiles_hbm, scaled_ref, note_ref, *room, ready)
    v = v_ref[...]
    note_ref[caps : caps + 1] = fold(rhs_ref[...] * v)
    note_ref[caps + 1 : caps + 2] = fold(v * v) + energy


def up_second_kernel(comms, blocks, index_ref, cap_index_ref, up_ref, got_ref, q_ref, scale_ref, tiles_hbm,
                     cap_tiles_hbm, scaled_ref, note_ref, *room, ready):
    arcs_up(comms, blocks, index_ref, cap_index_ref, up_ref, got_ref, q_ref, scale_ref, tiles_hbm,
            cap_tiles_hbm, scaled_ref, note_ref, *room, ready)


def up_third_kernel(comms, blocks, caps, index_ref, cap_index_ref, up_ref, got_ref, q_ref, scale_ref, z_ref, yz_ref,
                    r_ref, y0_ref, v_ref, tiles_hbm, cap_tiles_hbm, scaled_ref, notes_ref, note_ref, *room, ready):
    energy = arcs_up(comms, blocks, index_ref, cap_index_ref, up_ref, got_ref, q_ref, scale_ref, tiles_hbm,
                     cap_tiles_hbm, scaled_ref, note_ref, *room, ready)
    z, yz, r, y0, v = z_ref[...], yz_ref[...], r_ref[...], y0_ref[...], v_ref[...]
    pairs = ((z, y0), (z, yz), (v, y0), (v, yz), (v, v), (z, r), (v, r))
    for n, (one, other) in enumerate(pairs):
        note_ref[caps + n : caps + n + 1] = fold(one * other)
    note_ref[caps + 4 : caps + 5] += energy
    notes_ref[...] = jnp.broadcast_to(note_ref[...][None], notes_ref.shape)


def down_kernel(comms, blocks, step_number, index_ref, scaled_ref, sums_ref, tiles_ref, local_ref, back_ref, turn_ref, *room, ready):
    count, touched = tiles_ref.shape[:2]
    width = tiles_ref.shape[3]
    arcs = count // comms
    copies = []
    if step_number == 2:
        tiles_hbm, (tiles_ref, sems) = tiles_ref, room
        copies = fetch(tiles_hbm, tiles_ref, sems, 0, 2 * PARTS)
    local_ref[...] = jnp.zeros_like(local_ref)
    if step_number == 0:
        back_ref[...] = jnp.full(back_ref.shape, -1.0, F32)
    lane = lax.broadcasted_iota(jnp.int32, (width, width), 1)
    total = jnp.zeros((width, width), F32)
    for i in range(count):
        if copies and i % (count // len(copies)) == 0:
            copies[i // (count // len(copies))].wait()
        row = scaled_ref[i : i + 1]
        for k in range(touched):
            total = beside(tiles_ref[i, k], row, lane, k * count + i, total)
    turn_ref[...] = total.T
    ready()

    def put(i, _):
        c, j = lax.div(i, arcs), lax.rem(i, arcs)
        for k in range(2):
            b = c * blocks + lax.rem(index_ref[k, c, j], blocks)
            local_ref[pl.ds(b, 1)] += turn_ref[pl.ds(k * count + i, 1)]
        far = index_ref[2, c, j]
        to = lax.div(far, blocks)
        back_ref[to, pl.ds(c, 1)] = turn_ref[pl.ds(2 * count + i, 1)]
        if step_number == 0:
            local = lax.rem(far, blocks).astype(F32)
            back_ref[to, pl.ds(comms + c, 1)] = jnp.full((1, width), local, F32)
        return 0

    lax.fori_loop(0, count, put, 0, unroll=4)
    if step_number == 1:
        shape = (back_ref.shape[0], 2, width)
        back_ref[:, comms : comms + 2] = jnp.broadcast_to(sums_ref[0:2][None], shape)


def add_kernel(note_ref, other_ref, back_ref, out_ref, same_ref):
    del back_ref, same_ref
    out_ref[...] = note_ref[...] + other_ref[...]


def insert_kernel(comms, caps, notes_ref, sums_ref, back_ref, cap_ref, out_ref):
    del back_ref
    total = jnp.sum(notes_ref[...], axis=0)
    cap_ref[...] = total[:caps]
    sums = jnp.sum(total[caps:] + sums_ref[...], axis=1, keepdims=True)
    width = out_ref.shape[2]
    pick = lax.broadcasted_iota(jnp.int32, (NOTE, width), 0) == lax.broadcasted_iota(
        jnp.int32, (NOTE, width), 1
    )
    row = fold(jnp.where(pick, jnp.broadcast_to(sums, (NOTE, width)), 0.0))
    out_ref[:, comms : comms + 1] = jnp.broadcast_to(row[None], (out_ref.shape[0], 1, width))


def collect(comms, v_ref, local_ref, back_ref, asked, y_ref):
    blocks = v_ref.shape[0] // comms
    for c in range(comms):
        part = back_ref[:, c]
        for b in range(blocks):
            n = c * blocks + b
            came = fold(jnp.where(asked[c] == b, part, 0.0))
            y_ref[n : n + 1] = v_ref[n : n + 1] + local_ref[n : n + 1] + came


def pack(comms, v_ref, asked, send_ref):
    blocks = v_ref.shape[0] // comms
    for c in range(comms):
        row = jnp.zeros_like(asked[c])
        for b in range(blocks):
            n = c * blocks + b
            row = jnp.where(asked[c] == b, v_ref[n : n + 1], row)
        send_ref[:, c] = row


def rows_second_kernel(comms, v0_ref, local_ref, back_ref, precond_ref, y_ref, v_ref, send_ref, asked_ref):
    asked = [back_ref[:, comms + c] for c in range(comms)]
    for c in range(comms):
        asked_ref[c] = asked[c]
    collect(comms, v0_ref, local_ref, back_ref, asked, y_ref)
    precondition(precond_ref, y_ref[...], v_ref)
    pack(comms, v_ref, asked, send_ref)


def rows_third_kernel(comms, rhs_ref, v0_ref, y0_ref, v1_ref, local_ref, back_ref, asked_ref,
                      precond_ref, alpha_ref, z_ref, yz_ref, r_ref, v_ref, send_ref):
    asked = [asked_ref[c] for c in range(comms)]
    collect(comms, v1_ref, local_ref, back_ref, asked, yz_ref)
    first = jnp.sum(fold(back_ref[:, comms]), axis=1, keepdims=True)
    second = jnp.sum(fold(back_ref[:, comms + 1]), axis=1, keepdims=True)
    alpha = jnp.broadcast_to(first / second, (1, alpha_ref.shape[1]))
    alpha_ref[...] = jnp.broadcast_to(alpha, alpha_ref.shape)
    alpha_ref[1:2] = jnp.broadcast_to(second, (1, alpha_ref.shape[1]))
    y0 = y0_ref[...]
    z_ref[...] = v0_ref[...] - alpha * v1_ref[...]
    yz = y0 - alpha * yz_ref[...]
    yz_ref[...] = yz
    r_ref[...] = rhs_ref[...] - alpha * y0
    precondition(precond_ref, alpha * yz, v_ref)
    pack(comms, v_ref, asked, send_ref)


def last_kernel(comms, alpha_ref, v0_ref, y0_ref, z_ref, yz_ref, r_ref, v2_ref, local_ref, back_ref,
                asked_ref, q0_ref, yq0_ref, zq_ref, yzq_ref, rq_ref, q2_ref, cap_ref,
                sol_ref, cap_sol_ref, res_ref, cap_res_ref, y_ref):
    asked = [asked_ref[c] for c in range(comms)]
    collect(comms, v2_ref, local_ref, back_ref, asked, y_ref)
    row = fold(back_ref[:, comms])
    width = row.shape[1]
    lane = lax.broadcasted_iota(jnp.int32, row.shape, 1)
    s = [
        jnp.broadcast_to(
            jnp.sum(jnp.where(lane == n, row, 0.0), axis=1, keepdims=True), (1, width)
        )
        for n in range(7)
    ]
    alpha, h00 = alpha_ref[0:1], alpha_ref[1:2]
    h1, h2 = s[0] / h00, s[2] / h00
    a11 = s[1] - h1 * s[0]
    a12 = s[3] - h1 * s[2]
    a22 = s[4] - h2 * s[2]
    lower = a12 / a11
    c2 = (s[6] - lower * s[5]) / (a22 - lower * a12)
    c1 = s[5] / a11 - lower * c2
    c0 = c1 * h1 + c2 * h2
    sol_ref[...] = (alpha - c0) * v0_ref[...] + c1 * z_ref[...] + c2 * v2_ref[...]
    cap_sol_ref[...] = (alpha - c0) * q0_ref[...] + c1 * zq_ref[...] + c2 * q2_ref[...]
    res_ref[...] = r_ref[...] + c0 * y0_ref[...] - c1 * yz_ref[...] - c2 * y_ref[...]
    yq2 = q2_ref[...] + cap_ref[...]
    cap_res_ref[...] = rq_ref[...] + c0 * yq0_ref[...] - c1 * yzq_ref[...] - c2 * yq2


def body(
    tiles, cap_tiles, row_index, cap_index, arc_scale, rows_rhs, cap_rhs, precond, cap_precond
):
    comms, arcs, touched = row_index.shape
    blocks, width = rows_rhs.shape[1:]
    caps = cap_rhs.shape[0]
    groups = lax.axis_size("stn") * lax.axis_size("tm")
    peers = lax.axis_size("comm")
    rows, count = comms * blocks, comms * arcs
    flat = (width, width)
    tiles = tiles.reshape(count, touched, *flat)
    cap_tiles = cap_tiles.reshape(count, *flat)
    precond = precond.reshape(rows, *flat)
    index = jnp.transpose(row_index, (2, 0, 1))
    scale = arc_scale.reshape(count, width)
    rhs = rows_rhs.reshape(rows, width)
    row_shape, cap_shape, arc_shape = (rows, width), (caps, width), (count, width)
    small = (NOTE, width)
    note_shape = (caps + NOTE, width)
    send_shape = (groups, comms, width)
    back_shape = (groups, SLOT, width)
    unit = 2 * count * width * width

    def room(*shape):
        return pltpu.VMEM(shape, F32)

    def sems(n):
        return pltpu.SemaphoreType.DMA((n,))

    def exchange(x):
        return lax.all_to_all(x, GROUP, 0, 0)

    def across(x, step):
        return lax.ppermute(x, "comm", [(i, i ^ step) for i in range(peers)])

    def near(v):
        up, pre = call(
            functools.partial(near_kernel, comms), [arc_shape, pltpu.VMEM((caps, *flat), F32)],
            (index, v, tiles, cap_precond), 1,
            [room(count, 2, *flat), room(rows, *flat), sems(PARTS + 1)], flops=2 * unit, hbm=(2, 3),
        )
        return up, kept(pre)

    up_room = [
        room(*arc_shape), room(count, *flat), room(count, *flat), room(caps, *flat), room(*flat), sems(2 * PARTS),
    ]

    def spread(step_number, scaled, sums):
        return call(
            functools.partial(down_kernel, comms, blocks, step_number), [row_shape, back_shape],
            (index, scaled, sums, kept(tiles) if step_number < 2 else tiles), 1,
            [room(*flat)] + ([room(count, touched, *flat), sems(2 * PARTS)] if step_number == 2 else []),
            flops=3 * unit, hbm=(3,) if step_number == 2 else (),
        )

    def add(note, other, back):
        return call(add_kernel, [note_shape, back.shape], (note, other, back), aliases={2: 1}, still=(1,))

    v0, send = call(
        first_kernel, [row_shape, (groups, rows, width)], (rhs, precond), 0,
        [room(*row_shape), room(rows, *flat), sems(PARTS + 1)], hbm=(0, 1),
    )
    got = exchange(send)
    up, pre = near(v0)
    (q0,) = call(cap_first_kernel, [cap_shape], (cap_rhs, pre), flops=unit)
    scaled, note = call(
        functools.partial(up_first_kernel, comms, blocks, caps), [arc_shape, note_shape],
        (index, cap_index, up, got, q0, scale, rhs, v0, tiles, cap_tiles), 2, up_room, flops=3 * unit, hbm=(8, 9),
    )
    other = across(note, 1)
    local, back = spread(0, scaled, rhs)
    note, back = add(note, other, back)
    back = exchange(back)
    other = across(note, 4)
    y0, v1, send, asked = call(
        functools.partial(rows_second_kernel, comms),
        [row_shape, row_shape, send_shape, (comms, groups, width)],
        (v0, local, back, kept(precond)),
    )
    half, send = add(note, other, send)
    got = exchange(send)
    other = across(half, 2)
    up, pre = near(v1)
    yq0, q1, sums = call(
        cap_second_kernel, [cap_shape, cap_shape, small], (cap_rhs, q0, half, other, pre), flops=unit,
    )
    scaled, note = call(
        functools.partial(up_second_kernel, comms, blocks), [arc_shape, note_shape],
        (index, cap_index, up, got, q1, scale, tiles, cap_tiles), 2, up_room, flops=3 * unit, hbm=(6, 7),
    )
    other = across(note, 1)
    local, back = spread(1, scaled, sums)
    note, back = add(note, other, back)
    back = exchange(back)
    other = across(note, 4)
    alpha, z1, yz, r1, v2, send = call(
        functools.partial(rows_third_kernel, comms),
        [small, row_shape, row_shape, row_shape, row_shape, send_shape],
        (rhs, v0, y0, v1, local, back, asked, kept(precond)),
    )
    half, send = add(note, other, send)
    got = exchange(send)
    other = across(half, 2)
    up, pre = near(v2)
    zq1, yzq, rq1, q2, sums = call(
        cap_third_kernel, [cap_shape] * 4 + [small],
        (alpha, cap_rhs, q0, yq0, q1, half, other, pre), flops=unit,
    )
    scaled, notes = call(
        functools.partial(up_third_kernel, comms, blocks, caps), [arc_shape, (peers, *note_shape)],
        (index, cap_index, up, got, q2, scale, z1, yz, r1, y0, v2, tiles, cap_tiles), 2,
        [room(*note_shape), *up_room], flops=3 * unit, hbm=(11, 12),
    )
    notes = lax.all_to_all(notes, "comm", 0, 0)
    local, back = spread(2, scaled, sums)
    cap_sum, back = call(
        functools.partial(insert_kernel, comms, caps), [cap_shape, back_shape], (notes, sums, back),
        aliases={2: 1},
    )
    back = exchange(back)
    sol, cap_sol, res, cap_res = call(
        functools.partial(last_kernel, comms), [row_shape, cap_shape, row_shape, cap_shape],
        (alpha, v0, y0, z1, yz, r1, v2, local, back, asked, q0, yq0, zq1, yzq, rq1, q2, cap_sum), 0,
        [pltpu.VMEM(row_shape, F32)],
    )
    return sol.reshape(rows_rhs.shape), cap_sol, res.reshape(rows_rhs.shape), cap_res


def solution(mesh):
    placed = (
        P("comm", GROUP, None, None, None),
        P("comm", GROUP, None, None),
        P("comm", GROUP, None),
        P("comm", GROUP),
        P("comm", GROUP, None),
        P("comm", GROUP, None),
        P(GROUP, None),
        P("comm", GROUP, None, None),
        P(GROUP, None, None),
    )
    return jax.shard_map(
        body,
        mesh=mesh,
        in_specs=placed,
        out_specs=(
            P("comm", GROUP, None),
            P(GROUP, None),
            P("comm", GROUP, None),
            P(GROUP, None),
        ),
        check_vma=False,
    )
```

```python
import functools

import jax
import jax.numpy as jnp
from jax import lax
from jax.experimental import pallas as pl
from jax.experimental.pallas import tpu as pltpu
from jax.sharding import PartitionSpec as P

GROUP = ("stn", "tm")
F32 = jnp.float32
SLOT = 4
NOTE = 8
VMEM = pl.BlockSpec(memory_space=pltpu.VMEM)
HBM = pl.BlockSpec(memory_space=pltpu.HBM)
ANY = pl.BlockSpec(memory_space=pl.ANY)
PARTS = 4


def call(kernel, outs, args, scalars=0, scratch=(), aliases=None, flops=0, hbm=(), still=()):
    if scalars:
        inner = kernel

        def kernel(*refs):
            sems, held = refs[-1], refs[-1 - scalars : -1]
            copies = [pltpu.make_async_copy(refs[n], held[n], sems.at[n]) for n in range(scalars)]
            for copy in copies:
                copy.start()

            def ready():
                for copy in copies:
                    copy.wait()

            inner(*held, *refs[scalars : -1 - scalars], ready=ready)

        hbm = (*range(scalars), *hbm)
        scratch = [
            *scratch, *(pltpu.SMEM(x.shape, x.dtype) for x in args[:scalars]), pltpu.SemaphoreType.DMA((scalars,)),
        ]
    outs = [jax.ShapeDtypeStruct(o, F32) if isinstance(o, tuple) else o for o in outs]
    args = [
        pltpu.with_memory_space_constraint(x, pltpu.HBM) if n in hbm else x for n, x in enumerate(args)
    ]
    return pl.pallas_call(
        kernel,
        out_shape=outs,
        in_specs=[
            HBM if n in hbm else ANY if (aliases or {}).get(n) in still else VMEM for n in range(len(args))
        ],
        out_specs=[ANY if n in still else VMEM for n in range(len(outs))],
        scratch_shapes=list(scratch),
        input_output_aliases=aliases or {},
        compiler_params=pltpu.CompilerParams(vmem_limit_bytes=12 * 1024 * 1024),
        cost_estimate=pl.CostEstimate(flops=flops, bytes_accessed=4 * 1024 * 1024, transcendentals=0),
    )(*args)


def fetch(source, target, sems, first, parts):
    step = target.shape[0] // parts
    copies = []
    for n in range(parts):
        part = pl.ds(n * step, step)
        copies.append(pltpu.make_async_copy(source.at[part], target.at[part], sems.at[first + n]))
        copies[-1].start()
    return copies


def kept(x):
    return pltpu.with_memory_space_constraint(x, pltpu.VMEM)


def down(block, column):
    return jnp.sum(block * jnp.broadcast_to(column, block.shape), axis=0, keepdims=True)


def fold(x):
    return jnp.sum(x, axis=0, keepdims=True)


def precondition(blocks_ref, x, out_ref, copies=()):
    xt = x.T
    for i in range(x.shape[0]):
        if copies and i % (x.shape[0] // len(copies)) == 0:
            copies[i // (x.shape[0] // len(copies))].wait()
        out_ref[i : i + 1] = down(blocks_ref[i], xt[:, i : i + 1])


def first_kernel(rhs_hbm, precond_hbm, v_ref, send_ref, rhs_ref, precond_ref, sems):
    (small,) = fetch(rhs_hbm, rhs_ref, sems, PARTS, 1)
    copies = fetch(precond_hbm, precond_ref, sems, 0, PARTS)
    small.wait()
    precondition(precond_ref, rhs_ref[...], v_ref, copies)
    send_ref[...] = jnp.broadcast_to(v_ref[...][None], send_ref.shape)


def widen(x, wide_ref):
    xt = x.T
    for i in range(x.shape[0]):
        wide_ref[i] = jnp.broadcast_to(xt[:, i : i + 1], wide_ref.shape[1:])


def own_rows(i, blocks, arcs, index_ref, tiles_ref, wide_ref):
    c, j = lax.div(i, arcs), lax.rem(i, arcs)
    total = tiles_ref[i, 0] * wide_ref[c * blocks + lax.rem(index_ref[0, c, j], blocks)]
    return total + tiles_ref[i, 1] * wide_ref[c * blocks + lax.rem(index_ref[1, c, j], blocks)]


def near_kernel(comms, index_ref, v_ref, tiles_hbm, pre_hbm, up_ref, pre_ref, tiles_ref, wide_ref, sems, ready):
    count = up_ref.shape[0]
    arcs = count // comms
    blocks = v_ref.shape[0] // comms
    own = fetch(tiles_hbm.at[:, pl.ds(0, 2)], tiles_ref, sems, 0, PARTS)
    (pre,) = fetch(pre_hbm, pre_ref, sems, PARTS, 1)
    widen(v_ref[...], wide_ref)
    ready()
    step = count // PARTS
    for n in range(PARTS):
        own[n].wait()

        def one(i, _):
            up_ref[pl.ds(i, 1)] = fold(own_rows(i, blocks, arcs, index_ref, tiles_ref, wide_ref))
            return 0

        lax.fori_loop(n * step, (n + 1) * step, one, 0, unroll=4)
    pre.wait()


def cap_first_kernel(cap_rhs_ref, cap_precond_ref, q_ref):
    precondition(cap_precond_ref, cap_rhs_ref[...], q_ref)


def cap_second_kernel(
    cap_rhs_ref, q0_ref, half_ref, other_ref, cap_precond_ref, yq_ref, q_ref, sums_ref
):
    caps = q0_ref.shape[0]
    note = half_ref[...] + other_ref[...]
    q0 = q0_ref[...]
    yq_ref[...] = q0 + note[:caps]
    sums_ref[...] = note[caps:]
    sums_ref[0:1] += fold(cap_rhs_ref[...] * q0)
    sums_ref[1:2] += fold(q0 * q0)
    precondition(cap_precond_ref, yq_ref[...], q_ref)


def cap_third_kernel(
    alpha_ref, cap_rhs_ref, q0_ref, yq0_ref, q1_ref, half_ref, other_ref, cap_precond_ref,
    zq_ref, yzq_ref, rq_ref, q_ref, sums_ref,
):
    caps = q0_ref.shape[0]
    alpha = alpha_ref[0:1]
    yq0, q1 = yq0_ref[...], q1_ref[...]
    yq1 = q1 + half_ref[:caps] + other_ref[:caps]
    zq = q0_ref[...] - alpha * q1
    yzq = yq0 - alpha * yq1
    rq = cap_rhs_ref[...] - alpha * yq0
    zq_ref[...] = zq
    yzq_ref[...] = yzq
    rq_ref[...] = rq
    precondition(cap_precond_ref, alpha * yzq, q_ref)
    q = q_ref[...]
    pairs = ((zq, yq0), (zq, yzq), (q, yq0), (q, yzq), (q, q), (zq, rq), (q, rq))
    for n, (one, other) in enumerate(pairs):
        sums_ref[n : n + 1] = fold(one * other)
    sums_ref[7:8] = jnp.zeros_like(sums_ref[7:8])


def beside(block, row, lane, n, total):
    return jnp.where(lane == n, jnp.sum(block * row, axis=1, keepdims=True), total)


def arcs_up(comms, blocks, index_ref, cap_index_ref, up_ref, got_ref, q_ref, scale_ref, tiles_hbm, cap_tiles_hbm,
            scaled_ref, note_ref, far_ref, third_ref, cap_tiles_ref, wide_ref, turn_ref, sems, ready):
    count = up_ref.shape[0]
    arcs = count // comms
    width = scale_ref.shape[1]
    thirds = fetch(tiles_hbm.at[:, 2], third_ref, sems, 0, PARTS)
    caps_in = fetch(cap_tiles_hbm, cap_tiles_ref, sems, PARTS, PARTS)
    widen(q_ref[...], wide_ref)
    ready()

    def place(i, _):
        c, j = lax.div(i, arcs), lax.rem(i, arcs)
        far = index_ref[2, c, j]
        row = c if got_ref.shape[1] == comms else c * blocks + lax.rem(far, blocks)
        far_ref[pl.ds(i, 1)] = got_ref[lax.div(far, blocks), pl.ds(row, 1)]
        return 0

    lax.fori_loop(0, count, place, 0, unroll=4)
    ft = far_ref[...].T
    step = count // PARTS
    for i in range(count):
        if i % step == 0:
            thirds[i // step].wait()
            caps_in[i // step].wait()
        column = jnp.broadcast_to(ft[:, i : i + 1], third_ref.shape[1:])
        total = third_ref[i] * column + cap_tiles_ref[i] * wide_ref[cap_index_ref[i // arcs, i % arcs]]
        far_ref[i : i + 1] = up_ref[i : i + 1] + fold(total)
    upward = far_ref[...]
    scaled = scale_ref[...] * upward
    scaled_ref[...] = scaled
    lane = lax.broadcasted_iota(jnp.int32, (width, width), 1)

    total = jnp.zeros((width, width), F32)
    for i in range(count):
        total = beside(cap_tiles_ref[i], scaled[i : i + 1], lane, i, total)
    turn_ref[...] = total.T
    note_ref[...] = jnp.zeros_like(note_ref)

    for i in range(count):
        note_ref[pl.ds(cap_index_ref[i // arcs, i % arcs], 1)] += turn_ref[i : i + 1]
    return fold(upward * scaled)


def up_first_kernel(comms, blocks, caps, index_ref, cap_index_ref, up_ref, got_ref, q_ref, scale_ref, rhs_ref, v_ref,
                    tiles_hbm, cap_tiles_hbm, scaled_ref, note_ref, *room, ready):
    energy = arcs_up(comms, blocks, index_ref, cap_index_ref, up_ref, got_ref, q_ref, scale_ref, tiles_hbm,
                     cap_tiles_hbm, scaled_ref, note_ref, *room, ready)
    v = v_ref[...]
    note_ref[caps : caps + 1] = fold(rhs_ref[...] * v)
    note_ref[caps + 1 : caps + 2] = fold(v * v) + energy


def up_second_kernel(comms, blocks, index_ref, cap_index_ref, up_ref, got_ref, q_ref, scale_ref, tiles_hbm,
                     cap_tiles_hbm, scaled_ref, note_ref, *room, ready):
    arcs_up(comms, blocks, index_ref, cap_index_ref, up_ref, got_ref, q_ref, scale_ref, tiles_hbm,
            cap_tiles_hbm, scaled_ref, note_ref, *room, ready)


def up_third_kernel(comms, blocks, caps, index_ref, cap_index_ref, up_ref, got_ref, q_ref, scale_ref, z_ref, yz_ref,
                    r_ref, y0_ref, v_ref, tiles_hbm, cap_tiles_hbm, scaled_ref, notes_ref, note_ref, *room, ready):
    energy = arcs_up(comms, blocks, index_ref, cap_index_ref, up_ref, got_ref, q_ref, scale_ref, tiles_hbm,
                     cap_tiles_hbm, scaled_ref, note_ref, *room, ready)
    z, yz, r, y0, v = z_ref[...], yz_ref[...], r_ref[...], y0_ref[...], v_ref[...]
    pairs = ((z, y0), (z, yz), (v, y0), (v, yz), (v, v), (z, r), (v, r))
    for n, (one, other) in enumerate(pairs):
        note_ref[caps + n : caps + n + 1] = fold(one * other)
    note_ref[caps + 4 : caps + 5] += energy
    notes_ref[...] = jnp.broadcast_to(note_ref[...][None], notes_ref.shape)


def down_kernel(comms, blocks, step_number, index_ref, scaled_ref, sums_ref, tiles_ref, local_ref, back_ref, turn_ref, *room, ready):
    count, touched = tiles_ref.shape[:2]
    width = tiles_ref.shape[3]
    arcs = count // comms
    copies = []
    if step_number == 2:
        tiles_hbm, (tiles_ref, sems) = tiles_ref, room
        copies = fetch(tiles_hbm, tiles_ref, sems, 0, 2 * PARTS)
    local_ref[...] = jnp.zeros_like(local_ref)
    if step_number == 0:
        back_ref[...] = jnp.full(back_ref.shape, -1.0, F32)
    lane = lax.broadcasted_iota(jnp.int32, (width, width), 1)
    total = jnp.zeros((width, width), F32)
    for i in range(count):
        if copies and i % (count // len(copies)) == 0:
            copies[i // (count // len(copies))].wait()
        row = scaled_ref[i : i + 1]
        for k in range(touched):
            total = beside(tiles_ref[i, k], row, lane, k * count + i, total)
    turn_ref[...] = total.T
    ready()

    for i in range(count):
        c, j = i // arcs, i % arcs
        for k in range(2):
            b = c * blocks + lax.rem(index_ref[k, c, j], blocks)
            local_ref[pl.ds(b, 1)] += turn_ref[k * count + i : k * count + i + 1]
        far = index_ref[2, c, j]
        to = lax.div(far, blocks)
        back_ref[to, c : c + 1] = turn_ref[2 * count + i : 2 * count + i + 1]
        if step_number == 0:
            local = lax.rem(far, blocks).astype(F32)
            back_ref[to, comms + c : comms + c + 1] = jnp.full((1, width), local, F32)
    if step_number == 1:
        shape = (back_ref.shape[0], 2, width)
        back_ref[:, comms : comms + 2] = jnp.broadcast_to(sums_ref[0:2][None], shape)


def add_kernel(note_ref, other_ref, back_ref, out_ref, same_ref):
    del back_ref, same_ref
    out_ref[...] = note_ref[...] + other_ref[...]


def insert_kernel(comms, caps, notes_ref, sums_ref, back_ref, cap_ref, out_ref):
    del back_ref
    total = jnp.sum(notes_ref[...], axis=0)
    cap_ref[...] = total[:caps]
    sums = jnp.sum(total[caps:] + sums_ref[...], axis=1, keepdims=True)
    width = out_ref.shape[2]
    pick = lax.broadcasted_iota(jnp.int32, (NOTE, width), 0) == lax.broadcasted_iota(
        jnp.int32, (NOTE, width), 1
    )
    row = fold(jnp.where(pick, jnp.broadcast_to(sums, (NOTE, width)), 0.0))
    out_ref[:, comms : comms + 1] = jnp.broadcast_to(row[None], (out_ref.shape[0], 1, width))


def collect(comms, v_ref, local_ref, back_ref, asked, y_ref):
    blocks = v_ref.shape[0] // comms
    for c in range(comms):
        part = back_ref[:, c]
        for b in range(blocks):
            n = c * blocks + b
            came = fold(jnp.where(asked[c] == b, part, 0.0))
            y_ref[n : n + 1] = v_ref[n : n + 1] + local_ref[n : n + 1] + came


def pack(comms, v_ref, asked, send_ref):
    blocks = v_ref.shape[0] // comms
    for c in range(comms):
        row = jnp.zeros_like(asked[c])
        for b in range(blocks):
            n = c * blocks + b
            row = jnp.where(asked[c] == b, v_ref[n : n + 1], row)
        send_ref[:, c] = row


def rows_second_kernel(comms, v0_ref, local_ref, back_ref, precond_ref, y_ref, v_ref, send_ref, asked_ref):
    asked = [back_ref[:, comms + c] for c in range(comms)]
    for c in range(comms):
        asked_ref[c] = asked[c]
    collect(comms, v0_ref, local_ref, back_ref, asked, y_ref)
    precondition(precond_ref, y_ref[...], v_ref)
    pack(comms, v_ref, asked, send_ref)


def rows_third_kernel(comms, rhs_ref, v0_ref, y0_ref, v1_ref, local_ref, back_ref, asked_ref,
                      precond_ref, alpha_ref, z_ref, yz_ref, r_ref, v_ref, send_ref):
    asked = [asked_ref[c] for c in range(comms)]
    collect(comms, v1_ref, local_ref, back_ref, asked, yz_ref)
    first = jnp.sum(fold(back_ref[:, comms]), axis=1, keepdims=True)
    second = jnp.sum(fold(back_ref[:, comms + 1]), axis=1, keepdims=True)
    alpha = jnp.broadcast_to(first / second, (1, alpha_ref.shape[1]))
    alpha_ref[...] = jnp.broadcast_to(alpha, alpha_ref.shape)
    alpha_ref[1:2] = jnp.broadcast_to(second, (1, alpha_ref.shape[1]))
    y0 = y0_ref[...]
    z_ref[...] = v0_ref[...] - alpha * v1_ref[...]
    yz = y0 - alpha * yz_ref[...]
    yz_ref[...] = yz
    r_ref[...] = rhs_ref[...] - alpha * y0
    precondition(precond_ref, alpha * yz, v_ref)
    pack(comms, v_ref, asked, send_ref)


def last_kernel(comms, alpha_ref, v0_ref, y0_ref, z_ref, yz_ref, r_ref, v2_ref, local_ref, back_ref,
                asked_ref, q0_ref, yq0_ref, zq_ref, yzq_ref, rq_ref, q2_ref, cap_ref,
                sol_ref, cap_sol_ref, res_ref, cap_res_ref, y_ref):
    asked = [asked_ref[c] for c in range(comms)]
    collect(comms, v2_ref, local_ref, back_ref, asked, y_ref)
    row = fold(back_ref[:, comms])
    width = row.shape[1]
    lane = lax.broadcasted_iota(jnp.int32, row.shape, 1)
    s = [
        jnp.broadcast_to(
            jnp.sum(jnp.where(lane == n, row, 0.0), axis=1, keepdims=True), (1, width)
        )
        for n in range(7)
    ]
    alpha, h00 = alpha_ref[0:1], alpha_ref[1:2]
    h1, h2 = s[0] / h00, s[2] / h00
    a11 = s[1] - h1 * s[0]
    a12 = s[3] - h1 * s[2]
    a22 = s[4] - h2 * s[2]
    lower = a12 / a11
    c2 = (s[6] - lower * s[5]) / (a22 - lower * a12)
    c1 = s[5] / a11 - lower * c2
    c0 = c1 * h1 + c2 * h2
    sol_ref[...] = (alpha - c0) * v0_ref[...] + c1 * z_ref[...] + c2 * v2_ref[...]
    cap_sol_ref[...] = (alpha - c0) * q0_ref[...] + c1 * zq_ref[...] + c2 * q2_ref[...]
    res_ref[...] = r_ref[...] + c0 * y0_ref[...] - c1 * yz_ref[...] - c2 * y_ref[...]
    yq2 = q2_ref[...] + cap_ref[...]
    cap_res_ref[...] = rq_ref[...] + c0 * yq0_ref[...] - c1 * yzq_ref[...] - c2 * yq2


def body(
    tiles, cap_tiles, row_index, cap_index, arc_scale, rows_rhs, cap_rhs, precond, cap_precond
):
    comms, arcs, touched = row_index.shape
    blocks, width = rows_rhs.shape[1:]
    caps = cap_rhs.shape[0]
    groups = lax.axis_size("stn") * lax.axis_size("tm")
    peers = lax.axis_size("comm")
    rows, count = comms * blocks, comms * arcs
    flat = (width, width)
    tiles = tiles.reshape(count, touched, *flat)
    cap_tiles = cap_tiles.reshape(count, *flat)
    precond = precond.reshape(rows, *flat)
    index = jnp.transpose(row_index, (2, 0, 1))
    scale = arc_scale.reshape(count, width)
    rhs = rows_rhs.reshape(rows, width)
    row_shape, cap_shape, arc_shape = (rows, width), (caps, width), (count, width)
    small = (NOTE, width)
    note_shape = (caps + NOTE, width)
    send_shape = (groups, comms, width)
    back_shape = (groups, SLOT, width)
    unit = 2 * count * width * width

    def room(*shape):
        return pltpu.VMEM(shape, F32)

    def sems(n):
        return pltpu.SemaphoreType.DMA((n,))

    def exchange(x):
        return lax.all_to_all(x, GROUP, 0, 0)

    def across(x, step):
        return lax.ppermute(x, "comm", [(i, i ^ step) for i in range(peers)])

    def near(v):
        up, pre = call(
            functools.partial(near_kernel, comms), [arc_shape, pltpu.VMEM((caps, *flat), F32)],
            (index, v, tiles, cap_precond), 1,
            [room(count, 2, *flat), room(rows, *flat), sems(PARTS + 1)], flops=2 * unit, hbm=(2, 3),
        )
        return up, kept(pre)

    up_room = [
        room(*arc_shape), room(count, *flat), room(count, *flat), room(caps, *flat), room(*flat), sems(2 * PARTS),
    ]

    def spread(step_number, scaled, sums):
        return call(
            functools.partial(down_kernel, comms, blocks, step_number), [row_shape, back_shape],
            (index, scaled, sums, kept(tiles) if step_number < 2 else tiles), 1,
            [room(*flat)] + ([room(count, touched, *flat), sems(2 * PARTS)] if step_number == 2 else []),
            flops=3 * unit, hbm=(3,) if step_number == 2 else (),
        )

    def add(note, other, back):
        return call(add_kernel, [note_shape, back.shape], (note, other, back), aliases={2: 1}, still=(1,))

    v0, send = call(
        first_kernel, [row_shape, (groups, rows, width)], (rhs, precond), 0,
        [room(*row_shape), room(rows, *flat), sems(PARTS + 1)], hbm=(0, 1),
    )
    got = exchange(send)
    up, pre = near(v0)
    (q0,) = call(cap_first_kernel, [cap_shape], (cap_rhs, pre), flops=unit)
    scaled, note = call(
        functools.partial(up_first_kernel, comms, blocks, caps), [arc_shape, note_shape],
        (index, cap_index, up, got, q0, scale, rhs, v0, tiles, cap_tiles), 2, up_room, flops=3 * unit, hbm=(8, 9),
    )
    other = across(note, 1)
    local, back = spread(0, scaled, rhs)
    note, back = add(note, other, back)
    back = exchange(back)
    other = across(note, 4)
    y0, v1, send, asked = call(
        functools.partial(rows_second_kernel, comms),
        [row_shape, row_shape, send_shape, (comms, groups, width)],
        (v0, local, back, kept(precond)),
    )
    half, send = add(note, other, send)
    got = exchange(send)
    other = across(half, 2)
    up, pre = near(v1)
    yq0, q1, sums = call(
        cap_second_kernel, [cap_shape, cap_shape, small], (cap_rhs, q0, half, other, pre), flops=unit,
    )
    scaled, note = call(
        functools.partial(up_second_kernel, comms, blocks), [arc_shape, note_shape],
        (index, cap_index, up, got, q1, scale, tiles, cap_tiles), 2, up_room, flops=3 * unit, hbm=(6, 7),
    )
    other = across(note, 1)
    local, back = spread(1, scaled, sums)
    note, back = add(note, other, back)
    back = exchange(back)
    other = across(note, 4)
    alpha, z1, yz, r1, v2, send = call(
        functools.partial(rows_third_kernel, comms),
        [small, row_shape, row_shape, row_shape, row_shape, send_shape],
        (rhs, v0, y0, v1, local, back, asked, kept(precond)),
    )
    half, send = add(note, other, send)
    got = exchange(send)
    other = across(half, 2)
    up, pre = near(v2)
    zq1, yzq, rq1, q2, sums = call(
        cap_third_kernel, [cap_shape] * 4 + [small],
        (alpha, cap_rhs, q0, yq0, q1, half, other, pre), flops=unit,
    )
    scaled, notes = call(
        functools.partial(up_third_kernel, comms, blocks, caps), [arc_shape, (peers, *note_shape)],
        (index, cap_index, up, got, q2, scale, z1, yz, r1, y0, v2, tiles, cap_tiles), 2,
        [room(*note_shape), *up_room], flops=3 * unit, hbm=(11, 12),
    )
    notes = lax.all_to_all(notes, "comm", 0, 0)
    local, back = spread(2, scaled, sums)
    cap_sum, back = call(
        functools.partial(insert_kernel, comms, caps), [cap_shape, back_shape], (notes, sums, back),
        aliases={2: 1},
    )
    back = exchange(back)
    sol, cap_sol, res, cap_res = call(
        functools.partial(last_kernel, comms), [row_shape, cap_shape, row_shape, cap_shape],
        (alpha, v0, y0, z1, yz, r1, v2, local, back, asked, q0, yq0, zq1, yzq, rq1, q2, cap_sum), 0,
        [pltpu.VMEM(row_shape, F32)],
    )
    return sol.reshape(rows_rhs.shape), cap_sol, res.reshape(rows_rhs.shape), cap_res


def solution(mesh):
    placed = (
        P("comm", GROUP, None, None, None),
        P("comm", GROUP, None, None),
        P("comm", GROUP, None),
        P("comm", GROUP),
        P("comm", GROUP, None),
        P("comm", GROUP, None),
        P(GROUP, None),
        P("comm", GROUP, None, None),
        P(GROUP, None, None),
    )
    return jax.shard_map(
        body,
        mesh=mesh,
        in_specs=placed,
        out_specs=(
            P("comm", GROUP, None),
            P(GROUP, None),
            P("comm", GROUP, None),
            P(GROUP, None),
        ),
        check_vma=False,
    )
```
